32 devices in a mesh: row: 8 (over z, x), col: 4 (over y, core).
Axes of the slice: x: 2, y: 2, z: 4, core: 2. Of those that a mesh axis runs over, the one named last changes fastest.
Arguments:
- features: bfloat16 [4, 1024, 2048], P('col', 'row'), may hold values from -6 to 6
- weight: bfloat16 [2048, 2048], P(('row', 'col')), may hold values from -0.125 to 0.125
- bias: bfloat16 [2048], P(('row', 'col')), may hold values from -3 to 3
- node_mask: int32 [8, 512], P('row', 'col'), may hold values 0 or 1
- neighbour_tiles: int32 [8, 4, 4, 3], P('row', 'col'), may hold values from -1 to 7, as said below
- tile_weights: bfloat16 [8, 4, 4, 3, 128, 128], P('row', 'col'), may hold values from -0.3125 to 0.3125
- out_grad: bfloat16 [8, 512, 2048], P('row', 'col'), may hold values from -6 to 6
Outputs:
- activations: bfloat16 [8, 512, 2048], P('row', 'col')
- input_grad: bfloat16 [4, 1024, 2048], P('col', 'row')
- weight_grad: float32 [2048, 2048], P(('row', 'col'))
- bias_grad: float32 [2048], P(('row', 'col'))
The draws below stay inside these ranges and needn't reach their ends.
Inputs may be any that keep to these rules, and one draw needn't show every extreme that they name: `neighbour_tiles`: in each destination tile the first 1 to 3 slots list distinct source tiles and the rest hold -1; destination tile 0 of block (0, 0) lists 3 tiles, the first of them 8 - 1.
All inputs are finite; a program needn't handle non-finite values. No bound on the sum of `node_mask` on one device may be relied on, other than what follows from the above.
Results may differ from the reference program's by a relative error of at most 0.0064.
Values may be sent and summed in bfloat16 or wider, within the bound.
No kernel may reach another device: no remote copies, remote signals or barrier semaphores. Data moves between devices by JAX's collectives and lax.ppermute only.
A program may use at most 128 MiB of HBM per device.

```python
import jax
import jax.numpy as jnp
from jax import lax

D = 2048
TILE = 128
SLOTS = 3
NODES_DEV = 128
DEST_TILES = 4
SOURCE_TILES = 8
N_ROW = 8
N_COL = 4


def draw_neighbour_tiles(key, part):
    first, second, third = jax.random.split(key, 3)
    total_rows = N_ROW * N_COL * DEST_TILES
    scores = jax.random.randint(first, (total_rows, SOURCE_TILES), 0, 2 ** 20)
    scores = scores * SOURCE_TILES + jnp.arange(SOURCE_TILES, dtype=jnp.int32)[None, :]
    scores = scores.at[0, SOURCE_TILES - 1].set(-1)
    order = jnp.argsort(scores, axis=1, stable=True)[:, :SLOTS].astype(jnp.int32)
    left = jax.random.randint(second, (total_rows,), 0, SLOTS)
    right = jax.random.randint(third, (total_rows,), 0, SLOTS)
    row_block = jnp.arange(total_rows, dtype=jnp.int32) // (N_COL * DEST_TILES)
    heavy = row_block < max(N_ROW // 4, 1)
    counts = jnp.where(heavy, SLOTS, jnp.maximum(left, right) + 1)
    counts = counts.at[0].set(SLOTS)
    position = jnp.arange(SLOTS, dtype=jnp.int32)[None, :]
    listed = jnp.where(position < counts[:, None], order, -1)
    return listed.reshape(N_ROW, N_COL, DEST_TILES, SLOTS).astype(jnp.int32)


def touch_ends(array, rng, low, top_value):
    spot = [jax.random.randint(jax.random.fold_in(rng, axis), (), 0, length) for axis, length in enumerate(array.shape)]
    longest = array.shape.index(max(array.shape))
    next_to = spot[:longest] + [(spot[longest] + 1) % array.shape[longest]] + spot[longest + 1:]
    return array.at[tuple(spot)].set(low).at[tuple(next_to)].set(top_value)


def shard_levels(rng, shape, cuts, least, high):
    def one(dim, shards_of):
        heights = jax.random.uniform(jax.random.fold_in(jax.random.fold_in(rng, 6), dim), (shards_of,), jnp.float32, least / len(cuts), high / len(cuts))
        return jnp.repeat(jnp.exp(heights), shape[dim] // shards_of).reshape((-1,) + (1,) * (len(shape) - dim - 1))

    gain = one(*cuts[0])
    for cut in cuts[1:]:
        gain = gain * one(*cut)
    return gain


def noise(key, dims, deviation, most, cuts=(), kind=jnp.bfloat16):
    result = jax.random.normal(key, dims, jnp.float32) * deviation
    if len(cuts) > 0:
        result = shard_levels(key, dims, cuts, -0.22, 0.18) * result
    return jnp.clip(result, min=-most, max=most).astype(kind)


def setup_inputs(seed: int = 0) -> dict:
    key_of = jax.random.split(jax.random.key(seed), 8)
    features = noise(key_of[0], (N_COL, N_ROW * NODES_DEV, D), 1.0, 6.0, ((0, 4), (1, 8)))
    weight = noise(key_of[1], (D, D), D ** -0.5, 0.125, ((0, 32),))
    bias = noise(key_of[2], (D,), 0.5, 3.0, ((0, 32),))
    node_mask = touch_ends((jax.random.randint(key_of[3], (N_ROW, N_COL * NODES_DEV), 0, 8) < 7).astype(jnp.int32), jax.random.fold_in(key_of[3], 1), 0, 1)
    neighbour_tiles = draw_neighbour_tiles(jax.random.fold_in(key_of[7], 71), 0)
    tile_weights = noise(key_of[5], (N_ROW, N_COL, DEST_TILES, SLOTS, TILE, TILE), (SLOTS * TILE) ** -0.5, 0.3125, ((0, 8), (1, 4)))
    out_grad = noise(key_of[6], (N_ROW, N_COL * NODES_DEV, D), 1.0, 6.0, ((0, 8), (1, 4)))
    return dict(features=features, weight=weight, bias=bias, node_mask=node_mask, neighbour_tiles=neighbour_tiles, tile_weights=tile_weights, out_grad=out_grad)


@jax.custom_vjp
def low(v):
    return lax.optimization_barrier(v.astype(jnp.bfloat16)).astype(jnp.float32)

@jax.custom_vjp
def low_back(v):
    return v

def low_keep(v):
    return (low(v), None)

def low_pass(kept, grad):
    return (grad,)

def back_keep(v):
    return (v, None)

def back_low(kept, grad):
    return (low(grad),)
low.defvjp(low_keep, low_pass)
low_back.defvjp(back_keep, back_low)

def reference(features, weight, bias, node_mask, neighbour_tiles, tile_weights, out_grad):
    width = features.shape[-1]
    valid = neighbour_tiles >= 0
    listed = jnp.maximum(neighbour_tiles, 0).astype(jnp.int32)
    blocks = jnp.where(valid[..., None, None], tile_weights.astype(jnp.float32), jnp.float32(0.0))
    keep = node_mask.astype(jnp.float32)[..., None]
    column_ids = jnp.repeat(jnp.arange(N_COL, dtype=jnp.int32), SLOTS)

    def forward(inputs, matrix, offset):
        source = inputs.reshape(N_COL, SOURCE_TILES, TILE, width)

        @jax.checkpoint
        def one_row(pieces):
            row_lists, row_blocks = pieces
            flat_lists = jnp.transpose(row_lists, (0, 2, 1)).reshape(N_COL * SLOTS, DEST_TILES)
            flat_blocks = jnp.transpose(row_blocks, (0, 2, 1, 3, 4)).reshape(N_COL * SLOTS, DEST_TILES, TILE, TILE)

            @jax.checkpoint
            def one_slot(total, step_pieces):
                slot_lists, slot_blocks, column = step_pieces
                source_block = lax.dynamic_index_in_dim(source, column, 0, keepdims=False)
                taken = source_block[slot_lists]
                total = total + jnp.einsum('mij,mjd->mid', slot_blocks, taken, precision=lax.Precision.HIGHEST)
                return (total, None)
            start = jnp.zeros((DEST_TILES, TILE, width), jnp.float32)
            total, unused = lax.scan(one_slot, start, (flat_lists, flat_blocks, column_ids))
            return total.reshape(DEST_TILES * TILE, width)
        aggregate = lax.map(one_row, (listed, blocks))
        aggregate = low(low_back(aggregate))
        pre = jnp.einsum('rnd,de->rne', aggregate, matrix, precision=lax.Precision.HIGHEST) + offset
        pre = low_back(pre)
        return keep * jax.nn.silu(pre)
    output, pullback = jax.vjp(forward, features.astype(jnp.float32), weight.astype(jnp.float32), bias.astype(jnp.float32))
    input_grad, weight_grad, bias_grad = pullback(out_grad.astype(jnp.float32))
    return (output.astype(jnp.bfloat16), input_grad.astype(jnp.bfloat16), weight_grad, bias_grad)
```

```python
import functools

import jax
import jax.numpy as jnp
from jax import lax
from jax.experimental import pallas as pl
from jax.experimental.pallas import tpu as pltpu
from jax.sharding import PartitionSpec as P

BOTH = ("row", "col")
F32 = jnp.float32
BF16 = jnp.bfloat16
VMEM = pl.BlockSpec(memory_space=pltpu.VMEM)
SMEM = pl.BlockSpec(memory_space=pltpu.SMEM)
CORE, Y, X, Z = 1, 2, 4, 8
GROUP = 4


def swap(value, mask, total=32):
    return lax.ppermute(value, BOTH, [(i, i ^ mask) for i in range(total)])


def call(kernel, outs, *operands, scratch=(), smem=1, flops=0):
    moved = sum(o.size * o.dtype.itemsize for o in operands)
    moved += sum(o.size * o.dtype.itemsize for o in outs)
    return pl.pallas_call(
        kernel,
        out_shape=outs,
        in_specs=[SMEM] * smem + [VMEM] * (len(operands) - smem),
        out_specs=[VMEM] * len(outs),
        scratch_shapes=list(scratch),
        compiler_params=pltpu.CompilerParams(vmem_limit_bytes=48 * 2**20),
        cost_estimate=pl.CostEstimate(flops=flops, bytes_accessed=moved, transcendentals=0),
    )(*operands)


def shape(dims, dtype):
    return jax.ShapeDtypeStruct(dims, dtype)


def gather_kernel(ids, l0, l1, l2, l3, a0, a1, a2, a3, source, keep, send):
    member, core = ids[0], ids[1]
    for i, (lists, tiles) in enumerate(zip((l0, l1, l2, l3), (a0, a1, a2, a3))):
        dests, slots = tiles.shape[0], tiles.shape[1]
        for pair in range(dests // 2):
            for other in range(2):
                m = pair * 2 + (core if other == 0 else 1 - core)
                left, right = [], []
                for s in range(slots):
                    listed = lists[m, s]
                    block = tiles[m, s]
                    left.append(jnp.where(listed >= 0, block, jnp.zeros_like(block)))
                    right.append(source[jnp.maximum(listed, 0)])
                total = jnp.dot(
                    jnp.concatenate(left, axis=1),
                    jnp.concatenate(right, axis=0),
                    preferred_element_type=F32,
                )
                if other == 0:
                    keep[member ^ i, pair] = total
                else:
                    send[member ^ i, pair] = total.astype(BF16)


def aggregate_kernel(ids, terms, full, s1, s2, s3):
    place = ids[2]
    quarter = terms.shape[-1]
    for part in range(GROUP):
        total = terms[2 * part].astype(F32) + terms[2 * part + 1].astype(F32)
        full[:, part * quarter : (part + 1) * quarter] = total.astype(BF16)
    block = quarter // GROUP
    for i, piece in ((1, s1), (2, s2), (3, s3)):
        for part in range(GROUP):
            start = pl.multiple_of(part * quarter + (place ^ i) * block, block)
            piece[:, part * block : (part + 1) * block] = full[:, pl.ds(start, block)]


def dense_kernel(ids, own, other, bias, grad_own, grad_other, *rest):
    chips = 16
    weights = rest[:chips]
    act_own, act_other, pre_grad, back_own, back_other, bias_sum, left = rest[chips:]
    chip = ids[3]
    nodes, width = own.shape
    block = width // chips
    half = pre_grad.shape[1]
    for i in range(chips):
        start = pl.multiple_of((chip ^ i) * block, block)
        left[:nodes, i * block : (i + 1) * block] = own[:, pl.ds(start, block)]
        left[nodes:, i * block : (i + 1) * block] = other[:, pl.ds(start, block)]
    step = 256
    for n in range(half // step):
        cols = slice(n * step, (n + 1) * step)
        matrix = jnp.concatenate([w[:, cols] for w in weights], axis=0)
        pre = jnp.dot(left[...], matrix, preferred_element_type=F32) + bias[:, cols]
        sigmoid = 1.0 / (1.0 + jnp.exp(-pre))
        act = (pre * sigmoid).astype(BF16)
        act_own[:, cols] = act[:nodes]
        act_other[:, cols] = act[nodes:]
        slope = sigmoid * (1.0 + pre * (1.0 - sigmoid))
        og = jnp.concatenate([grad_own[:, cols], grad_other[:, cols]], axis=0).astype(F32)
        grad = (og * slope).astype(BF16)
        pre_grad[:, cols] = grad
        bias_sum[:, cols] = jnp.sum(grad.astype(F32), axis=0, keepdims=True)
    for i in range(0, chips, 2):
        matrix = jnp.concatenate([weights[i][...], weights[i + 1][...]], axis=0)
        back = lax.dot_general(
            pre_grad[...], matrix, (((1,), (1,)), ((), ())), preferred_element_type=F32
        )
        for j in range(2):
            start = pl.multiple_of((chip ^ (i + j)) * block, block)
            back_own[:, pl.ds(start, block)] = back[:nodes, j * block : (j + 1) * block]
            back_other[:, pl.ds(start, block)] = back[nodes:, j * block : (j + 1) * block].astype(BF16)


def pieces_kernel(own, received, pieces):
    quarter = pieces.shape[-1]
    for part in range(GROUP):
        cols = slice(part * quarter, (part + 1) * quarter)
        total = (own[:, cols] + received[:, cols].astype(F32)).astype(BF16)
        pieces[2 * part] = total
        pieces[2 * part + 1] = total


def spread_kernel(ids, l0, l1, l2, l3, a0, a1, a2, a3, same, cross, out, total):
    member, core = ids[0], ids[1]
    total[...] = jnp.zeros_like(total)
    for i, (lists, tiles) in enumerate(zip((l0, l1, l2, l3), (a0, a1, a2, a3))):
        dests, slots, tile = tiles.shape[0], tiles.shape[1], tiles.shape[2]
        for pair in range(dests // 2):
            for other in range(2):
                m = pair * 2 + (core if other == 0 else 1 - core)
                grads = (same if other == 0 else cross)[(member ^ i) * 2 + pair]
                left = []
                for s in range(slots):
                    block = tiles[m, s]
                    left.append(jnp.where(lists[m, s] >= 0, block, jnp.zeros_like(block)))
                terms = lax.dot_general(
                    jnp.concatenate(left, axis=1), grads, (((0,), (0,)), ((), ())),
                    preferred_element_type=F32,
                )
                for s in range(slots):
                    at = jnp.maximum(lists[m, s], 0)
                    total[at] += terms[s * tile : (s + 1) * tile]
    out[...] = total[...].astype(BF16)


def finish_kernel(terms, out):
    quarter = terms.shape[-1]
    for part in range(GROUP):
        total = terms[part].astype(F32) + terms[part + GROUP].astype(F32)
        out[:, part * quarter : (part + 1) * quarter] = total.astype(BF16)


def weight_grad_kernel(ids, own, other, r1, r2, r3, c1, c2, c3, g0, g1, g2, g3, mine, s1, s2, s3, total):
    place, depth = ids[2], ids[4]
    nodes, width = own.shape
    quarter = width // GROUP
    block = quarter // GROUP
    first = []
    for part in range(GROUP):
        start = pl.multiple_of(part * quarter + place * block, block)
        first.append(jnp.concatenate([own[:, pl.ds(start, block)], other[:, pl.ds(start, block)]], axis=0))
    lefts = [jnp.concatenate(first, axis=1)]
    for a, b in ((r1, c1), (r2, c2), (r3, c3)):
        lefts.append(jnp.concatenate([a[...], b[...]], axis=0))
    total[...] = lax.dot_general(
        jnp.concatenate(lefts, axis=0),
        jnp.concatenate([g0[...], g1[...], g2[...], g3[...]], axis=0),
        (((0,), (0,)), ((), ())),
        preferred_element_type=F32,
    )
    for i, out in enumerate((mine, s1, s2, s3)):
        start = pl.multiple_of((depth ^ i) * block, block)
        out[...] = total[pl.ds(start, block), :].astype(out.dtype)


def weight_sum_kernel(mine, r1, r2, r3, out):
    out[...] = mine[...] + r1[...].astype(F32) + r2[...].astype(F32) + r3[...].astype(F32)


def halves(value, core):
    width = value.shape[1] // 2
    mine = lax.dynamic_slice_in_dim(value, core * width, width, axis=1)
    rest = lax.dynamic_slice_in_dim(value, (1 - core) * width, width, axis=1)
    return mine, rest


def in_order(mine, received, core, axis):
    return jnp.where(
        core == 0,
        jnp.concatenate([mine, received], axis=axis),
        jnp.concatenate([received, mine], axis=axis),
    )


def chip_body(features, weight, bias, node_mask, neighbour_tiles, tile_weights, out_grad):
    rows, cols = lax.axis_size("row"), lax.axis_size("col")
    devices = rows * cols
    r, c = lax.axis_index("row"), lax.axis_index("col")
    core = c & 1
    ids = jnp.stack([r & 3, core, (r & 1) * 2 + (c >> 1), r * 2 + (c >> 1), r >> 1]).astype(jnp.int32)
    nodes, width = features.shape[1:]
    half, quarter = width // 2, width // GROUP
    lists, tiles = neighbour_tiles[0, 0], tile_weights[0, 0]
    dests, slots, tile = tiles.shape[0], tiles.shape[1], tiles.shape[2]
    sources = rows
    groups = [
        [((zh * GROUP + g) * cols + y * 2 + k) for g in range(GROUP) for y in range(cols // 2)]
        for zh in range(rows // GROUP)
        for k in range(2)
    ]

    quarters = features[0].reshape(nodes, GROUP, quarter).transpose(1, 0, 2)
    source = lax.all_to_all(
        jnp.concatenate([quarters] * (rows // GROUP), axis=0), "row", 0, 0, tiled=True
    )
    lists_of = [lists] + [swap(lists, m) for m in (X, Z, X | Z)]
    tiles_of = [tiles, swap(tiles, X), swap(tiles, Z)]
    tiles_of.append(swap(tiles_of[2], X))

    mine, rest = halves(weight, core)
    block = in_order(mine, swap(rest, CORE), core, 0)
    along_z = [block, swap(block, Z), swap(block, 2 * Z), swap(block, 3 * Z)]
    weights = []
    for value in along_z:
        across = swap(value, X)
        weights += [value, swap(value, Y), across, swap(across, Y)]
    gathered = lax.all_to_all(
        jnp.broadcast_to(bias[None], (devices, bias.shape[0])), BOTH, 0, 0, tiled=True
    )
    bias_half = lax.dynamic_slice_in_dim(gathered.reshape(1, width), core * half, half, axis=1).astype(F32)

    keep_mask = node_mask[0][:, None]
    masked = out_grad[0] * keep_mask.astype(BF16)
    grad_own, grad_rest = halves(masked, core)
    grad_other = swap(grad_rest, CORE)

    piece = (GROUP, dests // 2, tile, quarter)
    kept, sent = call(
        gather_kernel, [shape(piece, F32), shape(piece, BF16)],
        ids, *lists_of, *tiles_of, source,
        smem=5, flops=2 * GROUP * dests * slots * tile * tile * quarter,
    )
    partial = (kept + swap(sent, CORE).astype(F32)).astype(BF16).reshape(-1, tile, quarter)
    terms = lax.all_to_all(partial, BOTH, 0, 0, axis_index_groups=groups, tiled=True)
    aggregate, p1, p2, p3 = call(
        aggregate_kernel,
        [shape((nodes, width), BF16)] + [shape((nodes, quarter), BF16)] * 3,
        ids, terms,
    )
    aggregate_other = swap(aggregate, CORE)

    act_own, act_other, pre_grad, back_own, back_other, bias_sum = call(
        dense_kernel,
        [shape((nodes, half), BF16)] * 2
        + [shape((2 * nodes, half), BF16), shape((nodes, width), F32), shape((nodes, width), BF16), shape((1, half), F32)],
        ids, aggregate, aggregate_other, bias_half, grad_own, grad_other, *weights,
        scratch=[pltpu.VMEM((2 * nodes, width), BF16)],
        flops=8 * nodes * half * width,
    )
    act = in_order(act_own, swap(act_other, CORE), core, 1)
    activations = jnp.where(keep_mask != 0, act, jnp.zeros_like(act))[None]

    (pieces,) = call(
        pieces_kernel, [shape((2 * GROUP, nodes, quarter), BF16)], back_own, swap(back_other, CORE), smem=0
    )
    same = lax.all_to_all(pieces, BOTH, 0, 0, axis_index_groups=groups, tiled=True)
    cross = swap(same, CORE)
    (spread,) = call(
        spread_kernel, [shape((sources, tile, quarter), BF16)],
        ids, *lists_of, *tiles_of, same, cross,
        scratch=[pltpu.VMEM((sources, tile, quarter), F32)],
        smem=5, flops=2 * GROUP * dests * slots * tile * tile * quarter,
    )
    grads = lax.all_to_all(spread, "row", 0, 0, tiled=True)
    (input_grad,) = call(finish_kernel, [shape((nodes, width), BF16)], grads, smem=0)

    received = [swap(p1, Y), swap(p2, X), swap(p3, X | Y)]
    crossed = [swap(p, CORE) for p in received]
    pre_grads = [pre_grad, swap(pre_grad, Y), swap(pre_grad, X), swap(pre_grad, X | Y)]
    mine, w1, w2, w3 = call(
        weight_grad_kernel,
        [shape((tile, half), F32)] + [shape((tile, half), BF16)] * 3,
        ids, aggregate, aggregate_other, *received, *crossed, *pre_grads,
        scratch=[pltpu.VMEM((quarter, half), F32)],
        flops=2 * quarter * half * 8 * nodes,
    )
    (summed,) = call(
        weight_sum_kernel, [shape((tile, half), F32)],
        mine, swap(w1, Z), swap(w2, 2 * Z), swap(w3, 3 * Z), smem=0,
    )
    own_rows = weight.shape[0]
    mine = lax.dynamic_slice_in_dim(summed, core * own_rows, own_rows, axis=0)
    rest = lax.dynamic_slice_in_dim(summed, (1 - core) * own_rows, own_rows, axis=0)
    weight_grad = in_order(mine, swap(rest, CORE), core, 1)

    nothing = jnp.zeros_like(bias_sum)
    placed = in_order(bias_sum, nothing, core, 1).reshape(devices, -1)
    bias_grad = jnp.sum(lax.all_to_all(placed, BOTH, 0, 0, tiled=True), axis=0)
    return activations, input_grad[None], weight_grad, bias_grad
def fetch_weights(weight, bias):
    return (
        lax.all_gather(weight, ("row", "col"), axis=0, tiled=True),
        lax.all_gather(bias, ("row", "col"), axis=0, tiled=True),
    )


def body(features, weight, bias, node_mask, neighbour_tiles, tile_weights, out_grad):
    tile = tile_weights.shape[-1]
    dest_count = neighbour_tiles.shape[2]
    slot_count = neighbour_tiles.shape[3]
    lists = neighbour_tiles[0, 0]
    valid = lists >= 0
    blocks = jnp.where(valid[:, :, None, None], tile_weights[0, 0], jnp.zeros((), jnp.bfloat16))
    group = 4
    turns = dest_count // group
    full_weight, full_bias = fetch_weights(weight, bias)
    source = lax.all_gather(features, "row", axis=1, tiled=True)[0]
    width = source.shape[-1]
    source_count = source.shape[0] // tile
    source_index = jnp.arange(source_count, dtype=jnp.int32)
    selector = ((lists[:, :, None] == source_index[None, None, :]) & valid[:, :, None]).astype(
        jnp.bfloat16
    )
    grouped_selector = selector.reshape(turns, group, slot_count, source_count)
    grouped_blocks = blocks.reshape(turns, group, slot_count, tile, tile)

    def dense_strip(group_selector, group_blocks):
        strip = jnp.einsum(
            "gsj,gsik->gijk", group_selector, group_blocks, preferred_element_type=jnp.float32
        )
        return strip.astype(jnp.bfloat16).reshape(group * tile, source_count * tile)

    def aggregate_group(pieces):
        group_selector, group_blocks = pieces
        strip = dense_strip(group_selector, group_blocks)
        return jnp.dot(strip, source, preferred_element_type=jnp.float32)

    partial_value = lax.map(aggregate_group, (grouped_selector, grouped_blocks)).reshape(-1, width)
    summed = lax.psum_scatter(partial_value, "col", scatter_dimension=0, tiled=True)
    aggregate = summed.astype(jnp.bfloat16)
    pre = jnp.dot(aggregate, full_weight, preferred_element_type=jnp.float32) + full_bias.astype(
        jnp.float32
    )
    keep = node_mask[0].astype(jnp.float32)[:, None]
    sigmoid_pre = jax.nn.sigmoid(pre)
    activations = (keep * (pre * sigmoid_pre)).astype(jnp.bfloat16)[None]
    slope = sigmoid_pre * (1.0 + pre * (1.0 - sigmoid_pre))
    pre_grad = (out_grad[0].astype(jnp.float32) * keep * slope).astype(jnp.bfloat16)
    weight_term = lax.dot_general(
        aggregate, pre_grad, (((0,), (0,)), ((), ())), preferred_element_type=jnp.float32
    )
    bias_term = jnp.sum(pre_grad.astype(jnp.float32), axis=0)
    weight_grad, bias_grad = (
        lax.psum_scatter(weight_term, ("row", "col"), scatter_dimension=0, tiled=True),
        lax.psum_scatter(bias_term, ("row", "col"), scatter_dimension=0, tiled=True),
    )
    aggregate_grad = lax.dot_general(
        pre_grad, full_weight, (((1,), (1,)), ((), ())), preferred_element_type=jnp.float32
    ).astype(jnp.bfloat16)
    dest_rows = lax.all_gather(aggregate_grad, "col", axis=0, tiled=True)
    grouped_grads = dest_rows.reshape(turns, group * tile, width)

    def spread_group(totals, pieces):
        group_selector, group_blocks, group_grads = pieces
        strip = dense_strip(group_selector, group_blocks)
        terms = lax.dot_general(
            strip, group_grads, (((0,), (0,)), ((), ())), preferred_element_type=jnp.float32
        )
        return (totals + terms, None)

    initial = jnp.zeros((source_count * tile, width), jnp.float32)
    source_terms, unused = lax.scan(
        spread_group, initial, (grouped_selector, grouped_blocks, grouped_grads)
    )
    input_grad = lax.psum_scatter(source_terms, "row", scatter_dimension=0, tiled=True)
    input_grad = input_grad.astype(jnp.bfloat16)[None]
    return (activations, input_grad, weight_grad, bias_grad)


def solution(mesh):
    chips = mesh.shape["row"] == 8 and mesh.shape["col"] == 4
    return jax.shard_map(
        chip_body if chips else body,
        mesh=mesh,
        in_specs=(
            P("col", "row", None),
            P(("row", "col"), None),
            P(("row", "col")),
            P("row", "col"),
            P("row", "col", None, None),
            P("row", "col", None, None, None, None),
            P("row", "col", None),
        ),
        out_specs=(
            P("row", "col", None),
            P("col", "row", None),
            P(("row", "col"), None),
            P(("row", "col")),
        ),
        check_vma=False,
    )
```

```python
import jax
import jax.numpy as jnp
from jax import lax
from jax.experimental import pallas as pl
from jax.experimental.pallas import tpu as pltpu
from jax.sharding import PartitionSpec as P

BOTH = ("row", "col")
F32 = jnp.float32
BF16 = jnp.bfloat16
VMEM = pl.BlockSpec(memory_space=pltpu.VMEM)
SMEM = pl.BlockSpec(memory_space=pltpu.SMEM)
CORE, Y, X, Z = 1, 2, 4, 8
GROUP = 4
SLOTS = 3
ROWS = 16


def swap(value, mask, total=32):
    return lax.ppermute(value, BOTH, [(i, i ^ mask) for i in range(total)])


def after(value, *others):
    return lax.optimization_barrier((value,) + others)[0]


def shape(dims, dtype):
    return jax.ShapeDtypeStruct(dims, dtype)


def call(kernel, outs, *operands, scratch=(), smem=1, flops=0, vmem=24):
    moved = sum(o.size * o.dtype.itemsize for o in operands)
    moved += sum(o.size * o.dtype.itemsize for o in outs)
    return pl.pallas_call(
        kernel,
        out_shape=outs,
        in_specs=[SMEM] * smem + [VMEM] * (len(operands) - smem),
        out_specs=[VMEM] * len(outs),
        scratch_shapes=list(scratch),
        compiler_params=pltpu.CompilerParams(vmem_limit_bytes=vmem * 2**20),
        cost_estimate=pl.CostEstimate(flops=flops, bytes_accessed=moved, transcendentals=0),
    )(*operands)


def split_kernel(ids, value, row, *pieces):
    part = pieces[0].shape[-1]
    for i, piece in enumerate(pieces):
        piece[:-ROWS] = value[:, pl.ds(pl.multiple_of((ids[7] ^ i) * part, part), part)]
        piece[-ROWS:] = row[...]


def split_masked_kernel(ids, mask, value, *pieces):
    part, lanes = pieces[0].shape[-1], mask.shape[-1]
    for i, piece in enumerate(pieces):
        start = pl.multiple_of((ids[7] ^ i) * part, part)
        for j in range(part // lanes):
            cols = pl.ds(start + j * lanes, lanes)
            piece[:, j * lanes : (j + 1) * lanes] = value[:, cols] * mask[...]


def block_kernel(ids, p0, p1, p2, p3, block):
    rows = p0.shape[0] - ROWS
    for i, piece in enumerate((p0, p1, p2, p3)):
        block[pl.ds(pl.multiple_of((ids[7] ^ i) * rows, rows), rows), :] = piece[:rows]
    block[4 * rows :] = p0[rows:] + p1[rows:] + p2[rows:] + p3[rows:]


def columns_kernel(ids, own, far, *pieces):
    member = ids[0]
    part, half = pieces[0].shape[-1] // 2, far.shape[-1] // 2
    for i, piece in enumerate(pieces):
        for j in range(2):
            cols = pl.ds(pl.multiple_of(j * half + (member ^ i) * part, part), part)
            piece[0, :, j * part : (j + 1) * part] = own[0, :, cols]
            piece[1, :, j * part : (j + 1) * part] = far[:, cols]


def gather_kernel(ids, lists, a0, a1, a2, a3, h0, h1, h2, h3, keep, send, source):
    member, core, row = ids[0], ids[1], ids[8]
    tile, dests = keep.shape[2], 2 * keep.shape[1]
    for i, piece in enumerate((h0, h1, h2, h3)):
        source[row ^ i] = piece[0]
        source[row ^ i ^ GROUP] = piece[1]
    for i, tiles in enumerate((a0, a1, a2, a3)):
        for pair in range(dests // 2):
            for other in range(2):
                m = pair * 2 + (core if other == 0 else 1 - core)
                left, right = [], []
                for s in range(SLOTS):
                    slot = m * SLOTS + s
                    listed = lists[i, slot]
                    block = tiles[pl.ds(pl.multiple_of(slot * tile, tile), tile), :]
                    left.append(jnp.where(listed >= 0, block, jnp.zeros_like(block)))
                    right.append(source[jnp.maximum(listed, 0)])
                total = jnp.dot(
                    jnp.concatenate(left, axis=1),
                    jnp.concatenate(right, axis=0),
                    preferred_element_type=F32,
                )
                if other == 0:
                    keep[member ^ i, pair] = total
                else:
                    send[member ^ i, pair] = total.astype(BF16)


def pair_sum_kernel(ids, kept, received, mine, send):
    y = ids[2]
    for g in range(GROUP):
        mine[g] = kept[g, y] + received[g, y].astype(F32)
        send[g] = (kept[g, 1 - y] + received[g, 1 - y].astype(F32)).astype(BF16)


def group_kernel(ids, mine, received, near, far):
    low = ids[6]
    for out, z in ((near, low), (far, 1 - low)):
        for x in range(2):
            out[x] = (mine[2 * z + x] + received[2 * z + x].astype(F32)).astype(BF16)


def aggregate_kernel(ids, own, rx, rz, rxz, full, away):
    member, y = ids[0], ids[2]
    nodes, part, half = own.shape[1], own.shape[2] // 2, full.shape[1] // 2
    for i, term in enumerate((own, rx, rz, rxz)):
        for j in range(2):
            cols = pl.ds(pl.multiple_of(j * half + (member ^ i) * part, part), part)
            for x in range(2):
                full[x * nodes : (x + 1) * nodes, cols] = term[x, :, j * part : (j + 1) * part]
    block = full.shape[1] // 16
    for i in range(8):
        cols = pl.ds(pl.multiple_of((2 * i + 1 - y) * block, block), block)
        away[:, i * block : (i + 1) * block] = full[:, cols]


def dense_kernel(ids, own, other, o0, o1, o2, o3, *rest):
    weights = rest[:8]
    a0, a1, a2, a3, pre_grad, back_own, back_other, left, grads, acts = rest[8:]
    y, z, x = ids[2], ids[3], ids[5]
    pair, width = own.shape
    nodes, block = pair // 2, width // 16
    part = pre_grad.shape[1]

    def chip(i, other_x):
        return pl.multiple_of(((z ^ (i >> 1)) * 4 + other_x * 2 + (y ^ (i & 1))) * block, block)

    def place(i):
        return pl.ds(pl.multiple_of((i & 1) * pair + (x ^ (i >> 1)) * nodes, nodes), nodes)

    for i in range(8):
        for j in range(2):
            cols = slice((2 * i + j) * block, (2 * i + j + 1) * block)
            left[:pair, cols] = own[:, pl.ds(chip(i, j), block)]
            left[pair:, cols] = other[:, pl.ds(chip(i, j), block)]
    for i, piece in enumerate((o0, o1, o2, o3)):
        grads[place(i), :] = piece[...]
    many = 2 * block
    bias = sum(
        w[many:, :].astype(F32) * (z ^ (i >> 1) == ids[7]).astype(F32) for i, w in enumerate(weights)
    )[:1]
    step = 256
    for n in range(part // step):
        cols = slice(n * step, (n + 1) * step)
        matrix = jnp.concatenate([w[:many, cols] for w in weights], axis=0)
        pre = jnp.dot(left[...], matrix, preferred_element_type=F32) + bias[:, cols]
        sigmoid = 1.0 / (1.0 + jnp.exp(-pre))
        acts[:, cols] = (pre * sigmoid).astype(BF16)
        slope = sigmoid * (1.0 + pre * (1.0 - sigmoid))
        grad = (grads[:, cols].astype(F32) * slope).astype(BF16)
        pre_grad[:, cols] = grad
    for i, piece in enumerate((a0, a1, a2, a3)):
        piece[...] = acts[place(i), :]
    for i, weight in enumerate(weights):
        back = lax.dot_general(
            pre_grad[...], weight[:many, :], (((1,), (1,)), ((), ())), preferred_element_type=F32
        )
        for j in range(2):
            cols = pl.ds(chip(i, j), block)
            back_own[:, cols] = back[:pair, j * block : (j + 1) * block]
            back_other[:, cols] = back[pair:, j * block : (j + 1) * block].astype(BF16)


def back_kernel(ids, own, received, v0, v1, v2, v3):
    member = ids[0]
    nodes, part, half = v0.shape[1], v0.shape[2] // 2, own.shape[1] // 2
    for i, out in enumerate((v0, v1, v2, v3)):
        for j in range(2):
            cols = pl.ds(pl.multiple_of(j * half + (member ^ i) * part, part), part)
            for x in range(2):
                rows = slice(x * nodes, (x + 1) * nodes)
                total = own[rows, cols] + received[rows, cols].astype(F32)
                out[x, :, j * part : (j + 1) * part] = total.astype(out.dtype)


def add_kernel(v0, vx, vz, vxz, out):
    out[:2] = (v0[...] + vx[...].astype(F32)).astype(BF16)
    out[2:] = (vz[...].astype(F32) + vxz[...].astype(F32)).astype(BF16)


def spread_kernel(ids, lists, a0, a1, a2, a3, *rest):
    grads, (out, total) = rest[:4], rest[4:]
    core, y, x = ids[1], ids[2], ids[5]
    tile = out.shape[1]
    total[...] = jnp.zeros_like(total)
    for i, tiles in enumerate((a0, a1, a2, a3)):
        for away in range(4):
            m = (y ^ (away >> 1)) * 2 + (core ^ (away & 1))
            left = []
            for s in range(SLOTS):
                slot = m * SLOTS + s
                block = tiles[pl.ds(pl.multiple_of(slot * tile, tile), tile), :]
                left.append(jnp.where(lists[i, slot] >= 0, block, jnp.zeros_like(block)))
            terms = lax.dot_general(
                jnp.concatenate(left, axis=1), grads[away][2 * (i >> 1) + (x ^ (i & 1))],
                (((0,), (0,)), ((), ())), preferred_element_type=F32,
            )
            for s in range(SLOTS):
                at = jnp.maximum(lists[i, m * SLOTS + s], 0)
                total[at] += terms[s * tile : (s + 1) * tile]
    out[...] = total[...].astype(BF16)


def finish_kernel(terms, out):
    part, half = terms.shape[-1] // 2, out.shape[-1] // 2
    for g in range(GROUP):
        total = sum(terms[i].astype(F32) for i in range(g, terms.shape[0], GROUP)).astype(BF16)
        out[:, g * part : (g + 1) * part] = total[:, :part]
        out[:, half + g * part : half + (g + 1) * part] = total[:, part:]


def act_kernel(ids, mask, a0, a1, a2, a3, out):
    part, lanes = a0.shape[-1], mask.shape[-1]
    for i, piece in enumerate((a0, a1, a2, a3)):
        start = pl.multiple_of((ids[7] ^ i) * part, part)
        for j in range(part // lanes):
            out[:, pl.ds(start + j * lanes, lanes)] = piece[:, j * lanes : (j + 1) * lanes] * mask[...]


def weight_grad_kernel(ids, own, other, away, away_other, g0, g1, keep, send, row, left, total):
    y, high, low = ids[2], ids[4], ids[6]
    pair, block = own.shape[0], keep.shape[1]
    for i in range(8):
        take = pl.ds(pl.multiple_of((2 * i + y) * block, block), block)
        cols = slice(i * block, (i + 1) * block)
        left[:pair, cols] = own[:, take]
        left[pair : 2 * pair, cols] = other[:, take]
    left[2 * pair : 3 * pair, :] = away[...]
    left[3 * pair :, :] = away_other[...]
    total[...] = lax.dot_general(
        left[...], jnp.concatenate([g0[...], g1[...]], axis=0),
        (((0,), (0,)), ((), ())), preferred_element_type=F32,
    )
    for j in range(2):
        for i in range(2):
            for out, flip in ((keep, 0), (send, 1)):
                at = (high ^ j) * 4 + (low ^ flip) * 2 + i
                rows = pl.ds(pl.multiple_of(at * block, block), block)
                value = total[rows, :].astype(out.dtype)
                if flip:
                    out[(2 * j + i) * block : (2 * j + i + 1) * block, :] = value
                else:
                    out[2 * j + i] = value
    sums = sum(jnp.sum(g[...].astype(F32), axis=0, keepdims=True) for g in (g0, g1))
    row[...] = jnp.broadcast_to(sums, row.shape)
    send[4 * block :, :] = row[...].astype(send.dtype)


def fold_low_kernel(ids, keep, row, received, own, send, both):
    x, block = ids[5], keep.shape[1]
    for i in range(4):
        total = keep[i] + received[i * block : (i + 1) * block, :].astype(F32)
        place = jnp.int32(i & 1) == x
        j = i >> 1

        @pl.when(place)
        def _():
            own[j] = total

        @pl.when(jnp.logical_not(place))
        def _():
            send[j * block : (j + 1) * block, :] = total.astype(BF16)

    both[...] = row[...] + received[4 * block :, :].astype(F32)
    send[2 * block :, :] = both[...].astype(BF16)


def fold_x_kernel(own, row, received, mine, rows, send):
    block = own.shape[1]
    mine[0] = own[0]
    mine[1] = received[:block, :].astype(F32)
    send[:block, :] = own[1].astype(BF16)
    send[block : 2 * block, :] = received[block : 2 * block, :]
    rows[0] = row[...]
    rows[1] = received[2 * block :, :].astype(F32)
    send[2 * block : 2 * block + ROWS, :] = row[...].astype(BF16)
    send[2 * block + ROWS :, :] = received[2 * block :, :]


def fold_high_kernel(ids, own, rows, received, mine, sums, send):
    core, block = ids[1], own.shape[1]
    many = mine.shape[1]
    for i in range(2):
        for out, k in ((mine, core), (send, 1 - core)):
            at = pl.multiple_of(k * many, many)
            take = pl.ds(pl.multiple_of(i * block + k * many, many), many)
            value = own[i, pl.ds(at, many), :] + received[take, :].astype(F32)
            if out is mine:
                out[i] = value
            else:
                out[i * many : (i + 1) * many, :] = value
        first = 2 * block + i * ROWS
        sums[i] = rows[i] + received[first : first + ROWS, :].astype(F32)
        send[2 * many + i * ROWS : 2 * many + (i + 1) * ROWS, :] = sums[i]


def weight_out_kernel(ids, mine, sums, received, out, bias):
    many, part = mine.shape[1:]
    block = 2 * many
    for i in range(2):
        cols = pl.ds(pl.multiple_of((ids[7] ^ (2 * i)) * part, part), part)
        out[:, cols] = mine[i]
        cols = pl.ds(pl.multiple_of((ids[7] ^ (2 * i + 1)) * part, part), part)
        out[:, cols] = received[i * many : (i + 1) * many, :]
    quarters = (
        sums[0], received[block : block + ROWS, :], sums[1], received[block + ROWS :, :],
    )
    bias[...] = sum(q * (ids[3] ^ ids[7] == i).astype(F32) for i, q in enumerate(quarters))


def chip_body(features, weight, bias, node_mask, neighbour_tiles, tile_weights, out_grad):
    rows, cols = lax.axis_size("row"), lax.axis_size("col")
    devices = rows * cols
    r, c = lax.axis_index("row"), lax.axis_index("col")
    core, z = c & 1, r >> 1
    place = (r & 1) * 2 + core
    ids = jnp.stack([r & 3, core, c >> 1, z, r >> 2, r & 1, z & 1, place, r]).astype(jnp.int32)
    nodes, width = features.shape[1:]
    half, quarter = width // 2, width // GROUP
    lists, tiles = neighbour_tiles[0, 0], tile_weights[0, 0]
    dests, slots, tile = tiles.shape[0], tiles.shape[1], tiles.shape[2]
    masks = (X, Z, X | Z)
    shares = (CORE, X, X | CORE)

    lists = jnp.pad(lists.reshape(1, -1), ((0, 15), (0, tile - dests * slots))).astype(BF16)
    tiles = jnp.concatenate([tiles.reshape(-1, tile), lists], axis=0)
    tiles_of = [tiles, swap(tiles, X), swap(tiles, Z)]
    tiles_of.append(swap(tiles_of[2], X))
    lists_of = jnp.stack([t[-16, : dests * slots] for t in tiles_of]).astype(jnp.int32)

    own_rows = weight.shape[0]
    at = (r & 1) * (quarter // 2) + c * own_rows
    row = lax.dynamic_update_slice(jnp.zeros((ROWS, quarter), BF16), bias[None], (0, at))
    pieces = call(split_kernel, [shape((own_rows + ROWS, quarter), BF16)] * 4, ids, weight, row)
    pieces = [pieces[0]] + [swap(p, m) for p, m in zip(pieces[1:], shares)]
    pieces[0] = after(pieces[0], tiles_of[1])
    (block,) = call(block_kernel, [shape((4 * own_rows + ROWS, quarter), BF16)], ids, *pieces)

    columns = call(
        columns_kernel, [shape((2, nodes, quarter), BF16)] * 4, ids, features, swap(features[0], 2 * Z)
    )
    source = [columns[0]] + [swap(value, m) for value, m in zip(columns[1:], masks)]
    y0, z1, z2 = [swap(block, m) for m in (Y, Z, 2 * Z)]
    z3 = swap(z2, Z)
    y1, y2, y3 = [swap(value, Y) for value in (z1, z2, z3)]
    weights = [block, y0, z1, y1, z2, y2, z3, y3]

    lanes = jnp.broadcast_to(node_mask[0][:, None].astype(BF16), (nodes, 128))
    grads = call(split_masked_kernel, [shape((nodes, quarter), BF16)] * 4, ids, lanes, out_grad[0])
    grads = [grads[0]] + [swap(g, m) for g, m in zip(grads[1:], shares)]

    source[0] = after(source[0], y0, z1, z2)
    piece = (GROUP, dests // 2, tile, quarter)
    kept, sent = call(
        gather_kernel, [shape(piece, F32), shape(piece, BF16)],
        ids, lists_of, *tiles_of, *source,
        scratch=[pltpu.VMEM((rows, tile, quarter), BF16)],
        smem=2, flops=2 * GROUP * dests * slots * tile * tile * quarter,
    )
    mine, send = call(
        pair_sum_kernel, [shape((GROUP, tile, quarter), F32), shape((GROUP, tile, quarter), BF16)],
        ids, kept, swap(after(sent, y1), CORE),
    )
    received = after(swap(send, Y), z3, y2, grads[2], grads[3])
    near, far = call(group_kernel, [shape((2, tile, quarter), BF16)] * 2, ids, mine, received)
    aggregate, away = call(
        aggregate_kernel, [shape((2 * nodes, width), BF16), shape((2 * nodes, half), BF16)],
        ids, after(near, y3), swap(near, X), swap(far, Z), swap(far, X | Z),
    )
    aggregate_other = swap(aggregate, CORE)
    away = swap(away, Y)
    away_other = swap(away, CORE)

    *acts, pre_grad, back_own, back_other = call(
        dense_kernel,
        [shape((nodes, quarter), BF16)] * 4
        + [shape((4 * nodes, quarter), BF16)]
        + [shape((2 * nodes, width), F32), shape((2 * nodes, width), BF16)],
        ids, aggregate, aggregate_other, *grads, *weights,
        scratch=[pltpu.VMEM((4 * nodes, width), BF16)] + [pltpu.VMEM((4 * nodes, quarter), BF16)] * 2,
        flops=16 * nodes * quarter * width, vmem=56,
    )

    v0, *others = call(
        back_kernel, [shape((2, nodes, quarter), F32)] + [shape((2, nodes, quarter), BF16)] * 3,
        ids, back_own, swap(back_other, CORE),
    )
    vx, vz, vxz = [swap(v, m) for v, m in zip(others, masks)]
    pre_grad_y = swap(pre_grad, Y)
    grads_own = call(add_kernel, [shape((4, nodes, quarter), BF16)], v0, vx, vz, vxz, smem=0)[0]
    grads_away = swap(grads_own, Y)
    keep, send, row = call(
        weight_grad_kernel,
        [shape((4, tile, quarter), F32), shape((4 * tile + ROWS, quarter), BF16), shape((ROWS, quarter), F32)],
        ids, aggregate, aggregate_other, away, away_other, pre_grad, pre_grad_y,
        scratch=[pltpu.VMEM((8 * nodes, half), BF16), pltpu.VMEM((half, quarter), F32)],
        flops=16 * nodes * quarter * half,
    )
    grads_away, send = lax.optimization_barrier((grads_away, send))
    (spread,) = call(
        spread_kernel, [shape((rows, tile, quarter), BF16)],
        ids, lists_of, *tiles_of,
        grads_own, swap(grads_own, CORE), grads_away, swap(grads_away, CORE),
        scratch=[pltpu.VMEM((rows, tile, quarter), F32)],
        smem=2, flops=2 * GROUP * dests * slots * tile * tile * quarter,
    )

    acts = [acts[0]] + [swap(a, m) for a, m in zip(acts[1:], shares)]
    received = swap(send, Z)
    spread = after(spread, received)
    spread_all = lax.all_to_all(spread, "row", 0, 0, tiled=True)
    own, send, row = call(
        fold_low_kernel,
        [shape((2, tile, quarter), F32), shape((2 * tile + ROWS, quarter), BF16), shape((ROWS, quarter), F32)],
        ids, keep, row, received,
    )
    own, rows_of, send = call(
        fold_x_kernel,
        [shape((2, tile, quarter), F32), shape((2, ROWS, quarter), F32), shape((2 * tile + 2 * ROWS, quarter), BF16)],
        own, row, swap(send, X), smem=0,
    )
    own = after(own, *acts[1:])
    own, rows_of, send = call(
        fold_high_kernel,
        [shape((2, own_rows, quarter), F32), shape((2, ROWS, quarter), F32), shape((2 * own_rows + 2 * ROWS, quarter), F32)],
        ids, own, rows_of, swap(send, 2 * Z),
    )
    weight_grad, row = call(
        weight_out_kernel, [shape((own_rows, width), F32), shape((ROWS, quarter), F32)],
        ids, own, rows_of, swap(send, CORE),
    )
    bias_grad = lax.dynamic_slice_in_dim(row[0], at, own_rows)

    (activations,) = call(act_kernel, [shape((nodes, width), BF16)], ids, lanes, *acts)
    (input_grad,) = call(finish_kernel, [shape((nodes, width), BF16)], spread_all, smem=0)
    return activations[None], input_grad[None], weight_grad, bias_grad


def fetch_weights(weight, bias):
    return (
        lax.all_gather(weight, ("row", "col"), axis=0, tiled=True),
        lax.all_gather(bias, ("row", "col"), axis=0, tiled=True),
    )


def body(features, weight, bias, node_mask, neighbour_tiles, tile_weights, out_grad):
    tile = tile_weights.shape[-1]
    dest_count = neighbour_tiles.shape[2]
    slot_count = neighbour_tiles.shape[3]
    lists = neighbour_tiles[0, 0]
    valid = lists >= 0
    blocks = jnp.where(valid[:, :, None, None], tile_weights[0, 0], jnp.zeros((), jnp.bfloat16))
    group = 4
    turns = dest_count // group
    full_weight, full_bias = fetch_weights(weight, bias)
    source = lax.all_gather(features, "row", axis=1, tiled=True)[0]
    width = source.shape[-1]
    source_count = source.shape[0] // tile
    source_index = jnp.arange(source_count, dtype=jnp.int32)
    selector = ((lists[:, :, None] == source_index[None, None, :]) & valid[:, :, None]).astype(
        jnp.bfloat16
    )
    grouped_selector = selector.reshape(turns, group, slot_count, source_count)
    grouped_blocks = blocks.reshape(turns, group, slot_count, tile, tile)

    def dense_strip(group_selector, group_blocks):
        strip = jnp.einsum(
            "gsj,gsik->gijk", group_selector, group_blocks, preferred_element_type=jnp.float32
        )
        return strip.astype(jnp.bfloat16).reshape(group * tile, source_count * tile)

    def aggregate_group(pieces):
        group_selector, group_blocks = pieces
        strip = dense_strip(group_selector, group_blocks)
        return jnp.dot(strip, source, preferred_element_type=jnp.float32)

    partial_value = lax.map(aggregate_group, (grouped_selector, grouped_blocks)).reshape(-1, width)
    summed = lax.psum_scatter(partial_value, "col", scatter_dimension=0, tiled=True)
    aggregate = summed.astype(jnp.bfloat16)
    pre = jnp.dot(aggregate, full_weight, preferred_element_type=jnp.float32) + full_bias.astype(
        jnp.float32
    )
    keep = node_mask[0].astype(jnp.float32)[:, None]
    sigmoid_pre = jax.nn.sigmoid(pre)
    activations = (keep * (pre * sigmoid_pre)).astype(jnp.bfloat16)[None]
    slope = sigmoid_pre * (1.0 + pre * (1.0 - sigmoid_pre))
    pre_grad = (out_grad[0].astype(jnp.float32) * keep * slope).astype(jnp.bfloat16)
    weight_term = lax.dot_general(
        aggregate, pre_grad, (((0,), (0,)), ((), ())), preferred_element_type=jnp.float32
    )
    bias_term = jnp.sum(pre_grad.astype(jnp.float32), axis=0)
    weight_grad, bias_grad = (
        lax.psum_scatter(weight_term, ("row", "col"), scatter_dimension=0, tiled=True),
        lax.psum_scatter(bias_term, ("row", "col"), scatter_dimension=0, tiled=True),
    )
    aggregate_grad = lax.dot_general(
        pre_grad, full_weight, (((1,), (1,)), ((), ())), preferred_element_type=jnp.float32
    ).astype(jnp.bfloat16)
    dest_rows = lax.all_gather(aggregate_grad, "col", axis=0, tiled=True)
    grouped_grads = dest_rows.reshape(turns, group * tile, width)

    def spread_group(totals, pieces):
        group_selector, group_blocks, group_grads = pieces
        strip = dense_strip(group_selector, group_blocks)
        terms = lax.dot_general(
            strip, group_grads, (((0,), (0,)), ((), ())), preferred_element_type=jnp.float32
        )
        return (totals + terms, None)

    initial = jnp.zeros((source_count * tile, width), jnp.float32)
    source_terms, unused = lax.scan(
        spread_group, initial, (grouped_selector, grouped_blocks, grouped_grads)
    )
    input_grad = lax.psum_scatter(source_terms, "row", scatter_dimension=0, tiled=True)
    input_grad = input_grad.astype(jnp.bfloat16)[None]
    return (activations, input_grad, weight_grad, bias_grad)


def solution(mesh):
    chips = mesh.shape["row"] == 8 and mesh.shape["col"] == 4
    return jax.shard_map(
        chip_body if chips else body,
        mesh=mesh,
        in_specs=(
            P("col", "row", None),
            P(("row", "col"), None),
            P(("row", "col")),
            P("row", "col"),
            P("row", "col", None, None),
            P("row", "col", None, None, None, None),
            P("row", "col", None),
        ),
        out_specs=(
            P("row", "col", None),
            P("col", "row", None),
            P(("row", "col"), None),
            P(("row", "col")),
        ),
        check_vma=False,
    )
```

```python
import functools

import jax
import jax.numpy as jnp
from jax import lax
from jax.experimental import pallas as pl
from jax.experimental.pallas import tpu as pltpu
from jax.sharding import PartitionSpec as P

BOTH = ("row", "col")
F32 = jnp.float32
BF16 = jnp.bfloat16
VMEM = pl.BlockSpec(memory_space=pltpu.VMEM)
SMEM = pl.BlockSpec(memory_space=pltpu.SMEM)
CORE, Y, X, Z = 1, 2, 4, 8
GROUP = 4
SLOTS = 3
ROWS = 16


def swap(value, mask, total=32):
    return lax.ppermute(value, BOTH, [(i, i ^ mask) for i in range(total)])


def after(value, *others):
    return lax.optimization_barrier((value,) + others)[0]


def shape(dims, dtype):
    return jax.ShapeDtypeStruct(dims, dtype)


def call(kernel, outs, *operands, scratch=(), smem=1, flops=0, vmem=24):
    moved = sum(o.size * o.dtype.itemsize for o in operands)
    moved += sum(o.size * o.dtype.itemsize for o in outs)
    return pl.pallas_call(
        kernel,
        out_shape=outs,
        in_specs=[SMEM] * smem + [VMEM] * (len(operands) - smem),
        out_specs=[VMEM] * len(outs),
        scratch_shapes=list(scratch),
        compiler_params=pltpu.CompilerParams(vmem_limit_bytes=vmem * 2**20),
        cost_estimate=pl.CostEstimate(flops=flops, bytes_accessed=moved, transcendentals=0),
    )(*operands)


def split_kernel(ids, value, row, *pieces):
    part = pieces[0].shape[-1]
    for i, piece in enumerate(pieces):
        piece[:-ROWS] = value[:, pl.ds(pl.multiple_of((ids[7] ^ i) * part, part), part)]
        piece[-ROWS:] = row[...]


def split_masked_kernel(ids, mask, value, *pieces):
    part, lanes = pieces[0].shape[-1], mask.shape[-1]
    for i, piece in enumerate(pieces):
        start = pl.multiple_of((ids[7] ^ i) * part, part)
        for j in range(part // lanes):
            cols = pl.ds(start + j * lanes, lanes)
            piece[:, j * lanes : (j + 1) * lanes] = value[:, cols] * mask[...]


def block_kernel(ids, p0, p1, p2, p3, block):
    rows = p0.shape[0] - ROWS
    for i, piece in enumerate((p0, p1, p2, p3)):
        block[pl.ds(pl.multiple_of((ids[7] ^ i) * rows, rows), rows), :] = piece[:rows]
    block[4 * rows :] = p0[rows:] + p1[rows:] + p2[rows:] + p3[rows:]


def columns_kernel(ids, own, far, *pieces):
    member = ids[0]
    part, half = pieces[0].shape[-1] // 2, far.shape[-1] // 2
    for i, piece in enumerate(pieces):
        for j in range(2):
            cols = pl.ds(pl.multiple_of(j * half + (member ^ i) * part, part), part)
            piece[0, :, j * part : (j + 1) * part] = own[0, :, cols]
            piece[1, :, j * part : (j + 1) * part] = far[:, cols]


def gather_kernel(ids, lists, a0, a1, a2, a3, h0, h1, h2, h3, keep, send, source):
    member, core, row = ids[0], ids[1], ids[8]
    tile, dests = keep.shape[2], 2 * keep.shape[1]
    for i, piece in enumerate((h0, h1, h2, h3)):
        source[row ^ i] = piece[0]
        source[row ^ i ^ GROUP] = piece[1]
    for i, tiles in enumerate((a0, a1, a2, a3)):
        for pair in range(dests // 2):
            for other in range(2):
                m = pair * 2 + (core if other == 0 else 1 - core)
                left, right = [], []
                for s in range(SLOTS):
                    slot = m * SLOTS + s
                    listed = lists[i, slot]
                    block = tiles[pl.ds(pl.multiple_of(slot * tile, tile), tile), :]
                    left.append(jnp.where(listed >= 0, block, jnp.zeros_like(block)))
                    right.append(source[jnp.maximum(listed, 0)])
                total = jnp.dot(
                    jnp.concatenate(left, axis=1),
                    jnp.concatenate(right, axis=0),
                    preferred_element_type=F32,
                )
                if other == 0:
                    keep[member ^ i, pair] = total
                else:
                    send[member ^ i, pair] = total.astype(BF16)


def pair_sum_kernel(ids, kept, received, mine, send):
    y = ids[2]
    for g in range(GROUP):
        mine[g] = kept[g, y] + received[g, y].astype(F32)
        send[g] = (kept[g, 1 - y] + received[g, 1 - y].astype(F32)).astype(BF16)


def group_kernel(ids, mine, received, near, far):
    low = ids[6]
    for out, z in ((near, low), (far, 1 - low)):
        for x in range(2):
            nodes = mine.shape[1]
            total = mine[2 * z + x] + received[2 * z + x].astype(F32)
            out[x * nodes : (x + 1) * nodes, :] = total.astype(BF16)
        out[2 * nodes :, :] = jnp.zeros((out.shape[0] - 2 * nodes, out.shape[1]), BF16)


def aggregate_kernel(ids, own, rx, rz, rxz, full):
    member = ids[0]
    nodes, part, half = full.shape[0] // 2, own.shape[1] // 2, full.shape[1] // 2
    for i, term in enumerate((own, rx, rz, rxz)):
        for j in range(2):
            cols = pl.ds(pl.multiple_of(j * half + (member ^ i) * part, part), part)
            for x in range(2):
                full[x * nodes : (x + 1) * nodes, cols] = term[x * nodes : (x + 1) * nodes, j * part : (j + 1) * part]


def dense_kernel(ids, own, other, o0, o1, o2, o3, *rest):
    weights = rest[:8]
    a0, a1, a2, a3, pre_grad, back_own, back_other, left, grads, acts = rest[8:]
    y, z, x = ids[2], ids[3], ids[5]
    pair, width = own.shape
    nodes, block = pair // 2, width // 16
    part = pre_grad.shape[1]

    def chip(i, other_x):
        return pl.multiple_of(((z ^ (i >> 1)) * 4 + other_x * 2 + (y ^ (i & 1))) * block, block)

    def place(i):
        return pl.ds(pl.multiple_of((i & 1) * pair + (x ^ (i >> 1)) * nodes, nodes), nodes)

    for i in range(8):
        for j in range(2):
            cols = slice((2 * i + j) * block, (2 * i + j + 1) * block)
            left[:pair, cols] = own[:, pl.ds(chip(i, j), block)]
            left[pair:, cols] = other[:, pl.ds(chip(i, j), block)]
    for i, piece in enumerate((o0, o1, o2, o3)):
        grads[place(i), :] = piece[...]
    many = 2 * block
    bias = sum(
        w[many:, :].astype(F32) * (z ^ (i >> 1) == ids[7]).astype(F32) for i, w in enumerate(weights)
    )[:1]
    step = 256
    for n in range(part // step):
        cols = slice(n * step, (n + 1) * step)
        matrix = jnp.concatenate([w[:many, cols] for w in weights], axis=0)
        pre = jnp.dot(left[...], matrix, preferred_element_type=F32) + bias[:, cols]
        sigmoid = 1.0 / (1.0 + jnp.exp(-pre))
        acts[:, cols] = (pre * sigmoid).astype(BF16)
        slope = sigmoid * (1.0 + pre * (1.0 - sigmoid))
        grad = (grads[:, cols].astype(F32) * slope).astype(BF16)
        pre_grad[:, cols] = grad
    for i, piece in enumerate((a0, a1, a2, a3)):
        piece[...] = acts[place(i), :]
    for i, weight in enumerate(weights):
        back = lax.dot_general(
            pre_grad[...], weight[:many, :], (((1,), (1,)), ((), ())), preferred_element_type=F32
        )
        for j in range(2):
            cols = pl.ds(chip(i, j), block)
            back_own[:, cols] = back[:pair, j * block : (j + 1) * block]
            back_other[:, cols] = back[pair:, j * block : (j + 1) * block].astype(BF16)


def back_kernel(ids, own, received, v0, v1, v2, v3):
    member = ids[0]
    nodes, part, half = v0.shape[1], v0.shape[2] // 2, own.shape[1] // 2
    for i, out in enumerate((v0, v1, v2, v3)):
        for j in range(2):
            cols = pl.ds(pl.multiple_of(j * half + (member ^ i) * part, part), part)
            for x in range(2):
                rows = slice(x * nodes, (x + 1) * nodes)
                total = own[rows, cols] + received[rows, cols].astype(F32)
                out[x, :, j * part : (j + 1) * part] = total.astype(out.dtype)


def add_kernel(v0, vx, vz, vxz, out):
    out[:2] = (v0[...] + vx[...].astype(F32)).astype(BF16)
    out[2:] = (vz[...].astype(F32) + vxz[...].astype(F32)).astype(BF16)


def spread_kernel(ids, lists, a0, a1, a2, a3, *rest):
    grads, (out, total) = rest[:4], rest[4:]
    core, y, x = ids[1], ids[2], ids[5]
    tile = out.shape[1]
    total[...] = jnp.zeros_like(total)
    for i, tiles in enumerate((a0, a1, a2, a3)):
        for away in range(4):
            m = (y ^ (away >> 1)) * 2 + (core ^ (away & 1))
            left = []
            for s in range(SLOTS):
                slot = m * SLOTS + s
                block = tiles[pl.ds(pl.multiple_of(slot * tile, tile), tile), :]
                left.append(jnp.where(lists[i, slot] >= 0, block, jnp.zeros_like(block)))
            terms = lax.dot_general(
                jnp.concatenate(left, axis=1), grads[away][2 * (i >> 1) + (x ^ (i & 1))],
                (((0,), (0,)), ((), ())), preferred_element_type=F32,
            )
            for s in range(SLOTS):
                at = jnp.maximum(lists[i, m * SLOTS + s], 0)
                total[at] += terms[s * tile : (s + 1) * tile]
    out[...] = total[...].astype(BF16)


def finish_kernel(terms, out):
    part, half = terms.shape[-1] // 2, out.shape[-1] // 2
    for g in range(GROUP):
        total = sum(terms[i].astype(F32) for i in range(g, terms.shape[0], GROUP)).astype(BF16)
        out[:, g * part : (g + 1) * part] = total[:, :part]
        out[:, half + g * part : half + (g + 1) * part] = total[:, part:]


def act_kernel(ids, mask, a0, a1, a2, a3, out):
    part, lanes = a0.shape[-1], mask.shape[-1]
    for i, piece in enumerate((a0, a1, a2, a3)):
        start = pl.multiple_of((ids[7] ^ i) * part, part)
        for j in range(part // lanes):
            out[:, pl.ds(start + j * lanes, lanes)] = piece[:, j * lanes : (j + 1) * lanes] * mask[...]


def weight_grad_kernel(far, ids, own, other, grads, keep, send, *rest):
    y, low = ids[2], ids[6]
    block = keep.shape[1]
    row, total = rest if far else (None,) + rest
    z = 1 - low if far else low
    for j in range(2):
        cols = pl.ds(pl.multiple_of((j * 8 + z * 4) * block, block), 4 * block)
        total[4 * j * block : 4 * (j + 1) * block, :] = lax.dot_general(
            jnp.concatenate([own[:, cols], other[:, cols]], axis=0), grads[...],
            (((0,), (0,)), ((), ())), preferred_element_type=F32,
        )
    for i in range(4):
        keep[i] = total[pl.ds(pl.multiple_of((2 * i + y) * block, block), block), :]
        value = total[pl.ds(pl.multiple_of((2 * i + 1 - y) * block, block), block), :]
        send[i * block : (i + 1) * block, :] = value.astype(BF16)
    if far:
        sums = jnp.sum(grads[...].astype(F32), axis=0, keepdims=True)
        row[...] = jnp.broadcast_to(sums, row.shape)
        send[4 * block :, :] = row[...].astype(BF16)


def fold_y_kernel(keep, row, received, send, both):
    block = keep.shape[1]
    for i in range(4):
        rows = slice(i * block, (i + 1) * block)
        send[rows, :] = (keep[i] + received[rows, :].astype(F32)).astype(BF16)
    both[...] = row[...] + received[4 * block :, :].astype(F32)
    send[4 * block :, :] = both[...].astype(BF16)


def fold_low_kernel(ids, keep, row, from_y, from_z, own, sums, s1, s2, s3):
    high, x, block = ids[4], ids[5], keep.shape[1]
    sums[...] = row[...] + from_z[4 * block :, :].astype(F32)
    for i, out in enumerate((own, s1, s2, s3)):
        at = (high ^ (i >> 1)) * 2 + (x ^ (i & 1))
        rows = pl.ds(pl.multiple_of(at * block, block), block)
        total = keep[at] + from_y[rows, :].astype(F32) + from_z[rows, :].astype(F32)
        if out is own:
            own[...] = total
        else:
            out[:block, :] = total.astype(BF16)
            out[block:, :] = sums[...].astype(BF16)


def fold_high_kernel(ids, own, row, r1, r2, r3, mine, sums, send):
    core, block = ids[1], own.shape[0]
    many = mine.shape[1]
    for i in range(2):
        for out, k in ((mine, core), (send, 1 - core)):
            at = pl.ds(pl.multiple_of(k * many, many), many)
            if i == 0:
                value = own[at, :] + r2[at, :].astype(F32)
            else:
                value = r1[at, :].astype(F32) + r3[at, :].astype(F32)
            if out is mine:
                out[i] = value
            else:
                out[i * many : (i + 1) * many, :] = value
    sums[0] = row[...] + r2[block:, :].astype(F32)
    sums[1] = r1[block:, :].astype(F32) + r3[block:, :].astype(F32)
    for i in range(2):
        send[2 * many + i * ROWS : 2 * many + (i + 1) * ROWS, :] = sums[i]


def weight_out_kernel(ids, mine, sums, received, out, bias):
    many, part = mine.shape[1:]
    block = 2 * many
    for i in range(2):
        cols = pl.ds(pl.multiple_of((ids[7] ^ (2 * i)) * part, part), part)
        out[:, cols] = mine[i]
        cols = pl.ds(pl.multiple_of((ids[7] ^ (2 * i + 1)) * part, part), part)
        out[:, cols] = received[i * many : (i + 1) * many, :]
    quarters = (
        sums[0], received[block : block + ROWS, :], sums[1], received[block + ROWS :, :],
    )
    total = sum(q * (ids[3] ^ ids[7] == i).astype(F32) for i, q in enumerate(quarters))
    step = 2 * many
    picked = sum(
        total[:1, i * step : (i + 1) * step] * ((ids[5] * 2 + ids[2]) == i).astype(F32) for i in range(4)
    )
    bias[...] = jnp.where(ids[1] == 0, picked[:, :many], picked[:, many:])


def chip_body(features, weight, bias, node_mask, neighbour_tiles, tile_weights, out_grad):
    rows, cols = lax.axis_size("row"), lax.axis_size("col")
    devices = rows * cols
    r, c = lax.axis_index("row"), lax.axis_index("col")
    core, z = c & 1, r >> 1
    place = (r & 1) * 2 + core
    ids = jnp.stack([r & 3, core, c >> 1, z, r >> 2, r & 1, z & 1, place, r]).astype(jnp.int32)
    nodes, width = features.shape[1:]
    half, quarter = width // 2, width // GROUP
    lists, tiles = neighbour_tiles[0, 0], tile_weights[0, 0]
    dests, slots, tile = tiles.shape[0], tiles.shape[1], tiles.shape[2]
    masks = (X, Z, X | Z)
    shares = (CORE, X, X | CORE)

    own_rows = weight.shape[0]
    at = (r & 1) * (quarter // 2) + c * own_rows
    row = lax.dynamic_update_slice(jnp.zeros((ROWS, quarter), BF16), bias[None], (0, at))
    pieces = call(split_kernel, [shape((own_rows + ROWS, quarter), BF16)] * 4, ids, weight, row)
    pieces = [pieces[0]] + [swap(p, m) for p, m in zip(pieces[1:], shares)]
    (block,) = call(block_kernel, [shape((4 * own_rows + ROWS, quarter), BF16)], ids, *pieces)

    lists = jnp.pad(lists.reshape(1, -1), ((0, 15), (0, tile - dests * slots))).astype(BF16)
    tiles, lists = lax.optimization_barrier((tiles, lists, pieces[1]))[:2]
    tiles = jnp.concatenate([tiles.reshape(-1, tile), lists], axis=0)
    tiles_of = [tiles, swap(after(tiles, *pieces[2:]), X), swap(tiles, Z)]
    tiles_of.append(swap(tiles_of[2], X))
    lists_of = jnp.stack([t[-16, : dests * slots] for t in tiles_of]).astype(jnp.int32)

    columns = call(
        columns_kernel, [shape((2, nodes, quarter), BF16)] * 4, ids, features, after(swap(features[0], 2 * Z), tiles_of[1])
    )
    source = [columns[0]] + [swap(value, m) for value, m in zip(columns[1:], masks)]
    lanes = jnp.broadcast_to(node_mask[0][:, None].astype(BF16), (nodes, 128))
    grads = call(split_masked_kernel, [shape((nodes, quarter), BF16)] * 4, ids, lanes, out_grad[0])
    grads = [grads[0]] + [swap(g, m) for g, m in zip(grads[1:], shares)]

    y0, z1 = swap(block, Y), swap(block, Z)
    z2 = swap(after(block, y0, z1), 2 * Z)
    z3 = swap(after(z2, *grads[2:]), Z)
    y1, y2, y3 = [swap(value, Y) for value in (z1, z2, z3)]
    weights = [block, y0, z1, y1, z2, y2, z3, y3]

    source[0] = after(source[0], y0, z1)
    piece = (GROUP, dests // 2, tile, quarter)
    kept, sent = call(
        gather_kernel, [shape(piece, F32), shape(piece, BF16)],
        ids, lists_of, *tiles_of, *source,
        scratch=[pltpu.VMEM((rows, tile, quarter), BF16)],
        smem=2, flops=2 * GROUP * dests * slots * tile * tile * quarter,
    )
    mine, send = call(
        pair_sum_kernel, [shape((GROUP, tile, quarter), F32), shape((GROUP, tile, quarter), BF16)],
        ids, kept, swap(after(sent, y1), CORE),
    )
    received = after(swap(send, Y), y1, z2, grads[1])
    near, far = call(group_kernel, [shape((2 * tile + 2 * ROWS, quarter), BF16)] * 2, ids, mine, received)
    (aggregate,) = call(
        aggregate_kernel, [shape((2 * nodes, width), BF16)],
        ids, after(near, y2, y3), swap(near, X), swap(far, Z), swap(far, X | Z),
    )
    aggregate_other = swap(aggregate, CORE)

    *acts, pre_grad, back_own, back_other = call(
        dense_kernel,
        [shape((nodes, quarter), BF16)] * 4
        + [shape((4 * nodes, quarter), BF16)]
        + [shape((2 * nodes, width), F32), shape((2 * nodes, width), BF16)],
        ids, aggregate, aggregate_other, *grads, *weights,
        scratch=[pltpu.VMEM((4 * nodes, width), BF16)] + [pltpu.VMEM((4 * nodes, quarter), BF16)] * 2,
        flops=16 * nodes * quarter * width, vmem=56,
    )

    far, send_far, row = call(
        functools.partial(weight_grad_kernel, True),
        [shape((4, tile, quarter), F32), shape((4 * tile + ROWS, quarter), BF16), shape((ROWS, quarter), F32)],
        ids, aggregate, aggregate_other, pre_grad,
        scratch=[pltpu.VMEM((half, quarter), F32)], flops=4 * nodes * quarter * width, vmem=56,
    )
    v0, *others = call(
        back_kernel, [shape((2, nodes, quarter), F32)] + [shape((2, nodes, quarter), BF16)] * 3,
        ids, back_own, after(swap(back_other, CORE), send_far),
    )
    vx, vz, vxz = [swap(v, m) for v, m in zip(others, masks)]
    from_y = swap(send_far, Y)
    near, send_near = call(
        functools.partial(weight_grad_kernel, False),
        [shape((4, tile, quarter), F32), shape((4 * tile, quarter), BF16)],
        ids, aggregate, aggregate_other, after(pre_grad, v0),
        scratch=[pltpu.VMEM((half, quarter), F32)], flops=4 * nodes * quarter * width, vmem=56,
    )
    vx, from_y, near = lax.optimization_barrier((vx, from_y, near))
    grads_own = call(add_kernel, [shape((4, nodes, quarter), BF16)], v0, vx, vz, vxz, smem=0)[0]
    grads_away = swap(grads_own, Y)
    send, row = call(
        fold_y_kernel, [shape((4 * tile + ROWS, quarter), BF16), shape((ROWS, quarter), F32)],
        far, row, from_y, smem=0,
    )
    from_z = swap(send, Z)
    grads_away = after(grads_away, from_z)
    from_y = swap(after(send_near, grads_own), Y)
    acts = [acts[0]] + [swap(after(a, grads_own), m) for a, m in zip(acts[1:], shares)]
    (spread,) = call(
        spread_kernel, [shape((rows, tile, quarter), BF16)],
        ids, lists_of, *tiles_of,
        grads_own, swap(grads_own, CORE), grads_away, swap(grads_away, CORE),
        scratch=[pltpu.VMEM((rows, tile, quarter), F32)],
        smem=2, flops=2 * GROUP * dests * slots * tile * tile * quarter,
    )

    pass
    spread_all = lax.all_to_all(spread, "row", 0, 0, tiled=True)
    own, row, *send = call(
        fold_low_kernel,
        [shape((tile, quarter), F32), shape((ROWS, quarter), F32)] + [shape((tile + ROWS, quarter), BF16)] * 3,
        ids, near, row, from_y, from_z,
    )
    received = [swap(s, m) for s, m in zip(send, (X, 2 * Z, 2 * Z | X))]
    (input_grad,) = call(finish_kernel, [shape((nodes, width), BF16)], spread_all, smem=0)
    (activations,) = call(act_kernel, [shape((nodes, width), BF16)], ids, lanes, *acts)
    own = after(own, input_grad, activations)
    own, rows_of, send = call(
        fold_high_kernel,
        [shape((2, own_rows, quarter), F32), shape((2, ROWS, quarter), F32), shape((2 * own_rows + 2 * ROWS, quarter), F32)],
        ids, own, row, *received,
    )
    weight_grad, row = call(
        weight_out_kernel, [shape((own_rows, width), F32), shape((1, own_rows), F32)],
        ids, own, rows_of, swap(send, CORE),
    )
    bias_grad = row.reshape(own_rows)

    return activations[None], input_grad[None], weight_grad, bias_grad


def fetch_weights(weight, bias):
    return (
        lax.all_gather(weight, ("row", "col"), axis=0, tiled=True),
        lax.all_gather(bias, ("row", "col"), axis=0, tiled=True),
    )


def body(features, weight, bias, node_mask, neighbour_tiles, tile_weights, out_grad):
    tile = tile_weights.shape[-1]
    dest_count = neighbour_tiles.shape[2]
    slot_count = neighbour_tiles.shape[3]
    lists = neighbour_tiles[0, 0]
    valid = lists >= 0
    blocks = jnp.where(valid[:, :, None, None], tile_weights[0, 0], jnp.zeros((), jnp.bfloat16))
    group = 4
    turns = dest_count // group
    full_weight, full_bias = fetch_weights(weight, bias)
    source = lax.all_gather(features, "row", axis=1, tiled=True)[0]
    width = source.shape[-1]
    source_count = source.shape[0] // tile
    source_index = jnp.arange(source_count, dtype=jnp.int32)
    selector = ((lists[:, :, None] == source_index[None, None, :]) & valid[:, :, None]).astype(
        jnp.bfloat16
    )
    grouped_selector = selector.reshape(turns, group, slot_count, source_count)
    grouped_blocks = blocks.reshape(turns, group, slot_count, tile, tile)

    def dense_strip(group_selector, group_blocks):
        strip = jnp.einsum(
            "gsj,gsik->gijk", group_selector, group_blocks, preferred_element_type=jnp.float32
        )
        return strip.astype(jnp.bfloat16).reshape(group * tile, source_count * tile)

    def aggregate_group(pieces):
        group_selector, group_blocks = pieces
        strip = dense_strip(group_selector, group_blocks)
        return jnp.dot(strip, source, preferred_element_type=jnp.float32)

    partial_value = lax.map(aggregate_group, (grouped_selector, grouped_blocks)).reshape(-1, width)
    summed = lax.psum_scatter(partial_value, "col", scatter_dimension=0, tiled=True)
    aggregate = summed.astype(jnp.bfloat16)
    pre = jnp.dot(aggregate, full_weight, preferred_element_type=jnp.float32) + full_bias.astype(
        jnp.float32
    )
    keep = node_mask[0].astype(jnp.float32)[:, None]
    sigmoid_pre = jax.nn.sigmoid(pre)
    activations = (keep * (pre * sigmoid_pre)).astype(jnp.bfloat16)[None]
    slope = sigmoid_pre * (1.0 + pre * (1.0 - sigmoid_pre))
    pre_grad = (out_grad[0].astype(jnp.float32) * keep * slope).astype(jnp.bfloat16)
    weight_term = lax.dot_general(
        aggregate, pre_grad, (((0,), (0,)), ((), ())), preferred_element_type=jnp.float32
    )
    bias_term = jnp.sum(pre_grad.astype(jnp.float32), axis=0)
    weight_grad, bias_grad = (
        lax.psum_scatter(weight_term, ("row", "col"), scatter_dimension=0, tiled=True),
        lax.psum_scatter(bias_term, ("row", "col"), scatter_dimension=0, tiled=True),
    )
    aggregate_grad = lax.dot_general(
        pre_grad, full_weight, (((1,), (1,)), ((), ())), preferred_element_type=jnp.float32
    ).astype(jnp.bfloat16)
    dest_rows = lax.all_gather(aggregate_grad, "col", axis=0, tiled=True)
    grouped_grads = dest_rows.reshape(turns, group * tile, width)

    def spread_group(totals, pieces):
        group_selector, group_blocks, group_grads = pieces
        strip = dense_strip(group_selector, group_blocks)
        terms = lax.dot_general(
            strip, group_grads, (((0,), (0,)), ((), ())), preferred_element_type=jnp.float32
        )
        return (totals + terms, None)

    initial = jnp.zeros((source_count * tile, width), jnp.float32)
    source_terms, unused = lax.scan(
        spread_group, initial, (grouped_selector, grouped_blocks, grouped_grads)
    )
    input_grad = lax.psum_scatter(source_terms, "row", scatter_dimension=0, tiled=True)
    input_grad = input_grad.astype(jnp.bfloat16)[None]
    return (activations, input_grad, weight_grad, bias_grad)


def solution(mesh):
    chips = mesh.shape["row"] == 8 and mesh.shape["col"] == 4
    return jax.shard_map(
        chip_body if chips else body,
        mesh=mesh,
        in_specs=(
            P("col", "row", None),
            P(("row", "col"), None),
            P(("row", "col")),
            P("row", "col"),
            P("row", "col", None, None),
            P("row", "col", None, None, None, None),
            P("row", "col", None),
        ),
        out_specs=(
            P("row", "col", None),
            P("col", "row", None),
            P(("row", "col"), None),
            P(("row", "col")),
        ),
        check_vma=False,
    )
```

```python
import functools

import jax
import jax.numpy as jnp
from jax import lax
from jax.experimental import pallas as pl
from jax.experimental.pallas import tpu as pltpu
from jax.sharding import PartitionSpec as P

BOTH = ("row", "col")
F32 = jnp.float32
BF16 = jnp.bfloat16
VMEM = pl.BlockSpec(memory_space=pltpu.VMEM)
SMEM = pl.BlockSpec(memory_space=pltpu.SMEM)
CORE, Y, X, Z = 1, 2, 4, 8
GROUP = 4
SLOTS = 3
ROWS = 16


def swap(value, mask, total=32):
    return lax.ppermute(value, BOTH, [(i, i ^ mask) for i in range(total)])


def after(value, *others):
    return lax.optimization_barrier((value,) + others)[0]


def shape(dims, dtype):
    return jax.ShapeDtypeStruct(dims, dtype)


def call(kernel, outs, *operands, scratch=(), smem=1, flops=0, vmem=24):
    moved = sum(o.size * o.dtype.itemsize for o in operands)
    moved += sum(o.size * o.dtype.itemsize for o in outs)
    return pl.pallas_call(
        kernel,
        out_shape=outs,
        in_specs=[SMEM] * smem + [VMEM] * (len(operands) - smem),
        out_specs=[VMEM] * len(outs),
        scratch_shapes=list(scratch),
        compiler_params=pltpu.CompilerParams(vmem_limit_bytes=vmem * 2**20),
        cost_estimate=pl.CostEstimate(flops=flops, bytes_accessed=moved, transcendentals=0),
    )(*operands)


def split_kernel(ids, value, bias, *pieces):
    part = pieces[0].shape[-1]
    many = bias.shape[1]
    own, none = bias[...].astype(F32), jnp.zeros(bias.shape, F32)
    row = jnp.where(
        ids[1] == 0, jnp.concatenate([own, none], axis=1), jnp.concatenate([none, own], axis=1)
    )
    at = pl.ds(pl.multiple_of((ids[5] * 2 + ids[2]) * (2 * many), 2 * many), 2 * many)
    for i, piece in enumerate(pieces):
        piece[:-ROWS] = value[:, pl.ds(pl.multiple_of((ids[7] ^ i) * part, part), part)]
        piece[-ROWS:] = jnp.zeros((ROWS, part), BF16)
        piece[-ROWS:, at] = jnp.broadcast_to(row, (ROWS, 2 * many)).astype(BF16)


def split_masked_kernel(ids, mask, value, *pieces):
    part, lanes = pieces[0].shape[-1], mask.shape[-1]
    for i, piece in enumerate(pieces):
        start = pl.multiple_of((ids[7] ^ i) * part, part)
        for j in range(part // lanes):
            cols = pl.ds(start + j * lanes, lanes)
            piece[:, j * lanes : (j + 1) * lanes] = value[:, cols] * mask[...]


def block_kernel(ids, p0, p1, p2, p3, block):
    rows = p0.shape[0] - ROWS
    for i, piece in enumerate((p0, p1, p2, p3)):
        at = (i >> 1) * 2 + (ids[1] ^ (i & 1))
        block[pl.ds(pl.multiple_of(at * rows, rows), rows), :] = piece[:rows]
    block[4 * rows :] = p0[rows:] + p1[rows:] + p2[rows:] + p3[rows:]


def columns_kernel(ids, own, far, *pieces):
    member = ids[0]
    part, half = pieces[0].shape[-1] // 2, far.shape[-1] // 2
    for i, piece in enumerate(pieces):
        for j in range(2):
            cols = pl.ds(pl.multiple_of(j * half + (member ^ i) * part, part), part)
            piece[0, :, j * part : (j + 1) * part] = own[0, :, cols]
            piece[1, :, j * part : (j + 1) * part] = far[:, cols]


def gather_kernel(ids, lists, a0, a1, a2, a3, h0, h1, h2, h3, keep, send, source):
    member, core, row = ids[0], ids[1], ids[8]
    tile, dests = keep.shape[2], 2 * keep.shape[1]
    for i, piece in enumerate((h0, h1, h2, h3)):
        source[row ^ i] = piece[0]
        source[row ^ i ^ GROUP] = piece[1]
    for i, tiles in enumerate((a0, a1, a2, a3)):
        for pair in range(dests // 2):
            for other in range(2):
                m = pair * 2 + (core if other == 0 else 1 - core)
                left, right = [], []
                for s in range(SLOTS):
                    slot = m * SLOTS + s
                    listed = lists[i, slot]
                    block = tiles[pl.ds(pl.multiple_of(slot * tile, tile), tile), :]
                    left.append(jnp.where(listed >= 0, block, jnp.zeros_like(block)))
                    right.append(source[jnp.maximum(listed, 0)])
                total = jnp.dot(
                    jnp.concatenate(left, axis=1),
                    jnp.concatenate(right, axis=0),
                    preferred_element_type=F32,
                )
                if other == 0:
                    keep[member ^ i, pair] = total
                else:
                    send[member ^ i, pair] = total.astype(BF16)


def pair_sum_kernel(ids, kept, received, mine, send):
    y = ids[2]
    for g in range(GROUP):
        mine[g] = kept[g, y] + received[g, y].astype(F32)
        send[g] = (kept[g, 1 - y] + received[g, 1 - y].astype(F32)).astype(BF16)


def group_kernel(ids, mine, received, near, far):
    low = ids[6]
    for out, z in ((near, low), (far, 1 - low)):
        for x in range(2):
            nodes = mine.shape[1]
            total = mine[2 * z + x] + received[2 * z + x].astype(F32)
            out[x * nodes : (x + 1) * nodes, :] = total.astype(BF16)
        out[2 * nodes :, :] = jnp.zeros((out.shape[0] - 2 * nodes, out.shape[1]), BF16)


def dense_kernel(ids, p0, p1, p2, p3, q0, q1, q2, q3, o0, o1, o2, o3, *rest):
    weights = rest[:8]
    a0, a1, a2, a3, pre_grad, b0, b1, b2, b3, back_other, left, grads, acts = rest[8:]
    back_own = (b0, b1, b2, b3)
    y, high, z, x = ids[2], ids[4], ids[3], ids[5]
    part = pre_grad.shape[1]
    pair, block = b0.shape[0], part // 4
    nodes = pair // 2

    def lanes(i):
        return pl.ds(pl.multiple_of(((high ^ (i >> 2)) * 2 + (y ^ (i & 1))) * block, block), block)

    def quarter(i, j):
        return (i & 2) + j

    def place(i):
        return pl.ds(pl.multiple_of((i & 1) * pair + (x ^ (i >> 1)) * nodes, nodes), nodes)

    for i in range(8):
        for j in range(2):
            cols = slice((2 * i + j) * block, (2 * i + j + 1) * block)
            left[:pair, cols] = (p0, p1, p2, p3)[quarter(i, j)][:pair, lanes(i)]
            left[pair:, cols] = (q0, q1, q2, q3)[quarter(i, j)][:pair, lanes(i)]
    for i, piece in enumerate((o0, o1, o2, o3)):
        grads[place(i), :] = piece[...]
    many = 2 * block
    bias = sum(
        w[many:, :].astype(F32) * (z ^ (i >> 1) == ids[7]).astype(F32) for i, w in enumerate(weights)
    )[:1]
    step = 256
    for n in range(part // step):
        cols = slice(n * step, (n + 1) * step)
        matrix = jnp.concatenate([w[:many, cols] for w in weights], axis=0)
        pre = jnp.dot(left[...], matrix, preferred_element_type=F32) + bias[:, cols]
        sigmoid = 1.0 / (1.0 + jnp.exp(-pre))
        acts[:, cols] = (pre * sigmoid).astype(BF16)
        slope = sigmoid * (1.0 + pre * (1.0 - sigmoid))
        pre_grad[:, cols] = (grads[:, cols].astype(F32) * slope).astype(BF16)
    for i, piece in enumerate((a0, a1, a2, a3)):
        piece[...] = acts[place(i), :]
    for i, weight in enumerate(weights):
        back = lax.dot_general(
            pre_grad[...], weight[:many, :], (((1,), (1,)), ((), ())), preferred_element_type=F32
        )
        for j in range(2):
            cols = slice(j * block, (j + 1) * block)
            back_own[quarter(i, j)][:, lanes(i)] = back[:pair, cols]
            back_other[quarter(i, j), :, lanes(i)] = back[pair:, cols].astype(BF16)


def back_kernel(b1, b2, b3, received, v1, v2, v3):
    nodes = v1.shape[1]
    for i, (own, out) in enumerate(((b1, v1), (b2, v2), (b3, v3))):
        for x in range(2):
            rows = slice(x * nodes, (x + 1) * nodes)
            out[x] = (own[rows, :] + received[i + 1, rows, :].astype(F32)).astype(BF16)


def add_kernel(own, received, vx, vz, vxz, out):
    nodes = vx.shape[1]
    for x in range(2):
        rows = slice(x * nodes, (x + 1) * nodes)
        out[x] = (own[rows, :] + received[0, rows, :].astype(F32) + vx[x].astype(F32)).astype(BF16)
        out[2 + x] = (vz[x].astype(F32) + vxz[x].astype(F32)).astype(BF16)


def spread_kernel(ids, lists, a0, a1, a2, a3, *rest):
    grads, (out, total) = rest[:4], rest[4:]
    core, y, x = ids[1], ids[2], ids[5]
    tile = out.shape[1]
    total[...] = jnp.zeros_like(total)
    for i, tiles in enumerate((a0, a1, a2, a3)):
        for away in range(4):
            m = (y ^ (away >> 1)) * 2 + (core ^ (away & 1))
            left = []
            for s in range(SLOTS):
                slot = m * SLOTS + s
                block = tiles[pl.ds(pl.multiple_of(slot * tile, tile), tile), :]
                left.append(jnp.where(lists[i, slot] >= 0, block, jnp.zeros_like(block)))
            terms = lax.dot_general(
                jnp.concatenate(left, axis=1), grads[away][2 * (i >> 1) + (x ^ (i & 1))],
                (((0,), (0,)), ((), ())), preferred_element_type=F32,
            )
            for s in range(SLOTS):
                at = jnp.maximum(lists[i, m * SLOTS + s], 0)
                total[at] += terms[s * tile : (s + 1) * tile]
    out[...] = total[...].astype(BF16)


def finish_kernel(terms, out):
    part, half = terms.shape[-1] // 2, out.shape[-1] // 2
    for g in range(GROUP):
        total = sum(terms[i].astype(F32) for i in range(g, terms.shape[0], GROUP)).astype(BF16)
        out[:, g * part : (g + 1) * part] = total[:, :part]
        out[:, half + g * part : half + (g + 1) * part] = total[:, part:]


def act_kernel(ids, mask, a0, a1, a2, a3, out):
    part, lanes = a0.shape[-1], mask.shape[-1]
    for i, piece in enumerate((a0, a1, a2, a3)):
        start = pl.multiple_of((ids[7] ^ i) * part, part)
        for j in range(part // lanes):
            out[:, pl.ds(start + j * lanes, lanes)] = piece[:, j * lanes : (j + 1) * lanes] * mask[...]


def weight_grad_kernel(far, ids, own0, own1, other0, other1, grads, keep, send, *rest):
    y, x = ids[2], ids[5]
    block = keep.shape[1]
    row, total = rest if far else (None,) + rest
    pair = grads.shape[0] // 2
    for j, (own, other) in enumerate(((own0, other0), (own1, other1))):
        total[4 * j * block : 4 * (j + 1) * block, :] = lax.dot_general(
            jnp.concatenate([own[:pair, :], other[:pair, :]], axis=0), grads[...],
            (((0,), (0,)), ((), ())), preferred_element_type=F32,
        )
    for i in range(4):
        at = ((i & 1) ^ x) * 4 + (i >> 1) * 2
        keep[i] = total[pl.ds(pl.multiple_of((at + y) * block, block), block), :]
        value = total[pl.ds(pl.multiple_of((at + 1 - y) * block, block), block), :]
        send[i * block : (i + 1) * block, :] = value.astype(BF16)
    if far:
        sums = jnp.sum(grads[...].astype(F32), axis=0, keepdims=True)
        row[...] = jnp.broadcast_to(sums, row.shape)
        send[4 * block :, :] = row[...].astype(BF16)


def fold_y_kernel(keep, row, received, send, both):
    block = keep.shape[1]
    for i in range(4):
        rows = slice(i * block, (i + 1) * block)
        send[rows, :] = (keep[i] + received[rows, :].astype(F32)).astype(BF16)
    both[...] = row[...] + received[4 * block :, :].astype(F32)
    send[4 * block :, :] = both[...].astype(BF16)


def fold_low_kernel(ids, keep, row, from_y, from_z, own, sums, s1, s2, s3):
    high, x, block = ids[4], ids[5], keep.shape[1]
    sums[...] = row[...] + from_z[4 * block :, :].astype(F32)
    for i, out in enumerate((own, s1, s2, s3)):
        at = (high ^ (i >> 1)) * 2 + (x ^ (i & 1))
        rows = pl.ds(pl.multiple_of(at * block, block), block)
        total = keep[at] + from_y[rows, :].astype(F32) + from_z[rows, :].astype(F32)
        if out is own:
            own[...] = total
        else:
            out[:block, :] = total.astype(BF16)
            out[block:, :] = sums[...].astype(BF16)


def fold_high_kernel(ids, own, row, r1, r2, r3, mine, sums, send):
    core, block = ids[1], own.shape[0]
    many = mine.shape[1]
    for i in range(2):
        for out, k in ((mine, core), (send, 1 - core)):
            at = pl.ds(pl.multiple_of(k * many, many), many)
            if i == 0:
                value = own[at, :] + r2[at, :].astype(F32)
            else:
                value = r1[at, :].astype(F32) + r3[at, :].astype(F32)
            if out is mine:
                out[i] = value
            else:
                out[i * many : (i + 1) * many, :] = value
    sums[0] = row[...] + r2[block:, :].astype(F32)
    sums[1] = r1[block:, :].astype(F32) + r3[block:, :].astype(F32)
    for i in range(2):
        send[2 * many + i * ROWS : 2 * many + (i + 1) * ROWS, :] = sums[i]


def weight_out_kernel(ids, mine, sums, received, out, bias):
    many, part = mine.shape[1:]
    block = 2 * many
    for i in range(2):
        cols = pl.ds(pl.multiple_of((ids[7] ^ (2 * i)) * part, part), part)
        out[:, cols] = mine[i]
        cols = pl.ds(pl.multiple_of((ids[7] ^ (2 * i + 1)) * part, part), part)
        out[:, cols] = received[i * many : (i + 1) * many, :]
    quarters = (
        sums[0], received[block : block + ROWS, :], sums[1], received[block + ROWS :, :],
    )
    total = sum(q * (ids[3] ^ ids[7] == i).astype(F32) for i, q in enumerate(quarters))
    step = 2 * many
    picked = sum(
        total[:1, i * step : (i + 1) * step] * ((ids[5] * 2 + ids[2]) == i).astype(F32) for i in range(4)
    )
    bias[...] = jnp.where(ids[1] == 0, picked[:, :many], picked[:, many:])


def chip_body(features, weight, bias, node_mask, neighbour_tiles, tile_weights, out_grad):
    rows, cols = lax.axis_size("row"), lax.axis_size("col")
    devices = rows * cols
    r, c = lax.axis_index("row"), lax.axis_index("col")
    core, z = c & 1, r >> 1
    place = (r & 1) * 2 + core
    ids = jnp.stack([r & 3, core, c >> 1, z, r >> 2, r & 1, z & 1, place, r]).astype(jnp.int32)
    nodes, width = features.shape[1:]
    half, quarter = width // 2, width // GROUP
    lists, tiles = neighbour_tiles[0, 0], tile_weights[0, 0]
    dests, slots, tile = tiles.shape[0], tiles.shape[1], tiles.shape[2]
    masks = (X, Z, X | Z)
    shares = (CORE, X, X | CORE)

    own_rows = weight.shape[0]
    pieces = call(split_kernel, [shape((own_rows + ROWS, quarter), BF16)] * 4, ids, weight, bias[None])
    pieces = [pieces[0]] + [swap(p, m) for p, m in zip(pieces[1:], shares)]
    (block,) = call(block_kernel, [shape((4 * own_rows + ROWS, quarter), BF16)], ids, *pieces)

    lists = jnp.pad(lists.reshape(1, -1), ((0, 15), (0, tile - dests * slots))).astype(BF16)
    tiles, lists = lax.optimization_barrier((tiles, lists, pieces[1]))[:2]
    tiles = jnp.concatenate([tiles.reshape(-1, tile), lists], axis=0)
    tiles_of = [tiles, swap(after(tiles, *pieces[2:]), X), swap(tiles, Z)]
    tiles_of.append(swap(tiles_of[2], X))
    lists_of = jnp.stack([t[-16, : dests * slots] for t in tiles_of]).astype(jnp.int32)

    columns = call(
        columns_kernel, [shape((2, nodes, quarter), BF16)] * 4, ids, features, after(swap(features[0], 2 * Z), tiles_of[1])
    )
    source = [columns[0]] + [swap(value, m) for value, m in zip(columns[1:], masks)]
    lanes = jnp.broadcast_to(node_mask[0][:, None].astype(BF16), (nodes, 128))
    grads = call(split_masked_kernel, [shape((nodes, quarter), BF16)] * 4, ids, lanes, out_grad[0])
    grads = [grads[0]] + [swap(g, m) for g, m in zip(grads[1:], shares)]

    y0, z1 = swap(block, Y), swap(block, Z)
    z2 = swap(after(block, y0, z1), 2 * Z)
    z3 = swap(after(z2, *grads[2:]), Z)
    y1, y2, y3 = [swap(value, Y) for value in (z1, z2, z3)]
    weights = [block, y0, z1, y1, z2, y2, z3, y3]

    source[0] = after(source[0], y0, z1)
    piece = (GROUP, dests // 2, tile, quarter)
    kept, sent = call(
        gather_kernel, [shape(piece, F32), shape(piece, BF16)],
        ids, lists_of, *tiles_of, *source,
        scratch=[pltpu.VMEM((rows, tile, quarter), BF16)],
        smem=2, flops=2 * GROUP * dests * slots * tile * tile * quarter,
    )
    mine, send = call(
        pair_sum_kernel, [shape((GROUP, tile, quarter), F32), shape((GROUP, tile, quarter), BF16)],
        ids, kept, swap(after(sent, y1), CORE),
    )
    received = after(swap(send, Y), y1, z2, grads[1])
    near, far = call(group_kernel, [shape((2 * tile + 2 * ROWS, quarter), BF16)] * 2, ids, mine, received)
    near = [near, swap(near, X), swap(far, Z), swap(far, X | Z)]
    near[2] = after(near[2], y2, y3)
    other = [swap(value, CORE) for value in near]

    *acts, pre_grad, b0, b1, b2, b3, back_other = call(
        dense_kernel,
        [shape((nodes, quarter), BF16)] * 4
        + [shape((4 * nodes, quarter), BF16)]
        + [shape((2 * nodes, quarter), F32)] * 4 + [shape((4, 2 * nodes, quarter), BF16)],
        ids, *near, *other, *grads, *weights,
        scratch=[pltpu.VMEM((4 * nodes, width), BF16)] + [pltpu.VMEM((4 * nodes, quarter), BF16)] * 2,
        flops=16 * nodes * quarter * width, vmem=40,
    )

    far, send_far, row = call(
        functools.partial(weight_grad_kernel, True),
        [shape((4, tile, quarter), F32), shape((4 * tile + ROWS, quarter), BF16), shape((ROWS, quarter), F32)],
        ids, *near[2:], *other[2:], pre_grad,
        scratch=[pltpu.VMEM((half, quarter), F32)], flops=4 * nodes * quarter * width, vmem=28,
    )
    received = after(swap(back_other, CORE), send_far)
    others = call(
        back_kernel, [shape((2, nodes, quarter), BF16)] * 3, b1, b2, b3, received, smem=0
    )
    vx, vz, vxz = [swap(v, m) for v, m in zip(others, masks)]
    from_y = swap(send_far, Y)
    kept_near, send_near = call(
        functools.partial(weight_grad_kernel, False),
        [shape((4, tile, quarter), F32), shape((4 * tile, quarter), BF16)],
        ids, *near[:2], *other[:2], after(pre_grad, others[0]),
        scratch=[pltpu.VMEM((half, quarter), F32)], flops=4 * nodes * quarter * width, vmem=28,
    )
    vx, from_y, kept_near = lax.optimization_barrier((vx, from_y, kept_near))
    grads_own = call(add_kernel, [shape((4, nodes, quarter), BF16)], b0, received, vx, vz, vxz, smem=0)[0]
    grads_away = swap(grads_own, Y)
    send, row = call(
        fold_y_kernel, [shape((4 * tile + ROWS, quarter), BF16), shape((ROWS, quarter), F32)],
        far, row, from_y, smem=0,
    )
    from_z = swap(send, Z)
    grads_away = after(grads_away, from_z)
    from_y = swap(after(send_near, grads_own), Y)
    acts = [acts[0]] + [swap(after(a, grads_own), m) for a, m in zip(acts[1:], shares)]
    (spread,) = call(
        spread_kernel, [shape((rows, tile, quarter), BF16)],
        ids, lists_of, *tiles_of,
        grads_own, swap(grads_own, CORE), grads_away, swap(grads_away, CORE),
        scratch=[pltpu.VMEM((rows, tile, quarter), F32)],
        smem=2, flops=2 * GROUP * dests * slots * tile * tile * quarter,
    )

    pass
    spread_all = lax.all_to_all(spread, "row", 0, 0, tiled=True)
    own, row, *send = call(
        fold_low_kernel,
        [shape((tile, quarter), F32), shape((ROWS, quarter), F32)] + [shape((tile + ROWS, quarter), BF16)] * 3,
        ids, kept_near, row, from_y, from_z,
    )
    received = [swap(s, m) for s, m in zip(send, (X, 2 * Z, 2 * Z | X))]
    (input_grad,) = call(finish_kernel, [shape((nodes, width), BF16)], spread_all, smem=0)
    (activations,) = call(act_kernel, [shape((nodes, width), BF16)], ids, lanes, *acts)
    own = after(own, input_grad, activations)
    own, rows_of, send = call(
        fold_high_kernel,
        [shape((2, own_rows, quarter), F32), shape((2, ROWS, quarter), F32), shape((2 * own_rows + 2 * ROWS, quarter), F32)],
        ids, own, row, *received,
    )
    weight_grad, row = call(
        weight_out_kernel, [shape((own_rows, width), F32), shape((1, own_rows), F32)],
        ids, own, rows_of, swap(send, CORE),
    )
    bias_grad = row.reshape(own_rows)

    return activations[None], input_grad[None], weight_grad, bias_grad


def fetch_weights(weight, bias):
    return (
        lax.all_gather(weight, ("row", "col"), axis=0, tiled=True),
        lax.all_gather(bias, ("row", "col"), axis=0, tiled=True),
    )


def body(features, weight, bias, node_mask, neighbour_tiles, tile_weights, out_grad):
    tile = tile_weights.shape[-1]
    dest_count = neighbour_tiles.shape[2]
    slot_count = neighbour_tiles.shape[3]
    lists = neighbour_tiles[0, 0]
    valid = lists >= 0
    blocks = jnp.where(valid[:, :, None, None], tile_weights[0, 0], jnp.zeros((), jnp.bfloat16))
    group = 4
    turns = dest_count // group
    full_weight, full_bias = fetch_weights(weight, bias)
    source = lax.all_gather(features, "row", axis=1, tiled=True)[0]
    width = source.shape[-1]
    source_count = source.shape[0] // tile
    source_index = jnp.arange(source_count, dtype=jnp.int32)
    selector = ((lists[:, :, None] == source_index[None, None, :]) & valid[:, :, None]).astype(
        jnp.bfloat16
    )
    grouped_selector = selector.reshape(turns, group, slot_count, source_count)
    grouped_blocks = blocks.reshape(turns, group, slot_count, tile, tile)

    def dense_strip(group_selector, group_blocks):
        strip = jnp.einsum(
            "gsj,gsik->gijk", group_selector, group_blocks, preferred_element_type=jnp.float32
        )
        return strip.astype(jnp.bfloat16).reshape(group * tile, source_count * tile)

    def aggregate_group(pieces):
        group_selector, group_blocks = pieces
        strip = dense_strip(group_selector, group_blocks)
        return jnp.dot(strip, source, preferred_element_type=jnp.float32)

    partial_value = lax.map(aggregate_group, (grouped_selector, grouped_blocks)).reshape(-1, width)
    summed = lax.psum_scatter(partial_value, "col", scatter_dimension=0, tiled=True)
    aggregate = summed.astype(jnp.bfloat16)
    pre = jnp.dot(aggregate, full_weight, preferred_element_type=jnp.float32) + full_bias.astype(
        jnp.float32
    )
    keep = node_mask[0].astype(jnp.float32)[:, None]
    sigmoid_pre = jax.nn.sigmoid(pre)
    activations = (keep * (pre * sigmoid_pre)).astype(jnp.bfloat16)[None]
    slope = sigmoid_pre * (1.0 + pre * (1.0 - sigmoid_pre))
    pre_grad = (out_grad[0].astype(jnp.float32) * keep * slope).astype(jnp.bfloat16)
    weight_term = lax.dot_general(
        aggregate, pre_grad, (((0,), (0,)), ((), ())), preferred_element_type=jnp.float32
    )
    bias_term = jnp.sum(pre_grad.astype(jnp.float32), axis=0)
    weight_grad, bias_grad = (
        lax.psum_scatter(weight_term, ("row", "col"), scatter_dimension=0, tiled=True),
        lax.psum_scatter(bias_term, ("row", "col"), scatter_dimension=0, tiled=True),
    )
    aggregate_grad = lax.dot_general(
        pre_grad, full_weight, (((1,), (1,)), ((), ())), preferred_element_type=jnp.float32
    ).astype(jnp.bfloat16)
    dest_rows = lax.all_gather(aggregate_grad, "col", axis=0, tiled=True)
    grouped_grads = dest_rows.reshape(turns, group * tile, width)

    def spread_group(totals, pieces):
        group_selector, group_blocks, group_grads = pieces
        strip = dense_strip(group_selector, group_blocks)
        terms = lax.dot_general(
            strip, group_grads, (((0,), (0,)), ((), ())), preferred_element_type=jnp.float32
        )
        return (totals + terms, None)

    initial = jnp.zeros((source_count * tile, width), jnp.float32)
    source_terms, unused = lax.scan(
        spread_group, initial, (grouped_selector, grouped_blocks, grouped_grads)
    )
    input_grad = lax.psum_scatter(source_terms, "row", scatter_dimension=0, tiled=True)
    input_grad = input_grad.astype(jnp.bfloat16)[None]
    return (activations, input_grad, weight_grad, bias_grad)


def solution(mesh):
    chips = mesh.shape["row"] == 8 and mesh.shape["col"] == 4
    return jax.shard_map(
        chip_body if chips else body,
        mesh=mesh,
        in_specs=(
            P("col", "row", None),
            P(("row", "col"), None),
            P(("row", "col")),
            P("row", "col"),
            P("row", "col", None, None),
            P("row", "col", None, None, None, None),
            P("row", "col", None),
        ),
        out_specs=(
            P("row", "col", None),
            P("col", "row", None),
            P(("row", "col"), None),
            P(("row", "col")),
        ),
        check_vma=False,
    )
```

```python
import functools

import jax
import jax.numpy as jnp
from jax import lax
from jax.experimental import pallas as pl
from jax.experimental.pallas import tpu as pltpu
from jax.sharding import PartitionSpec as P

BOTH = ("row", "col")
F32 = jnp.float32
BF16 = jnp.bfloat16
VMEM = pl.BlockSpec(memory_space=pltpu.VMEM)
SMEM = pl.BlockSpec(memory_space=pltpu.SMEM)
CORE, Y, X, Z = 1, 2, 4, 8
GROUP = 4
SLOTS = 3
ROWS = 16


def swap(value, mask, total=32):
    return lax.ppermute(value, BOTH, [(i, i ^ mask) for i in range(total)])


def after(value, *others):
    return lax.optimization_barrier((value,) + others)[0]


def shape(dims, dtype):
    return jax.ShapeDtypeStruct(dims, dtype)


def call(kernel, outs, *operands, scratch=(), smem=1, flops=0, vmem=24):
    moved = sum(o.size * o.dtype.itemsize for o in operands)
    moved += sum(o.size * o.dtype.itemsize for o in outs)
    return pl.pallas_call(
        kernel,
        out_shape=outs,
        in_specs=[SMEM] * smem + [VMEM] * (len(operands) - smem),
        out_specs=[VMEM] * len(outs),
        scratch_shapes=list(scratch),
        compiler_params=pltpu.CompilerParams(vmem_limit_bytes=vmem * 2**20),
        cost_estimate=pl.CostEstimate(flops=flops, bytes_accessed=moved, transcendentals=0),
    )(*operands)


def split_kernel(ids, value, bias, *pieces):
    part = pieces[0].shape[-1]
    many = bias.shape[1]
    own, none = bias[...].astype(F32), jnp.zeros(bias.shape, F32)
    row = jnp.where(
        ids[1] == 0, jnp.concatenate([own, none], axis=1), jnp.concatenate([none, own], axis=1)
    )
    at = pl.ds(pl.multiple_of((ids[5] * 2 + ids[2]) * (2 * many), 2 * many), 2 * many)
    for i, piece in enumerate(pieces):
        piece[:-ROWS] = value[:, pl.ds(pl.multiple_of((ids[7] ^ i) * part, part), part)]
        piece[-ROWS:] = jnp.zeros((ROWS, part), BF16)
        piece[-ROWS:, at] = jnp.broadcast_to(row, (ROWS, 2 * many)).astype(BF16)


def split_masked_kernel(ids, mask, value, *pieces):
    part, lanes = pieces[0].shape[-1], mask.shape[-1]
    for i, piece in enumerate(pieces):
        start = pl.multiple_of((ids[7] ^ i) * part, part)
        for j in range(part // lanes):
            cols = pl.ds(start + j * lanes, lanes)
            piece[:, j * lanes : (j + 1) * lanes] = value[:, cols] * mask[...]


def block_kernel(ids, p0, p1, p2, p3, block):
    rows = p0.shape[0] - ROWS
    for i, piece in enumerate((p0, p1, p2, p3)):
        at = (i >> 1) * 2 + (ids[1] ^ (i & 1))
        block[pl.ds(pl.multiple_of(at * rows, rows), rows), :] = piece[:rows]
    block[4 * rows :] = p0[rows:] + p1[rows:] + p2[rows:] + p3[rows:]


def columns_kernel(ids, own, far, *pieces):
    member = ids[0]
    part, half = pieces[0].shape[-1] // 2, far.shape[-1] // 2
    for i, piece in enumerate(pieces):
        for j in range(2):
            cols = pl.ds(pl.multiple_of(j * half + (member ^ i) * part, part), part)
            piece[0, :, j * part : (j + 1) * part] = own[0, :, cols]
            piece[1, :, j * part : (j + 1) * part] = far[:, cols]


def gather_kernel(ids, lists, a0, a1, a2, a3, h0, h1, h2, h3, keep, send, source):
    member, core, row = ids[0], ids[1], ids[8]
    tile, dests = keep.shape[2], 2 * keep.shape[1]
    for i, piece in enumerate((h0, h1, h2, h3)):
        source[row ^ i] = piece[0]
        source[row ^ i ^ GROUP] = piece[1]
    for i, tiles in enumerate((a0, a1, a2, a3)):
        for pair in range(dests // 2):
            for other in range(2):
                m = pair * 2 + (core if other == 0 else 1 - core)
                left, right = [], []
                for s in range(SLOTS):
                    slot = m * SLOTS + s
                    listed = lists[i, slot]
                    block = tiles[pl.ds(pl.multiple_of(slot * tile, tile), tile), :]
                    left.append(jnp.where(listed >= 0, block, jnp.zeros_like(block)))
                    right.append(source[jnp.maximum(listed, 0)])
                total = jnp.dot(
                    jnp.concatenate(left, axis=1),
                    jnp.concatenate(right, axis=0),
                    preferred_element_type=F32,
                )
                if other == 0:
                    keep[member ^ i, pair] = total
                else:
                    send[member ^ i, pair] = total.astype(BF16)


def pair_sum_kernel(ids, kept, received, mine, send):
    y = ids[2]
    for g in range(GROUP):
        mine[g] = kept[g, y] + received[g, y].astype(F32)
        send[g] = (kept[g, 1 - y] + received[g, 1 - y].astype(F32)).astype(BF16)


def group_kernel(ids, mine, received, near, far):
    low = ids[6]
    for out, z in ((near, low), (far, 1 - low)):
        for x in range(2):
            nodes = mine.shape[1]
            total = mine[2 * z + x] + received[2 * z + x].astype(F32)
            out[x * nodes : (x + 1) * nodes, :] = total.astype(BF16)
        out[2 * nodes :, :] = jnp.zeros((out.shape[0] - 2 * nodes, out.shape[1]), BF16)


def dense_kernel(ids, p0, p1, p2, p3, q0, q1, q2, q3, o0, o1, o2, o3, *rest):
    weights = rest[:8]
    a0, a1, a2, a3, pre_grad, b0, b1, b2, b3, back_other, left, grads, acts = rest[8:]
    back_own = (b0, b1, b2, b3)
    y, high, z, x = ids[2], ids[4], ids[3], ids[5]
    part = pre_grad.shape[1]
    pair, block = b0.shape[0], part // 4
    nodes = pair // 2

    def lanes(i):
        return pl.ds(pl.multiple_of(((high ^ (i >> 2)) * 2 + (y ^ (i & 1))) * block, block), block)

    def quarter(i, j):
        return (i & 2) + j

    def place(i):
        return pl.ds(pl.multiple_of((i & 1) * pair + (x ^ (i >> 1)) * nodes, nodes), nodes)

    for i in range(8):
        for j in range(2):
            cols = slice((2 * i + j) * block, (2 * i + j + 1) * block)
            left[:pair, cols] = (p0, p1, p2, p3)[quarter(i, j)][:pair, lanes(i)]
            left[pair:, cols] = (q0, q1, q2, q3)[quarter(i, j)][:pair, lanes(i)]
    for i, piece in enumerate((o0, o1, o2, o3)):
        grads[place(i), :] = piece[...]
    many = 2 * block
    bias = sum(
        w[many:, :].astype(F32) * (z ^ (i >> 1) == ids[7]).astype(F32) for i, w in enumerate(weights)
    )[:1]
    step = 256
    for n in range(part // step):
        cols = slice(n * step, (n + 1) * step)
        matrix = jnp.concatenate([w[:many, cols] for w in weights], axis=0)
        pre = jnp.dot(left[...], matrix, preferred_element_type=F32) + bias[:, cols]
        sigmoid = 1.0 / (1.0 + jnp.exp(-pre))
        acts[:, cols] = (pre * sigmoid).astype(BF16)
        slope = sigmoid * (1.0 + pre * (1.0 - sigmoid))
        pre_grad[:, cols] = (grads[:, cols].astype(F32) * slope).astype(BF16)
    for i, piece in enumerate((a0, a1, a2, a3)):
        piece[...] = acts[place(i), :]
    for i, weight in enumerate(weights):
        back = lax.dot_general(
            pre_grad[...], weight[:many, :], (((1,), (1,)), ((), ())), preferred_element_type=F32
        )
        for j in range(2):
            cols = slice(j * block, (j + 1) * block)
            back_own[quarter(i, j)][:, lanes(i)] = back[:pair, cols]
            back_other[quarter(i, j), :, lanes(i)] = back[pair:, cols].astype(BF16)


def back_kernel(b1, b2, b3, received, v1, v2, v3):
    nodes = v1.shape[1]
    for i, (own, out) in enumerate(((b1, v1), (b2, v2), (b3, v3))):
        for x in range(2):
            rows = slice(x * nodes, (x + 1) * nodes)
            out[x] = (own[rows, :] + received[i + 1, rows, :].astype(F32)).astype(BF16)


def add_kernel(own, received, vx, vz, vxz, out):
    nodes = vx.shape[1]
    for x in range(2):
        rows = slice(x * nodes, (x + 1) * nodes)
        out[x] = (own[rows, :] + received[0, rows, :].astype(F32) + vx[x].astype(F32)).astype(BF16)
        out[2 + x] = (vz[x].astype(F32) + vxz[x].astype(F32)).astype(BF16)


def spread_kernel(near, ids, lists, a0, a1, a2, a3, same, cross, *rest):
    start, out, total = (None,) + rest if near else rest
    core, y, x = ids[1], ids[2], ids[5]
    tile = out.shape[1]
    total[...] = jnp.zeros_like(total) if near else start[...]
    for i, tiles in enumerate((a0, a1, a2, a3)):
        for other, grads in enumerate((same, cross)):
            m = (y if near else 1 - y) * 2 + (core ^ other)
            left = []
            for s in range(SLOTS):
                slot = m * SLOTS + s
                block = tiles[pl.ds(pl.multiple_of(slot * tile, tile), tile), :]
                left.append(jnp.where(lists[i, slot] >= 0, block, jnp.zeros_like(block)))
            terms = lax.dot_general(
                jnp.concatenate(left, axis=1), grads[2 * (i >> 1) + (x ^ (i & 1))],
                (((0,), (0,)), ((), ())), preferred_element_type=F32,
            )
            for s in range(SLOTS):
                at = jnp.maximum(lists[i, m * SLOTS + s], 0)
                total[at] += terms[s * tile : (s + 1) * tile]
    out[...] = total[...].astype(out.dtype)


def finish_kernel(terms, out):
    part, half = terms.shape[-1] // 2, out.shape[-1] // 2
    for g in range(GROUP):
        total = sum(terms[i].astype(F32) for i in range(g, terms.shape[0], GROUP)).astype(BF16)
        out[:, g * part : (g + 1) * part] = total[:, :part]
        out[:, half + g * part : half + (g + 1) * part] = total[:, part:]


def act_kernel(ids, mask, a0, a1, a2, a3, out):
    part, lanes = a0.shape[-1], mask.shape[-1]
    for i, piece in enumerate((a0, a1, a2, a3)):
        start = pl.multiple_of((ids[7] ^ i) * part, part)
        for j in range(part // lanes):
            out[:, pl.ds(start + j * lanes, lanes)] = piece[:, j * lanes : (j + 1) * lanes] * mask[...]


def weight_grad_kernel(far, ids, own0, own1, other0, other1, grads, keep, send, *rest):
    y, x = ids[2], ids[5]
    block = keep.shape[1]
    row, total = rest if far else (None,) + rest
    pair = grads.shape[0] // 2
    for j, (own, other) in enumerate(((own0, other0), (own1, other1))):
        total[4 * j * block : 4 * (j + 1) * block, :] = lax.dot_general(
            jnp.concatenate([own[:pair, :], other[:pair, :]], axis=0), grads[...],
            (((0,), (0,)), ((), ())), preferred_element_type=F32,
        )
    for i in range(4):
        at = ((i & 1) ^ x) * 4 + (i >> 1) * 2
        keep[i] = total[pl.ds(pl.multiple_of((at + y) * block, block), block), :]
        value = total[pl.ds(pl.multiple_of((at + 1 - y) * block, block), block), :]
        send[i * block : (i + 1) * block, :] = value.astype(BF16)
    if far:
        sums = jnp.sum(grads[...].astype(F32), axis=0, keepdims=True)
        row[...] = jnp.broadcast_to(sums, row.shape)
        send[4 * block :, :] = row[...].astype(BF16)


def fold_y_kernel(keep, row, received, send, both):
    block = keep.shape[1]
    for i in range(4):
        rows = slice(i * block, (i + 1) * block)
        send[rows, :] = (keep[i] + received[rows, :].astype(F32)).astype(BF16)
    both[...] = row[...] + received[4 * block :, :].astype(F32)
    send[4 * block :, :] = both[...].astype(BF16)


def fold_low_kernel(ids, keep, row, from_y, from_z, own, s1, s2, s3):
    high, x, block = ids[4], ids[5], keep.shape[1]
    sums = row[...] + from_z[4 * block :, :].astype(F32)
    for i, out in enumerate((own, s1, s2, s3)):
        at = (high ^ (i >> 1)) * 2 + (x ^ (i & 1))
        rows = pl.ds(pl.multiple_of(at * block, block), block)
        total = keep[at] + from_y[rows, :].astype(F32) + from_z[rows, :].astype(F32)
        out[:block, :] = total.astype(out.dtype)
        out[block:, :] = sums.astype(out.dtype)


def weight_out_kernel(ids, own, r1, r2, r3, own_c, r1_c, r2_c, r3_c, out, bias):
    many, part = out.shape[0], own.shape[1]
    block = 2 * many
    rows = pl.ds(pl.multiple_of(ids[1] * many, many), many)
    pairs = ((own, r2), (own_c, r2_c), (r1, r3), (r1_c, r3_c))
    total = 0.0
    for i, (left, right) in enumerate(pairs):
        cols = pl.ds(pl.multiple_of((ids[7] ^ i) * part, part), part)
        out[:, cols] = left[rows, :].astype(F32) + right[rows, :].astype(F32)
        quarter = left[block:, :].astype(F32) + right[block:, :].astype(F32)
        total += quarter * (ids[3] ^ ids[7] == i).astype(F32)
    step = 2 * many
    picked = sum(
        total[:1, i * step : (i + 1) * step] * ((ids[5] * 2 + ids[2]) == i).astype(F32) for i in range(4)
    )
    bias[...] = jnp.where(ids[1] == 0, picked[:, :many], picked[:, many:])


def chip_body(features, weight, bias, node_mask, neighbour_tiles, tile_weights, out_grad):
    rows, cols = lax.axis_size("row"), lax.axis_size("col")
    devices = rows * cols
    r, c = lax.axis_index("row"), lax.axis_index("col")
    core, z = c & 1, r >> 1
    place = (r & 1) * 2 + core
    ids = jnp.stack([r & 3, core, c >> 1, z, r >> 2, r & 1, z & 1, place, r]).astype(jnp.int32)
    nodes, width = features.shape[1:]
    half, quarter = width // 2, width // GROUP
    lists, tiles = neighbour_tiles[0, 0], tile_weights[0, 0]
    dests, slots, tile = tiles.shape[0], tiles.shape[1], tiles.shape[2]
    masks = (X, Z, X | Z)
    shares = (CORE, X, X | CORE)

    own_rows = weight.shape[0]
    pieces = call(split_kernel, [shape((own_rows + ROWS, quarter), BF16)] * 4, ids, weight, bias[None])
    pieces = [pieces[0]] + [swap(p, m) for p, m in zip(pieces[1:], shares)]
    (block,) = call(block_kernel, [shape((4 * own_rows + ROWS, quarter), BF16)], ids, *pieces)

    lists = jnp.pad(lists.reshape(1, -1), ((0, 15), (0, tile - dests * slots))).astype(BF16)
    tiles, lists = lax.optimization_barrier((tiles, lists, pieces[1]))[:2]
    tiles = jnp.concatenate([tiles.reshape(-1, tile), lists], axis=0)
    tiles_of = [tiles, swap(after(tiles, *pieces[2:]), X), swap(tiles, Z)]
    tiles_of.append(swap(tiles_of[2], X))
    lists_of = jnp.stack([t[-16, : dests * slots] for t in tiles_of]).astype(jnp.int32)

    columns = call(
        columns_kernel, [shape((2, nodes, quarter), BF16)] * 4, ids, features, after(swap(features[0], 2 * Z), tiles_of[1])
    )
    source = [columns[0]] + [swap(value, m) for value, m in zip(columns[1:], masks)]
    lanes = jnp.broadcast_to(node_mask[0][:, None].astype(BF16), (nodes, 128))
    grads = call(split_masked_kernel, [shape((nodes, quarter), BF16)] * 4, ids, lanes, out_grad[0])
    grads = [grads[0]] + [swap(g, m) for g, m in zip(grads[1:], shares)]

    y0, z1 = swap(block, Y), swap(block, Z)
    z2 = swap(after(block, y0, z1), 2 * Z)
    z3 = swap(after(z2, *grads[2:]), Z)
    y1, y2, y3 = [swap(value, Y) for value in (z1, z2, z3)]
    weights = [block, y0, z1, y1, z2, y2, z3, y3]

    source[0] = after(source[0], y0, z1)
    piece = (GROUP, dests // 2, tile, quarter)
    kept, sent = call(
        gather_kernel, [shape(piece, F32), shape(piece, BF16)],
        ids, lists_of, *tiles_of, *source,
        scratch=[pltpu.VMEM((rows, tile, quarter), BF16)],
        smem=2, flops=2 * GROUP * dests * slots * tile * tile * quarter,
    )
    mine, send = call(
        pair_sum_kernel, [shape((GROUP, tile, quarter), F32), shape((GROUP, tile, quarter), BF16)],
        ids, kept, swap(after(sent, y1), CORE),
    )
    received = after(swap(send, Y), y1, z2, grads[1])
    near, far = call(group_kernel, [shape((2 * tile + 2 * ROWS, quarter), BF16)] * 2, ids, mine, received)
    near = [near, swap(near, X), swap(far, Z), swap(far, X | Z)]
    near[2] = after(near[2], y2, y3)
    other = [swap(value, CORE) for value in near]

    *acts, pre_grad, b0, b1, b2, b3, back_other = call(
        dense_kernel,
        [shape((nodes, quarter), BF16)] * 4
        + [shape((4 * nodes, quarter), BF16)]
        + [shape((2 * nodes, quarter), F32)] * 4 + [shape((4, 2 * nodes, quarter), BF16)],
        ids, *near, *other, *grads, *weights,
        scratch=[pltpu.VMEM((4 * nodes, width), BF16)] + [pltpu.VMEM((4 * nodes, quarter), BF16)] * 2,
        flops=16 * nodes * quarter * width, vmem=40,
    )

    far, send_far, row = call(
        functools.partial(weight_grad_kernel, True),
        [shape((4, tile, quarter), F32), shape((4 * tile + ROWS, quarter), BF16), shape((ROWS, quarter), F32)],
        ids, *near[2:], *other[2:], pre_grad,
        scratch=[pltpu.VMEM((half, quarter), F32)], flops=4 * nodes * quarter * width, vmem=28,
    )
    received = after(swap(back_other, CORE), send_far)
    others = call(
        back_kernel, [shape((2, nodes, quarter), BF16)] * 3, b1, b2, b3, received, smem=0
    )
    vx, vz, vxz = [swap(v, m) for v, m in zip(others, masks)]
    from_y = swap(send_far, Y)
    kept_near, send_near = call(
        functools.partial(weight_grad_kernel, False),
        [shape((4, tile, quarter), F32), shape((4 * tile, quarter), BF16)],
        ids, *near[:2], *other[:2], after(pre_grad, others[0]),
        scratch=[pltpu.VMEM((half, quarter), F32)], flops=4 * nodes * quarter * width, vmem=28,
    )
    vx, from_y, kept_near = lax.optimization_barrier((vx, from_y, kept_near))
    grads_own = call(add_kernel, [shape((4, nodes, quarter), BF16)], b0, received, vx, vz, vxz, smem=0)[0]
    grads_away = swap(grads_own, Y)
    send, row = call(
        fold_y_kernel, [shape((4 * tile + ROWS, quarter), BF16), shape((ROWS, quarter), F32)],
        far, row, from_y, smem=0,
    )
    from_z = swap(send, Z)
    grads_away = after(grads_away, from_z)
    from_y = swap(after(send_near, grads_own), Y)
    acts = [acts[0]] + [swap(after(a, grads_own), m) for a, m in zip(acts[1:], shares)]
    (spread,) = call(
        functools.partial(spread_kernel, True), [shape((rows, tile, quarter), F32)],
        ids, lists_of, *tiles_of, grads_own, swap(grads_own, CORE),
        scratch=[pltpu.VMEM((rows, tile, quarter), F32)],
        smem=2, flops=GROUP * dests * slots * tile * tile * quarter,
    )
    (spread,) = call(
        functools.partial(spread_kernel, False), [shape((rows, tile, quarter), BF16)],
        ids, lists_of, *tiles_of, grads_away, swap(grads_away, CORE), spread,
        scratch=[pltpu.VMEM((rows, tile, quarter), F32)],
        smem=2, flops=GROUP * dests * slots * tile * tile * quarter,
    )
    spread_all = lax.all_to_all(spread, "row", 0, 0, tiled=True)
    from_y = after(from_y, *acts[1:])
    own, *send = call(
        fold_low_kernel,
        [shape((tile + ROWS, quarter), F32)] + [shape((tile + ROWS, quarter), BF16)] * 3,
        ids, kept_near, row, from_y, from_z,
    )
    own_other = swap(own, CORE)
    send[0] = after(send[0], own_other)
    received = [swap(s, m) for s, m in zip(send, (X, 2 * Z, 2 * Z | X))]
    (input_grad,) = call(finish_kernel, [shape((nodes, width), BF16)], spread_all, smem=0)
    (activations,) = call(act_kernel, [shape((nodes, width), BF16)], ids, lanes, *acts)
    received_other = [
        swap(received[0], CORE),
        swap(after(received[1], input_grad, activations), CORE),
        swap(received[2], CORE),
    ]
    weight_grad, row = call(
        weight_out_kernel, [shape((own_rows, width), F32), shape((1, own_rows), F32)],
        ids, own, *received, own_other, *received_other,
    )
    bias_grad = row.reshape(own_rows)

    return activations[None], input_grad[None], weight_grad, bias_grad


def fetch_weights(weight, bias):
    return (
        lax.all_gather(weight, ("row", "col"), axis=0, tiled=True),
        lax.all_gather(bias, ("row", "col"), axis=0, tiled=True),
    )


def body(features, weight, bias, node_mask, neighbour_tiles, tile_weights, out_grad):
    tile = tile_weights.shape[-1]
    dest_count = neighbour_tiles.shape[2]
    slot_count = neighbour_tiles.shape[3]
    lists = neighbour_tiles[0, 0]
    valid = lists >= 0
    blocks = jnp.where(valid[:, :, None, None], tile_weights[0, 0], jnp.zeros((), jnp.bfloat16))
    group = 4
    turns = dest_count // group
    full_weight, full_bias = fetch_weights(weight, bias)
    source = lax.all_gather(features, "row", axis=1, tiled=True)[0]
    width = source.shape[-1]
    source_count = source.shape[0] // tile
    source_index = jnp.arange(source_count, dtype=jnp.int32)
    selector = ((lists[:, :, None] == source_index[None, None, :]) & valid[:, :, None]).astype(
        jnp.bfloat16
    )
    grouped_selector = selector.reshape(turns, group, slot_count, source_count)
    grouped_blocks = blocks.reshape(turns, group, slot_count, tile, tile)

    def dense_strip(group_selector, group_blocks):
        strip = jnp.einsum(
            "gsj,gsik->gijk", group_selector, group_blocks, preferred_element_type=jnp.float32
        )
        return strip.astype(jnp.bfloat16).reshape(group * tile, source_count * tile)

    def aggregate_group(pieces):
        group_selector, group_blocks = pieces
        strip = dense_strip(group_selector, group_blocks)
        return jnp.dot(strip, source, preferred_element_type=jnp.float32)

    partial_value = lax.map(aggregate_group, (grouped_selector, grouped_blocks)).reshape(-1, width)
    summed = lax.psum_scatter(partial_value, "col", scatter_dimension=0, tiled=True)
    aggregate = summed.astype(jnp.bfloat16)
    pre = jnp.dot(aggregate, full_weight, preferred_element_type=jnp.float32) + full_bias.astype(
        jnp.float32
    )
    keep = node_mask[0].astype(jnp.float32)[:, None]
    sigmoid_pre = jax.nn.sigmoid(pre)
    activations = (keep * (pre * sigmoid_pre)).astype(jnp.bfloat16)[None]
    slope = sigmoid_pre * (1.0 + pre * (1.0 - sigmoid_pre))
    pre_grad = (out_grad[0].astype(jnp.float32) * keep * slope).astype(jnp.bfloat16)
    weight_term = lax.dot_general(
        aggregate, pre_grad, (((0,), (0,)), ((), ())), preferred_element_type=jnp.float32
    )
    bias_term = jnp.sum(pre_grad.astype(jnp.float32), axis=0)
    weight_grad, bias_grad = (
        lax.psum_scatter(weight_term, ("row", "col"), scatter_dimension=0, tiled=True),
        lax.psum_scatter(bias_term, ("row", "col"), scatter_dimension=0, tiled=True),
    )
    aggregate_grad = lax.dot_general(
        pre_grad, full_weight, (((1,), (1,)), ((), ())), preferred_element_type=jnp.float32
    ).astype(jnp.bfloat16)
    dest_rows = lax.all_gather(aggregate_grad, "col", axis=0, tiled=True)
    grouped_grads = dest_rows.reshape(turns, group * tile, width)

    def spread_group(totals, pieces):
        group_selector, group_blocks, group_grads = pieces
        strip = dense_strip(group_selector, group_blocks)
        terms = lax.dot_general(
            strip, group_grads, (((0,), (0,)), ((), ())), preferred_element_type=jnp.float32
        )
        return (totals + terms, None)

    initial = jnp.zeros((source_count * tile, width), jnp.float32)
    source_terms, unused = lax.scan(
        spread_group, initial, (grouped_selector, grouped_blocks, grouped_grads)
    )
    input_grad = lax.psum_scatter(source_terms, "row", scatter_dimension=0, tiled=True)
    input_grad = input_grad.astype(jnp.bfloat16)[None]
    return (activations, input_grad, weight_grad, bias_grad)


def solution(mesh):
    chips = mesh.shape["row"] == 8 and mesh.shape["col"] == 4
    return jax.shard_map(
        chip_body if chips else body,
        mesh=mesh,
        in_specs=(
            P("col", "row", None),
            P(("row", "col"), None),
            P(("row", "col")),
            P("row", "col"),
            P("row", "col", None, None),
            P("row", "col", None, None, None, None),
            P("row", "col", None),
        ),
        out_specs=(
            P("row", "col", None),
            P("col", "row", None),
            P(("row", "col"), None),
            P(("row", "col")),
        ),
        check_vma=False,
    )
```

```python
import functools

import jax
import jax.numpy as jnp
from jax import lax
from jax.experimental import pallas as pl
from jax.experimental.pallas import tpu as pltpu
from jax.sharding import PartitionSpec as P

BOTH = ("row", "col")
F32 = jnp.float32
BF16 = jnp.bfloat16
VMEM = pl.BlockSpec(memory_space=pltpu.VMEM)
SMEM = pl.BlockSpec(memory_space=pltpu.SMEM)
CORE, Y, X, Z = 1, 2, 4, 8
GROUP = 4
SLOTS = 3
ROWS = 16


def swap(value, mask, total=32):
    return lax.ppermute(value, BOTH, [(i, i ^ mask) for i in range(total)])


def after(value, *others):
    return lax.optimization_barrier((value,) + others)[0]


def shape(dims, dtype):
    return jax.ShapeDtypeStruct(dims, dtype)


def call(kernel, outs, *operands, scratch=(), smem=1, flops=0, vmem=24):
    moved = sum(o.size * o.dtype.itemsize for o in operands)
    moved += sum(o.size * o.dtype.itemsize for o in outs)
    return pl.pallas_call(
        kernel,
        out_shape=outs,
        in_specs=[SMEM] * smem + [VMEM] * (len(operands) - smem),
        out_specs=[VMEM] * len(outs),
        scratch_shapes=list(scratch),
        compiler_params=pltpu.CompilerParams(vmem_limit_bytes=vmem * 2**20),
        cost_estimate=pl.CostEstimate(flops=flops, bytes_accessed=moved, transcendentals=0),
    )(*operands)


def split_kernel(ids, value, bias, *pieces):
    part = pieces[0].shape[-1]
    many = bias.shape[1]
    own, none = bias[...].astype(F32), jnp.zeros(bias.shape, F32)
    row = jnp.where(
        ids[1] == 0, jnp.concatenate([own, none], axis=1), jnp.concatenate([none, own], axis=1)
    )
    at = pl.ds(pl.multiple_of((ids[5] * 2 + ids[2]) * (2 * many), 2 * many), 2 * many)
    for i, piece in enumerate(pieces):
        piece[:-ROWS] = value[:, pl.ds(pl.multiple_of((ids[7] ^ i) * part, part), part)]
        piece[-ROWS:] = jnp.zeros((ROWS, part), BF16)
        piece[-ROWS:, at] = jnp.broadcast_to(row, (ROWS, 2 * many)).astype(BF16)


def split_masked_kernel(ids, mask, value, *pieces):
    part, lanes = pieces[0].shape[-1], mask.shape[-1]
    for i, piece in enumerate(pieces):
        start = pl.multiple_of((ids[7] ^ i) * part, part)
        for j in range(part // lanes):
            cols = pl.ds(start + j * lanes, lanes)
            piece[:, j * lanes : (j + 1) * lanes] = value[:, cols] * mask[...]


def block_kernel(ids, p0, p1, p2, p3, block):
    rows = p0.shape[0] - ROWS
    for i, piece in enumerate((p0, p1, p2, p3)):
        at = (i >> 1) * 2 + (ids[1] ^ (i & 1))
        block[pl.ds(pl.multiple_of(at * rows, rows), rows), :] = piece[:rows]
    block[4 * rows :] = p0[rows:] + p1[rows:] + p2[rows:] + p3[rows:]


def columns_kernel(ids, own, far, *pieces):
    member = ids[0]
    part, half = pieces[0].shape[-1] // 2, far.shape[-1] // 2
    for i, piece in enumerate(pieces):
        for j in range(2):
            cols = pl.ds(pl.multiple_of(j * half + (member ^ i) * part, part), part)
            piece[0, :, j * part : (j + 1) * part] = own[0, :, cols]
            piece[1, :, j * part : (j + 1) * part] = far[:, cols]


def gather_kernel(ids, lists, a0, a1, a2, a3, h0, h1, h2, h3, keep, send, source):
    member, core, row = ids[0], ids[1], ids[8]
    tile, dests = keep.shape[2], 2 * keep.shape[1]
    for i, piece in enumerate((h0, h1, h2, h3)):
        source[row ^ i] = piece[0]
        source[row ^ i ^ GROUP] = piece[1]
    for i, tiles in enumerate((a0, a1, a2, a3)):
        for pair in range(dests // 2):
            for other in range(2):
                m = pair * 2 + (core if other == 0 else 1 - core)
                left, right = [], []
                for s in range(SLOTS):
                    slot = m * SLOTS + s
                    listed = lists[i, slot]
                    block = tiles[pl.ds(pl.multiple_of(slot * tile, tile), tile), :]
                    left.append(jnp.where(listed >= 0, block, jnp.zeros_like(block)))
                    right.append(source[jnp.maximum(listed, 0)])
                total = jnp.dot(
                    jnp.concatenate(left, axis=1),
                    jnp.concatenate(right, axis=0),
                    preferred_element_type=F32,
                )
                if other == 0:
                    keep[member ^ i, pair] = total
                else:
                    send[member ^ i, pair] = total.astype(send.dtype)


def pair_sum_kernel(ids, kept, received, mine, send):
    y = ids[2]
    for g in range(GROUP):
        mine[g] = kept[g, y] + received[g, y].astype(F32)
        send[g] = (kept[g, 1 - y] + received[g, 1 - y].astype(F32)).astype(BF16)


def group_kernel(ids, mine, received, near, far):
    low = ids[6]
    for out, z in ((near, low), (far, 1 - low)):
        for x in range(2):
            nodes = mine.shape[1]
            total = mine[2 * z + x] + received[2 * z + x].astype(F32)
            out[x * nodes : (x + 1) * nodes, :] = total.astype(BF16)
        out[2 * nodes :, :] = jnp.zeros((out.shape[0] - 2 * nodes, out.shape[1]), BF16)


def dense_kernel(ids, p0, p1, p2, p3, q0, q1, q2, q3, o0, o1, o2, o3, *rest):
    weights = rest[:8]
    a0, a1, a2, a3, pre_grad, b0, b1, b2, b3, back_other, left, grads, acts = rest[8:]
    back_own = (b0, b1, b2, b3)
    y, high, z, x = ids[2], ids[4], ids[3], ids[5]
    part = pre_grad.shape[1]
    pair, block = b0.shape[0], part // 4
    nodes = pair // 2

    def lanes(i):
        return pl.ds(pl.multiple_of(((high ^ (i >> 2)) * 2 + (y ^ (i & 1))) * block, block), block)

    def quarter(i, j):
        return (i & 2) + j

    def place(i):
        return pl.ds(pl.multiple_of((i & 1) * pair + (x ^ (i >> 1)) * nodes, nodes), nodes)

    for i in range(8):
        for j in range(2):
            cols = slice((2 * i + j) * block, (2 * i + j + 1) * block)
            left[:pair, cols] = (p0, p1, p2, p3)[quarter(i, j)][:pair, lanes(i)]
            left[pair:, cols] = (q0, q1, q2, q3)[quarter(i, j)][:pair, lanes(i)]
    for i, piece in enumerate((o0, o1, o2, o3)):
        grads[place(i), :] = piece[...]
    many = 2 * block
    bias = sum(
        w[many:, :].astype(F32) * (z ^ (i >> 1) == ids[7]).astype(F32) for i, w in enumerate(weights)
    )[:1]
    step = 256
    for n in range(part // step):
        cols = slice(n * step, (n + 1) * step)
        matrix = jnp.concatenate([w[:many, cols] for w in weights], axis=0)
        pre = jnp.dot(left[...], matrix, preferred_element_type=F32) + bias[:, cols]
        sigmoid = 1.0 / (1.0 + jnp.exp(-pre))
        acts[:, cols] = (pre * sigmoid).astype(BF16)
        slope = sigmoid * (1.0 + pre * (1.0 - sigmoid))
        pre_grad[:, cols] = (grads[:, cols].astype(F32) * slope).astype(BF16)
    for i, piece in enumerate((a0, a1, a2, a3)):
        piece[...] = acts[place(i), :]
    for i, weight in enumerate(weights):
        back = lax.dot_general(
            pre_grad[...], weight[:many, :], (((1,), (1,)), ((), ())), preferred_element_type=F32
        )
        for j in range(2):
            cols = slice(j * block, (j + 1) * block)
            back_own[quarter(i, j)][:, lanes(i)] = back[:pair, cols]
            back_other[quarter(i, j), :, lanes(i)] = back[pair:, cols].astype(BF16)


def back_kernel(b1, b2, b3, received, v1, v2, v3):
    nodes = v1.shape[1]
    for i, (own, out) in enumerate(((b1, v1), (b2, v2), (b3, v3))):
        for x in range(2):
            rows = slice(x * nodes, (x + 1) * nodes)
            out[x] = (own[rows, :] + received[i + 1, rows, :].astype(F32)).astype(BF16)


def add_kernel(own, received, vx, vz, vxz, out):
    nodes = vx.shape[1]
    for x in range(2):
        rows = slice(x * nodes, (x + 1) * nodes)
        out[x] = (own[rows, :] + received[0, rows, :].astype(F32) + vx[x].astype(F32)).astype(BF16)
        out[2 + x] = (vz[x].astype(F32) + vxz[x].astype(F32)).astype(BF16)


def spread_kernel(near, ids, lists, a0, a1, a2, a3, same, cross, *rest):
    start, out, total = (None,) + rest if near else rest
    core, y, x = ids[1], ids[2], ids[5]
    tile = out.shape[1]
    total[...] = jnp.zeros_like(total) if near else start[...]
    for i, tiles in enumerate((a0, a1, a2, a3)):
        for other, grads in enumerate((same, cross)):
            m = (y if near else 1 - y) * 2 + (core ^ other)
            left = []
            for s in range(SLOTS):
                slot = m * SLOTS + s
                block = tiles[pl.ds(pl.multiple_of(slot * tile, tile), tile), :]
                left.append(jnp.where(lists[i, slot] >= 0, block, jnp.zeros_like(block)))
            terms = lax.dot_general(
                jnp.concatenate(left, axis=1), grads[2 * (i >> 1) + (x ^ (i & 1))],
                (((0,), (0,)), ((), ())), preferred_element_type=F32,
            )
            for s in range(SLOTS):
                at = jnp.maximum(lists[i, m * SLOTS + s], 0)
                total[at] += terms[s * tile : (s + 1) * tile]
    out[...] = total[...].astype(out.dtype)


def finish_kernel(terms, out):
    part, half = terms.shape[-1] // 2, out.shape[-1] // 2
    for g in range(GROUP):
        total = sum(terms[i].astype(F32) for i in range(g, terms.shape[0], GROUP)).astype(BF16)
        out[:, g * part : (g + 1) * part] = total[:, :part]
        out[:, half + g * part : half + (g + 1) * part] = total[:, part:]


def act_kernel(ids, mask, a0, a1, a2, a3, out):
    part, lanes = a0.shape[-1], mask.shape[-1]
    for i, piece in enumerate((a0, a1, a2, a3)):
        start = pl.multiple_of((ids[7] ^ i) * part, part)
        for j in range(part // lanes):
            out[:, pl.ds(start + j * lanes, lanes)] = piece[:, j * lanes : (j + 1) * lanes] * mask[...]


def weight_grad_kernel(far, ids, own0, own1, other0, other1, grads, keep, send, *rest):
    y, x = ids[2], ids[5]
    block = keep.shape[1]
    row, total = rest if far else (None,) + rest
    pair = grads.shape[0] // 2
    for j, (own, other) in enumerate(((own0, other0), (own1, other1))):
        total[4 * j * block : 4 * (j + 1) * block, :] = lax.dot_general(
            jnp.concatenate([own[:pair, :], other[:pair, :]], axis=0), grads[...],
            (((0,), (0,)), ((), ())), preferred_element_type=F32,
        )
    for i in range(4):
        at = ((i & 1) ^ x) * 4 + (i >> 1) * 2
        keep[i] = total[pl.ds(pl.multiple_of((at + y) * block, block), block), :]
        value = total[pl.ds(pl.multiple_of((at + 1 - y) * block, block), block), :]
        send[i * block : (i + 1) * block, :] = value.astype(BF16)
    if far:
        sums = jnp.sum(grads[...].astype(F32), axis=0, keepdims=True)
        row[...] = jnp.broadcast_to(sums, row.shape)
        send[4 * block :, :] = row[...].astype(BF16)


def fold_y_kernel(keep, row, received, send, both):
    block = keep.shape[1]
    for i in range(4):
        rows = slice(i * block, (i + 1) * block)
        send[rows, :] = (keep[i] + received[rows, :].astype(F32)).astype(BF16)
    both[...] = row[...] + received[4 * block :, :].astype(F32)
    send[4 * block :, :] = both[...].astype(BF16)


def fold_low_kernel(ids, keep, row, from_y, from_z, own, s1, s2, s3):
    high, x, block = ids[4], ids[5], keep.shape[1]
    sums = row[...] + from_z[4 * block :, :].astype(F32)
    for i, out in enumerate((own, s1, s2, s3)):
        at = (high ^ (i >> 1)) * 2 + (x ^ (i & 1))
        rows = pl.ds(pl.multiple_of(at * block, block), block)
        total = keep[at] + from_y[rows, :].astype(F32) + from_z[rows, :].astype(F32)
        out[:block, :] = total.astype(out.dtype)
        out[block:, :] = sums.astype(out.dtype)


def weight_out_kernel(ids, own, r1, r2, r3, own_c, r1_c, r2_c, r3_c, out, bias):
    many, part = out.shape[0], own.shape[1]
    block = 2 * many
    rows = pl.ds(pl.multiple_of(ids[1] * many, many), many)
    pairs = ((own, r2), (own_c, r2_c), (r1, r3), (r1_c, r3_c))
    total = 0.0
    for i, (left, right) in enumerate(pairs):
        cols = pl.ds(pl.multiple_of((ids[7] ^ i) * part, part), part)
        out[:, cols] = left[rows, :].astype(F32) + right[rows, :].astype(F32)
        quarter = left[block:, :].astype(F32) + right[block:, :].astype(F32)
        total += quarter * (ids[3] ^ ids[7] == i).astype(F32)
    step = 2 * many
    picked = sum(
        total[:1, i * step : (i + 1) * step] * ((ids[5] * 2 + ids[2]) == i).astype(F32) for i in range(4)
    )
    bias[...] = jnp.where(ids[1] == 0, picked[:, :many], picked[:, many:])


def chip_body(features, weight, bias, node_mask, neighbour_tiles, tile_weights, out_grad):
    rows, cols = lax.axis_size("row"), lax.axis_size("col")
    devices = rows * cols
    r, c = lax.axis_index("row"), lax.axis_index("col")
    core, z = c & 1, r >> 1
    place = (r & 1) * 2 + core
    ids = jnp.stack([r & 3, core, c >> 1, z, r >> 2, r & 1, z & 1, place, r]).astype(jnp.int32)
    nodes, width = features.shape[1:]
    half, quarter = width // 2, width // GROUP
    lists, tiles = neighbour_tiles[0, 0], tile_weights[0, 0]
    dests, slots, tile = tiles.shape[0], tiles.shape[1], tiles.shape[2]
    masks = (X, Z, X | Z)
    shares = (CORE, X, X | CORE)

    own_rows = weight.shape[0]
    pieces = call(split_kernel, [shape((own_rows + ROWS, quarter), BF16)] * 4, ids, weight, bias[None])
    pieces = [pieces[0]] + [swap(p, m) for p, m in zip(pieces[1:], shares)]
    (block,) = call(block_kernel, [shape((4 * own_rows + ROWS, quarter), BF16)], ids, *pieces)

    lists = jnp.pad(lists.reshape(1, -1), ((0, 15), (0, tile - dests * slots))).astype(BF16)
    tiles, lists = lax.optimization_barrier((tiles, lists, pieces[1]))[:2]
    tiles = jnp.concatenate([tiles.reshape(-1, tile), lists], axis=0)
    tiles_of = [tiles, swap(after(tiles, *pieces[2:]), X), swap(tiles, Z)]
    tiles_of.append(swap(tiles_of[2], X))
    lists_of = jnp.stack([t[-16, : dests * slots] for t in tiles_of]).astype(jnp.int32)

    columns = call(
        columns_kernel, [shape((2, nodes, quarter), BF16)] * 4, ids, features, after(swap(features[0], 2 * Z), tiles_of[1])
    )
    source = [columns[0]] + [swap(value, m) for value, m in zip(columns[1:], masks)]
    lanes = jnp.broadcast_to(node_mask[0][:, None].astype(BF16), (nodes, 128))
    grads = call(split_masked_kernel, [shape((nodes, quarter), BF16)] * 4, ids, lanes, out_grad[0])
    grads = [grads[0]] + [swap(g, m) for g, m in zip(grads[1:], shares)]

    y0, z1 = swap(block, Y), swap(block, Z)
    z2 = swap(after(block, y0, z1), 2 * Z)
    z3 = swap(after(z2, *grads[2:]), Z)
    y1, y2, y3 = [swap(value, Y) for value in (z1, z2, z3)]
    weights = [block, y0, z1, y1, z2, y2, z3, y3]

    source[0] = after(source[0], y0, z1)
    piece = (GROUP, dests // 2, tile, quarter)
    kept, sent = call(
        gather_kernel, [shape(piece, F32)] * 2,
        ids, lists_of, *tiles_of, *source,
        scratch=[pltpu.VMEM((rows, tile, quarter), BF16)],
        smem=2, flops=2 * GROUP * dests * slots * tile * tile * quarter,
    )
    mine, send = call(
        pair_sum_kernel, [shape((GROUP, tile, quarter), F32), shape((GROUP, tile, quarter), BF16)],
        ids, kept, swap(after(sent, y1), CORE),
    )
    received = after(swap(send, Y), y1, z2, grads[1])
    near, far = call(group_kernel, [shape((2 * tile + 2 * ROWS, quarter), BF16)] * 2, ids, mine, received)
    near = [near, swap(near, X), swap(far, Z), swap(far, X | Z)]
    near[2] = after(near[2], y2, y3)
    other = [swap(value, CORE) for value in near]

    *acts, pre_grad, b0, b1, b2, b3, back_other = call(
        dense_kernel,
        [shape((nodes, quarter), BF16)] * 4
        + [shape((4 * nodes, quarter), BF16)]
        + [shape((2 * nodes, quarter), F32)] * 4 + [shape((4, 2 * nodes, quarter), BF16)],
        ids, *near, *other, *grads, *weights,
        scratch=[pltpu.VMEM((4 * nodes, width), BF16)] + [pltpu.VMEM((4 * nodes, quarter), BF16)] * 2,
        flops=16 * nodes * quarter * width, vmem=40,
    )

    far, send_far, row = call(
        functools.partial(weight_grad_kernel, True),
        [shape((4, tile, quarter), F32), shape((4 * tile + ROWS, quarter), BF16), shape((ROWS, quarter), F32)],
        ids, *near[2:], *other[2:], pre_grad,
        scratch=[pltpu.VMEM((half, quarter), F32)], flops=4 * nodes * quarter * width, vmem=28,
    )
    received = after(swap(back_other, CORE), send_far)
    others = call(
        back_kernel, [shape((2, nodes, quarter), BF16)] * 3, b1, b2, b3, received, smem=0
    )
    vx, vz, vxz = [swap(v, m) for v, m in zip(others, masks)]
    from_y = swap(send_far, Y)
    kept_near, send_near = call(
        functools.partial(weight_grad_kernel, False),
        [shape((4, tile, quarter), F32), shape((4 * tile, quarter), BF16)],
        ids, *near[:2], *other[:2], after(pre_grad, others[0]),
        scratch=[pltpu.VMEM((half, quarter), F32)], flops=4 * nodes * quarter * width, vmem=28,
    )
    vx, from_y, kept_near = lax.optimization_barrier((vx, from_y, kept_near))
    grads_own = call(add_kernel, [shape((4, nodes, quarter), BF16)], b0, received, vx, vz, vxz, smem=0)[0]
    grads_away = swap(grads_own, Y)
    send, row = call(
        fold_y_kernel, [shape((4 * tile + ROWS, quarter), BF16), shape((ROWS, quarter), F32)],
        far, row, from_y, smem=0,
    )
    from_z = swap(send, Z)
    grads_away = after(grads_away, from_z)
    from_y = swap(after(send_near, grads_own), Y)
    acts = [acts[0]] + [swap(after(a, grads_own), m) for a, m in zip(acts[1:], shares)]
    (spread,) = call(
        functools.partial(spread_kernel, True), [shape((rows, tile, quarter), F32)],
        ids, lists_of, *tiles_of, grads_own, swap(grads_own, CORE),
        scratch=[pltpu.VMEM((rows, tile, quarter), F32)],
        smem=2, flops=GROUP * dests * slots * tile * tile * quarter,
    )
    (spread,) = call(
        functools.partial(spread_kernel, False), [shape((rows, tile, quarter), BF16)],
        ids, lists_of, *tiles_of, grads_away, swap(grads_away, CORE), spread,
        scratch=[pltpu.VMEM((rows, tile, quarter), F32)],
        smem=2, flops=GROUP * dests * slots * tile * tile * quarter,
    )
    spread_all = lax.all_to_all(spread, "row", 0, 0, tiled=True)
    from_y = after(from_y, *acts[1:])
    own, *send = call(
        fold_low_kernel,
        [shape((tile + ROWS, quarter), F32)] + [shape((tile + ROWS, quarter), BF16)] * 3,
        ids, kept_near, row, from_y, from_z,
    )
    own_other = swap(own, CORE)
    send[0] = after(send[0], own_other)
    received = [swap(s, m) for s, m in zip(send, (X, 2 * Z, 2 * Z | X))]
    (input_grad,) = call(finish_kernel, [shape((nodes, width), BF16)], spread_all, smem=0)
    (activations,) = call(act_kernel, [shape((nodes, width), BF16)], ids, lanes, *acts)
    received_other = [
        swap(received[0], CORE),
        swap(after(received[1], input_grad, activations), CORE),
        swap(received[2], CORE),
    ]
    weight_grad, row = call(
        weight_out_kernel, [shape((own_rows, width), F32), shape((1, own_rows), F32)],
        ids, own, *received, own_other, *received_other,
    )
    bias_grad = row.reshape(own_rows)

    return activations[None], input_grad[None], weight_grad, bias_grad


def fetch_weights(weight, bias):
    return (
        lax.all_gather(weight, ("row", "col"), axis=0, tiled=True),
        lax.all_gather(bias, ("row", "col"), axis=0, tiled=True),
    )


def body(features, weight, bias, node_mask, neighbour_tiles, tile_weights, out_grad):
    tile = tile_weights.shape[-1]
    dest_count = neighbour_tiles.shape[2]
    slot_count = neighbour_tiles.shape[3]
    lists = neighbour_tiles[0, 0]
    valid = lists >= 0
    blocks = jnp.where(valid[:, :, None, None], tile_weights[0, 0], jnp.zeros((), jnp.bfloat16))
    group = 4
    turns = dest_count // group
    full_weight, full_bias = fetch_weights(weight, bias)
    source = lax.all_gather(features, "row", axis=1, tiled=True)[0]
    width = source.shape[-1]
    source_count = source.shape[0] // tile
    source_index = jnp.arange(source_count, dtype=jnp.int32)
    selector = ((lists[:, :, None] == source_index[None, None, :]) & valid[:, :, None]).astype(
        jnp.bfloat16
    )
    grouped_selector = selector.reshape(turns, group, slot_count, source_count)
    grouped_blocks = blocks.reshape(turns, group, slot_count, tile, tile)

    def dense_strip(group_selector, group_blocks):
        strip = jnp.einsum(
            "gsj,gsik->gijk", group_selector, group_blocks, preferred_element_type=jnp.float32
        )
        return strip.astype(jnp.bfloat16).reshape(group * tile, source_count * tile)

    def aggregate_group(pieces):
        group_selector, group_blocks = pieces
        strip = dense_strip(group_selector, group_blocks)
        return jnp.dot(strip, source, preferred_element_type=jnp.float32)

    partial_value = lax.map(aggregate_group, (grouped_selector, grouped_blocks)).reshape(-1, width)
    summed = lax.psum_scatter(partial_value, "col", scatter_dimension=0, tiled=True)
    aggregate = summed.astype(jnp.bfloat16)
    pre = jnp.dot(aggregate, full_weight, preferred_element_type=jnp.float32) + full_bias.astype(
        jnp.float32
    )
    keep = node_mask[0].astype(jnp.float32)[:, None]
    sigmoid_pre = jax.nn.sigmoid(pre)
    activations = (keep * (pre * sigmoid_pre)).astype(jnp.bfloat16)[None]
    slope = sigmoid_pre * (1.0 + pre * (1.0 - sigmoid_pre))
    pre_grad = (out_grad[0].astype(jnp.float32) * keep * slope).astype(jnp.bfloat16)
    weight_term = lax.dot_general(
        aggregate, pre_grad, (((0,), (0,)), ((), ())), preferred_element_type=jnp.float32
    )
    bias_term = jnp.sum(pre_grad.astype(jnp.float32), axis=0)
    weight_grad, bias_grad = (
        lax.psum_scatter(weight_term, ("row", "col"), scatter_dimension=0, tiled=True),
        lax.psum_scatter(bias_term, ("row", "col"), scatter_dimension=0, tiled=True),
    )
    aggregate_grad = lax.dot_general(
        pre_grad, full_weight, (((1,), (1,)), ((), ())), preferred_element_type=jnp.float32
    ).astype(jnp.bfloat16)
    dest_rows = lax.all_gather(aggregate_grad, "col", axis=0, tiled=True)
    grouped_grads = dest_rows.reshape(turns, group * tile, width)

    def spread_group(totals, pieces):
        group_selector, group_blocks, group_grads = pieces
        strip = dense_strip(group_selector, group_blocks)
        terms = lax.dot_general(
            strip, group_grads, (((0,), (0,)), ((), ())), preferred_element_type=jnp.float32
        )
        return (totals + terms, None)

    initial = jnp.zeros((source_count * tile, width), jnp.float32)
    source_terms, unused = lax.scan(
        spread_group, initial, (grouped_selector, grouped_blocks, grouped_grads)
    )
    input_grad = lax.psum_scatter(source_terms, "row", scatter_dimension=0, tiled=True)
    input_grad = input_grad.astype(jnp.bfloat16)[None]
    return (activations, input_grad, weight_grad, bias_grad)


def solution(mesh):
    chips = mesh.shape["row"] == 8 and mesh.shape["col"] == 4
    return jax.shard_map(
        chip_body if chips else body,
        mesh=mesh,
        in_specs=(
            P("col", "row", None),
            P(("row", "col"), None),
            P(("row", "col")),
            P("row", "col"),
            P("row", "col", None, None),
            P("row", "col", None, None, None, None),
            P("row", "col", None),
        ),
        out_specs=(
            P("row", "col", None),
            P("col", "row", None),
            P(("row", "col"), None),
            P(("row", "col")),
        ),
        check_vma=False,
    )
```

```python
import functools

import jax
import jax.numpy as jnp
from jax import lax
from jax.experimental import pallas as pl
from jax.experimental.pallas import tpu as pltpu
from jax.sharding import PartitionSpec as P

BOTH = ("row", "col")
F32 = jnp.float32
BF16 = jnp.bfloat16
VMEM = pl.BlockSpec(memory_space=pltpu.VMEM)
SMEM = pl.BlockSpec(memory_space=pltpu.SMEM)
CORE, Y, X, Z = 1, 2, 4, 8
GROUP = 4
SLOTS = 3
ROWS = 16


def swap(value, mask, total=32):
    return lax.ppermute(value, BOTH, [(i, i ^ mask) for i in range(total)])


def after(value, *others):
    return lax.optimization_barrier((value,) + others)[0]


def shape(dims, dtype):
    return jax.ShapeDtypeStruct(dims, dtype)


def call(kernel, outs, *operands, scratch=(), smem=1, flops=0, vmem=24):
    moved = sum(o.size * o.dtype.itemsize for o in operands)
    moved += sum(o.size * o.dtype.itemsize for o in outs)
    return pl.pallas_call(
        kernel,
        out_shape=outs,
        in_specs=[SMEM] * smem + [VMEM] * (len(operands) - smem),
        out_specs=[VMEM] * len(outs),
        scratch_shapes=list(scratch),
        compiler_params=pltpu.CompilerParams(vmem_limit_bytes=vmem * 2**20),
        cost_estimate=pl.CostEstimate(flops=flops, bytes_accessed=moved, transcendentals=0),
    )(*operands)


def split_kernel(ids, value, bias, *pieces):
    part = pieces[0].shape[-1]
    many = bias.shape[1]
    own, none = bias[...].astype(F32), jnp.zeros(bias.shape, F32)
    row = jnp.where(
        ids[1] == 0, jnp.concatenate([own, none], axis=1), jnp.concatenate([none, own], axis=1)
    )
    at = pl.ds(pl.multiple_of((ids[5] * 2 + ids[2]) * (2 * many), 2 * many), 2 * many)
    for i, piece in enumerate(pieces):
        piece[:-ROWS] = value[:, pl.ds(pl.multiple_of((ids[7] ^ i) * part, part), part)]
        piece[-ROWS:] = jnp.zeros((ROWS, part), BF16)
        piece[-ROWS:, at] = jnp.broadcast_to(row, (ROWS, 2 * many)).astype(BF16)


def split_masked_kernel(ids, mask, value, *pieces):
    part, lanes = pieces[0].shape[-1], mask.shape[-1]
    for i, piece in enumerate(pieces):
        start = pl.multiple_of((ids[7] ^ i) * part, part)
        for j in range(part // lanes):
            cols = pl.ds(start + j * lanes, lanes)
            piece[:, j * lanes : (j + 1) * lanes] = value[:, cols] * mask[...]


def block_kernel(ids, p0, p1, p2, p3, block):
    rows = p0.shape[0] - ROWS
    for i, piece in enumerate((p0, p1, p2, p3)):
        at = (i >> 1) * 2 + (ids[1] ^ (i & 1))
        block[pl.ds(pl.multiple_of(at * rows, rows), rows), :] = piece[:rows]
    block[4 * rows :] = p0[rows:] + p1[rows:] + p2[rows:] + p3[rows:]


def columns_kernel(ids, own, far, *pieces):
    member = ids[0]
    part, half = pieces[0].shape[-1] // 2, far.shape[-1] // 2
    for i, piece in enumerate(pieces):
        for j in range(2):
            cols = pl.ds(pl.multiple_of(j * half + (member ^ i) * part, part), part)
            piece[0, :, j * part : (j + 1) * part] = own[0, :, cols]
            piece[1, :, j * part : (j + 1) * part] = far[:, cols]


def gather_kernel(ids, lists, a0, a1, a2, a3, h0, h1, h2, h3, keep, send, source):
    member, core, row = ids[0], ids[1], ids[8]
    tile, dests = keep.shape[2], 2 * keep.shape[1]
    for i, piece in enumerate((h0, h1, h2, h3)):
        source[row ^ i] = piece[0]
        source[row ^ i ^ GROUP] = piece[1]
    for i, tiles in enumerate((a0, a1, a2, a3)):
        for pair in range(dests // 2):
            for other in range(2):
                m = pair * 2 + (core if other == 0 else 1 - core)
                left, right = [], []
                for s in range(SLOTS):
                    slot = m * SLOTS + s
                    listed = lists[i, slot]
                    block = tiles[pl.ds(pl.multiple_of(slot * tile, tile), tile), :]
                    left.append(jnp.where(listed >= 0, block, jnp.zeros_like(block)))
                    right.append(source[jnp.maximum(listed, 0)])
                total = jnp.dot(
                    jnp.concatenate(left, axis=1),
                    jnp.concatenate(right, axis=0),
                    preferred_element_type=F32,
                )
                if other == 0:
                    keep[member ^ i, pair] = total
                else:
                    send[member ^ i, pair] = total.astype(send.dtype)


def pair_sum_kernel(ids, kept, received, mine, send):
    y = ids[2]
    for g in range(GROUP):
        mine[g] = kept[g, y] + received[g, y].astype(F32)
        send[g] = (kept[g, 1 - y] + received[g, 1 - y].astype(F32)).astype(send.dtype)


def group_kernel(ids, mine, received, near, far):
    low = ids[6]
    for out, z in ((near, low), (far, 1 - low)):
        for x in range(2):
            nodes = mine.shape[1]
            total = mine[2 * z + x] + received[2 * z + x].astype(F32)
            out[x * nodes : (x + 1) * nodes, :] = total.astype(BF16)
        out[2 * nodes :, :] = jnp.zeros((out.shape[0] - 2 * nodes, out.shape[1]), BF16)


def dense_kernel(ids, p0, p1, p2, p3, q0, q1, q2, q3, o0, o1, o2, o3, *rest):
    weights = rest[:8]
    a0, a1, a2, a3, pre_grad, b0, b1, b2, b3, back_other, left, grads, acts = rest[8:]
    back_own = (b0, b1, b2, b3)
    y, high, z, x = ids[2], ids[4], ids[3], ids[5]
    part = pre_grad.shape[1]
    pair, block = b0.shape[0], part // 4
    nodes = pair // 2

    def lanes(i):
        return pl.ds(pl.multiple_of(((high ^ (i >> 2)) * 2 + (y ^ (i & 1))) * block, block), block)

    def quarter(i, j):
        return (i & 2) + j

    def place(i):
        return pl.ds(pl.multiple_of((i & 1) * pair + (x ^ (i >> 1)) * nodes, nodes), nodes)

    for i in range(8):
        for j in range(2):
            cols = slice((2 * i + j) * block, (2 * i + j + 1) * block)
            left[:pair, cols] = (p0, p1, p2, p3)[quarter(i, j)][:pair, lanes(i)]
            left[pair:, cols] = (q0, q1, q2, q3)[quarter(i, j)][:pair, lanes(i)]
    for i, piece in enumerate((o0, o1, o2, o3)):
        grads[place(i), :] = piece[...]
    many = 2 * block
    bias = sum(
        w[many:, :].astype(F32) * (z ^ (i >> 1) == ids[7]).astype(F32) for i, w in enumerate(weights)
    )[:1]
    step = 256
    for n in range(part // step):
        cols = slice(n * step, (n + 1) * step)
        matrix = jnp.concatenate([w[:many, cols] for w in weights], axis=0)
        pre = jnp.dot(left[...], matrix, preferred_element_type=F32) + bias[:, cols]
        sigmoid = 1.0 / (1.0 + jnp.exp(-pre))
        acts[:, cols] = (pre * sigmoid).astype(BF16)
        slope = sigmoid * (1.0 + pre * (1.0 - sigmoid))
        pre_grad[:, cols] = (grads[:, cols].astype(F32) * slope).astype(BF16)
    for i, piece in enumerate((a0, a1, a2, a3)):
        piece[...] = acts[place(i), :]
    for i, weight in enumerate(weights):
        back = lax.dot_general(
            pre_grad[...], weight[:many, :], (((1,), (1,)), ((), ())), preferred_element_type=F32
        )
        for j in range(2):
            cols = slice(j * block, (j + 1) * block)
            back_own[quarter(i, j)][:, lanes(i)] = back[:pair, cols]
            back_other[quarter(i, j), :, lanes(i)] = back[pair:, cols].astype(BF16)


def back_kernel(b1, b2, b3, received, v1, v2, v3):
    nodes = v1.shape[1]
    for i, (own, out) in enumerate(((b1, v1), (b2, v2), (b3, v3))):
        for x in range(2):
            rows = slice(x * nodes, (x + 1) * nodes)
            out[x] = (own[rows, :] + received[i + 1, rows, :].astype(F32)).astype(BF16)


def add_kernel(own, received, vx, vz, vxz, out):
    nodes = vx.shape[1]
    for x in range(2):
        rows = slice(x * nodes, (x + 1) * nodes)
        out[x] = (own[rows, :] + received[0, rows, :].astype(F32) + vx[x].astype(F32)).astype(BF16)
        out[2 + x] = (vz[x].astype(F32) + vxz[x].astype(F32)).astype(BF16)


def spread_kernel(near, ids, lists, a0, a1, a2, a3, same, cross, *rest):
    start, out, total = (None,) + rest if near else rest
    core, y, x = ids[1], ids[2], ids[5]
    tile = out.shape[1]
    total[...] = jnp.zeros_like(total) if near else start[...]
    for i, tiles in enumerate((a0, a1, a2, a3)):
        for other, grads in enumerate((same, cross)):
            m = (y if near else 1 - y) * 2 + (core ^ other)
            left = []
            for s in range(SLOTS):
                slot = m * SLOTS + s
                block = tiles[pl.ds(pl.multiple_of(slot * tile, tile), tile), :]
                left.append(jnp.where(lists[i, slot] >= 0, block, jnp.zeros_like(block)))
            terms = lax.dot_general(
                jnp.concatenate(left, axis=1), grads[2 * (i >> 1) + (x ^ (i & 1))],
                (((0,), (0,)), ((), ())), preferred_element_type=F32,
            )
            for s in range(SLOTS):
                at = jnp.maximum(lists[i, m * SLOTS + s], 0)
                total[at] += terms[s * tile : (s + 1) * tile]
    out[...] = total[...].astype(out.dtype)


def finish_kernel(terms, out):
    part, half = terms.shape[-1] // 2, out.shape[-1] // 2
    for g in range(GROUP):
        total = sum(terms[i].astype(F32) for i in range(g, terms.shape[0], GROUP)).astype(BF16)
        out[:, g * part : (g + 1) * part] = total[:, :part]
        out[:, half + g * part : half + (g + 1) * part] = total[:, part:]


def act_kernel(ids, mask, a0, a1, a2, a3, out):
    part, lanes = a0.shape[-1], mask.shape[-1]
    for i, piece in enumerate((a0, a1, a2, a3)):
        start = pl.multiple_of((ids[7] ^ i) * part, part)
        for j in range(part // lanes):
            out[:, pl.ds(start + j * lanes, lanes)] = piece[:, j * lanes : (j + 1) * lanes] * mask[...]


def weight_grad_kernel(far, ids, own0, own1, other0, other1, grads, keep, send, *rest):
    y, x = ids[2], ids[5]
    block = keep.shape[1]
    row, total = rest if far else (None,) + rest
    pair = grads.shape[0] // 2
    for j, (own, other) in enumerate(((own0, other0), (own1, other1))):
        total[4 * j * block : 4 * (j + 1) * block, :] = lax.dot_general(
            jnp.concatenate([own[:pair, :], other[:pair, :]], axis=0), grads[...],
            (((0,), (0,)), ((), ())), preferred_element_type=F32,
        )
    for i in range(4):
        at = ((i & 1) ^ x) * 4 + (i >> 1) * 2
        keep[i] = total[pl.ds(pl.multiple_of((at + y) * block, block), block), :]
        value = total[pl.ds(pl.multiple_of((at + 1 - y) * block, block), block), :]
        send[i * block : (i + 1) * block, :] = value.astype(BF16)
    if far:
        sums = jnp.sum(grads[...].astype(F32), axis=0, keepdims=True)
        row[...] = jnp.broadcast_to(sums, row.shape)
        send[4 * block :, :] = row[...].astype(BF16)


def fold_y_kernel(keep, row, received, send, both):
    block = keep.shape[1]
    for i in range(4):
        rows = slice(i * block, (i + 1) * block)
        send[rows, :] = (keep[i] + received[rows, :].astype(F32)).astype(BF16)
    both[...] = row[...] + received[4 * block :, :].astype(F32)
    send[4 * block :, :] = both[...].astype(BF16)


def fold_low_kernel(ids, keep, row, from_y, from_z, own, s1, s2, s3):
    high, x, block = ids[4], ids[5], keep.shape[1]
    sums = row[...] + from_z[4 * block :, :].astype(F32)
    for i, out in enumerate((own, s1, s2, s3)):
        at = (high ^ (i >> 1)) * 2 + (x ^ (i & 1))
        rows = pl.ds(pl.multiple_of(at * block, block), block)
        total = keep[at] + from_y[rows, :].astype(F32) + from_z[rows, :].astype(F32)
        out[:block, :] = total.astype(out.dtype)
        out[block:, :] = sums.astype(out.dtype)


def weight_out_kernel(ids, own, r1, r2, r3, own_c, r1_c, r2_c, r3_c, out, bias):
    many, part = out.shape[0], own.shape[1]
    block = 2 * many
    rows = pl.ds(pl.multiple_of(ids[1] * many, many), many)
    pairs = ((own, r2), (own_c, r2_c), (r1, r3), (r1_c, r3_c))
    total = 0.0
    for i, (left, right) in enumerate(pairs):
        cols = pl.ds(pl.multiple_of((ids[7] ^ i) * part, part), part)
        out[:, cols] = left[rows, :].astype(F32) + right[rows, :].astype(F32)
        quarter = left[block:, :].astype(F32) + right[block:, :].astype(F32)
        total += quarter * (ids[3] ^ ids[7] == i).astype(F32)
    step = 2 * many
    picked = sum(
        total[:1, i * step : (i + 1) * step] * ((ids[5] * 2 + ids[2]) == i).astype(F32) for i in range(4)
    )
    bias[...] = jnp.where(ids[1] == 0, picked[:, :many], picked[:, many:])


def chip_body(features, weight, bias, node_mask, neighbour_tiles, tile_weights, out_grad):
    rows, cols = lax.axis_size("row"), lax.axis_size("col")
    devices = rows * cols
    r, c = lax.axis_index("row"), lax.axis_index("col")
    core, z = c & 1, r >> 1
    place = (r & 1) * 2 + core
    ids = jnp.stack([r & 3, core, c >> 1, z, r >> 2, r & 1, z & 1, place, r]).astype(jnp.int32)
    nodes, width = features.shape[1:]
    half, quarter = width // 2, width // GROUP
    lists, tiles = neighbour_tiles[0, 0], tile_weights[0, 0]
    dests, slots, tile = tiles.shape[0], tiles.shape[1], tiles.shape[2]
    masks = (X, Z, X | Z)
    shares = (CORE, X, X | CORE)

    own_rows = weight.shape[0]
    pieces = call(split_kernel, [shape((own_rows + ROWS, quarter), BF16)] * 4, ids, weight, bias[None])
    pieces = [pieces[0]] + [swap(p, m) for p, m in zip(pieces[1:], shares)]
    (block,) = call(block_kernel, [shape((4 * own_rows + ROWS, quarter), BF16)], ids, *pieces)

    lists = jnp.pad(lists.reshape(1, -1), ((0, 15), (0, tile - dests * slots))).astype(BF16)
    tiles, lists = lax.optimization_barrier((tiles, lists, pieces[1]))[:2]
    tiles = jnp.concatenate([tiles.reshape(-1, tile), lists], axis=0)
    tiles_of = [tiles, swap(after(tiles, *pieces[2:]), X), swap(tiles, Z)]
    tiles_of.append(swap(tiles_of[2], X))
    lists_of = jnp.stack([t[-16, : dests * slots] for t in tiles_of]).astype(jnp.int32)

    columns = call(
        columns_kernel, [shape((2, nodes, quarter), BF16)] * 4, ids, features, after(swap(features[0], 2 * Z), tiles_of[1])
    )
    source = [columns[0]] + [swap(value, m) for value, m in zip(columns[1:], masks)]
    lanes = jnp.broadcast_to(node_mask[0][:, None].astype(BF16), (nodes, 128))
    grads = call(split_masked_kernel, [shape((nodes, quarter), BF16)] * 4, ids, lanes, out_grad[0])
    grads = [grads[0]] + [swap(g, m) for g, m in zip(grads[1:], shares)]

    y0, z1 = swap(block, Y), swap(block, Z)
    z2 = swap(after(block, y0, z1), 2 * Z)
    z3 = swap(after(z2, *grads[2:]), Z)
    y1, y2, y3 = [swap(value, Y) for value in (z1, z2, z3)]
    weights = [block, y0, z1, y1, z2, y2, z3, y3]

    source[0] = after(source[0], y0, z1)
    piece = (GROUP, dests // 2, tile, quarter)
    kept, sent = call(
        gather_kernel, [shape(piece, F32)] * 2,
        ids, lists_of, *tiles_of, *source,
        scratch=[pltpu.VMEM((rows, tile, quarter), BF16)],
        smem=2, flops=2 * GROUP * dests * slots * tile * tile * quarter,
    )
    mine, send = call(
        pair_sum_kernel, [shape((GROUP, tile, quarter), F32)] * 2,
        ids, kept, swap(after(sent, y1), CORE),
    )
    received = after(swap(send, Y), y1, z2, grads[1])
    near, far = call(group_kernel, [shape((2 * tile + 2 * ROWS, quarter), BF16)] * 2, ids, mine, received)
    near = [near, swap(near, X), swap(far, Z), swap(far, X | Z)]
    near[2] = after(near[2], y2, y3)
    other = [swap(value, CORE) for value in near]

    *acts, pre_grad, b0, b1, b2, b3, back_other = call(
        dense_kernel,
        [shape((nodes, quarter), BF16)] * 4
        + [shape((4 * nodes, quarter), BF16)]
        + [shape((2 * nodes, quarter), F32)] * 4 + [shape((4, 2 * nodes, quarter), BF16)],
        ids, *near, *other, *grads, *weights,
        scratch=[pltpu.VMEM((4 * nodes, width), BF16)] + [pltpu.VMEM((4 * nodes, quarter), BF16)] * 2,
        flops=16 * nodes * quarter * width, vmem=40,
    )

    far, send_far, row = call(
        functools.partial(weight_grad_kernel, True),
        [shape((4, tile, quarter), F32), shape((4 * tile + ROWS, quarter), BF16), shape((ROWS, quarter), F32)],
        ids, *near[2:], *other[2:], pre_grad,
        scratch=[pltpu.VMEM((half, quarter), F32)], flops=4 * nodes * quarter * width, vmem=28,
    )
    received = after(swap(back_other, CORE), send_far)
    others = call(
        back_kernel, [shape((2, nodes, quarter), BF16)] * 3, b1, b2, b3, received, smem=0
    )
    vx, vz, vxz = [swap(v, m) for v, m in zip(others, masks)]
    from_y = swap(send_far, Y)
    kept_near, send_near = call(
        functools.partial(weight_grad_kernel, False),
        [shape((4, tile, quarter), F32), shape((4 * tile, quarter), BF16)],
        ids, *near[:2], *other[:2], after(pre_grad, others[0]),
        scratch=[pltpu.VMEM((half, quarter), F32)], flops=4 * nodes * quarter * width, vmem=28,
    )
    vx, from_y, kept_near = lax.optimization_barrier((vx, from_y, kept_near))
    grads_own = call(add_kernel, [shape((4, nodes, quarter), BF16)], b0, received, vx, vz, vxz, smem=0)[0]
    grads_away = swap(grads_own, Y)
    send, row = call(
        fold_y_kernel, [shape((4 * tile + ROWS, quarter), BF16), shape((ROWS, quarter), F32)],
        far, row, from_y, smem=0,
    )
    from_z = swap(send, Z)
    grads_away = after(grads_away, from_z)
    from_y = swap(after(send_near, grads_own), Y)
    acts = [acts[0]] + [swap(after(a, grads_own), m) for a, m in zip(acts[1:], shares)]
    (spread,) = call(
        functools.partial(spread_kernel, True), [shape((rows, tile, quarter), F32)],
        ids, lists_of, *tiles_of, grads_own, swap(grads_own, CORE),
        scratch=[pltpu.VMEM((rows, tile, quarter), F32)],
        smem=2, flops=GROUP * dests * slots * tile * tile * quarter,
    )
    (spread,) = call(
        functools.partial(spread_kernel, False), [shape((rows, tile, quarter), BF16)],
        ids, lists_of, *tiles_of, grads_away, swap(grads_away, CORE), spread,
        scratch=[pltpu.VMEM((rows, tile, quarter), F32)],
        smem=2, flops=GROUP * dests * slots * tile * tile * quarter,
    )
    spread_all = lax.all_to_all(spread, "row", 0, 0, tiled=True)
    from_y = after(from_y, *acts[1:])
    own, *send = call(
        fold_low_kernel,
        [shape((tile + ROWS, quarter), F32)] + [shape((tile + ROWS, quarter), BF16)] * 3,
        ids, kept_near, row, from_y, from_z,
    )
    own_other = swap(own, CORE)
    send[0] = after(send[0], own_other)
    received = [swap(s, m) for s, m in zip(send, (X, 2 * Z, 2 * Z | X))]
    (input_grad,) = call(finish_kernel, [shape((nodes, width), BF16)], spread_all, smem=0)
    (activations,) = call(act_kernel, [shape((nodes, width), BF16)], ids, lanes, *acts)
    received_other = [
        swap(received[0], CORE),
        swap(after(received[1], input_grad, activations), CORE),
        swap(received[2], CORE),
    ]
    weight_grad, row = call(
        weight_out_kernel, [shape((own_rows, width), F32), shape((1, own_rows), F32)],
        ids, own, *received, own_other, *received_other,
    )
    bias_grad = row.reshape(own_rows)

    return activations[None], input_grad[None], weight_grad, bias_grad


def fetch_weights(weight, bias):
    return (
        lax.all_gather(weight, ("row", "col"), axis=0, tiled=True),
        lax.all_gather(bias, ("row", "col"), axis=0, tiled=True),
    )


def body(features, weight, bias, node_mask, neighbour_tiles, tile_weights, out_grad):
    tile = tile_weights.shape[-1]
    dest_count = neighbour_tiles.shape[2]
    slot_count = neighbour_tiles.shape[3]
    lists = neighbour_tiles[0, 0]
    valid = lists >= 0
    blocks = jnp.where(valid[:, :, None, None], tile_weights[0, 0], jnp.zeros((), jnp.bfloat16))
    group = 4
    turns = dest_count // group
    full_weight, full_bias = fetch_weights(weight, bias)
    source = lax.all_gather(features, "row", axis=1, tiled=True)[0]
    width = source.shape[-1]
    source_count = source.shape[0] // tile
    source_index = jnp.arange(source_count, dtype=jnp.int32)
    selector = ((lists[:, :, None] == source_index[None, None, :]) & valid[:, :, None]).astype(
        jnp.bfloat16
    )
    grouped_selector = selector.reshape(turns, group, slot_count, source_count)
    grouped_blocks = blocks.reshape(turns, group, slot_count, tile, tile)

    def dense_strip(group_selector, group_blocks):
        strip = jnp.einsum(
            "gsj,gsik->gijk", group_selector, group_blocks, preferred_element_type=jnp.float32
        )
        return strip.astype(jnp.bfloat16).reshape(group * tile, source_count * tile)

    def aggregate_group(pieces):
        group_selector, group_blocks = pieces
        strip = dense_strip(group_selector, group_blocks)
        return jnp.dot(strip, source, preferred_element_type=jnp.float32)

    partial_value = lax.map(aggregate_group, (grouped_selector, grouped_blocks)).reshape(-1, width)
    summed = lax.psum_scatter(partial_value, "col", scatter_dimension=0, tiled=True)
    aggregate = summed.astype(jnp.bfloat16)
    pre = jnp.dot(aggregate, full_weight, preferred_element_type=jnp.float32) + full_bias.astype(
        jnp.float32
    )
    keep = node_mask[0].astype(jnp.float32)[:, None]
    sigmoid_pre = jax.nn.sigmoid(pre)
    activations = (keep * (pre * sigmoid_pre)).astype(jnp.bfloat16)[None]
    slope = sigmoid_pre * (1.0 + pre * (1.0 - sigmoid_pre))
    pre_grad = (out_grad[0].astype(jnp.float32) * keep * slope).astype(jnp.bfloat16)
    weight_term = lax.dot_general(
        aggregate, pre_grad, (((0,), (0,)), ((), ())), preferred_element_type=jnp.float32
    )
    bias_term = jnp.sum(pre_grad.astype(jnp.float32), axis=0)
    weight_grad, bias_grad = (
        lax.psum_scatter(weight_term, ("row", "col"), scatter_dimension=0, tiled=True),
        lax.psum_scatter(bias_term, ("row", "col"), scatter_dimension=0, tiled=True),
    )
    aggregate_grad = lax.dot_general(
        pre_grad, full_weight, (((1,), (1,)), ((), ())), preferred_element_type=jnp.float32
    ).astype(jnp.bfloat16)
    dest_rows = lax.all_gather(aggregate_grad, "col", axis=0, tiled=True)
    grouped_grads = dest_rows.reshape(turns, group * tile, width)

    def spread_group(totals, pieces):
        group_selector, group_blocks, group_grads = pieces
        strip = dense_strip(group_selector, group_blocks)
        terms = lax.dot_general(
            strip, group_grads, (((0,), (0,)), ((), ())), preferred_element_type=jnp.float32
        )
        return (totals + terms, None)

    initial = jnp.zeros((source_count * tile, width), jnp.float32)
    source_terms, unused = lax.scan(
        spread_group, initial, (grouped_selector, grouped_blocks, grouped_grads)
    )
    input_grad = lax.psum_scatter(source_terms, "row", scatter_dimension=0, tiled=True)
    input_grad = input_grad.astype(jnp.bfloat16)[None]
    return (activations, input_grad, weight_grad, bias_grad)


def solution(mesh):
    chips = mesh.shape["row"] == 8 and mesh.shape["col"] == 4
    return jax.shard_map(
        chip_body if chips else body,
        mesh=mesh,
        in_specs=(
            P("col", "row", None),
            P(("row", "col"), None),
            P(("row", "col")),
            P("row", "col"),
            P("row", "col", None, None),
            P("row", "col", None, None, None, None),
            P("row", "col", None),
        ),
        out_specs=(
            P("row", "col", None),
            P("col", "row", None),
            P(("row", "col"), None),
            P(("row", "col")),
        ),
        check_vma=False,
    )
```

```python
import functools

import jax
import jax.numpy as jnp
from jax import lax
from jax.experimental import pallas as pl
from jax.experimental.pallas import tpu as pltpu
from jax.sharding import PartitionSpec as P

BOTH = ("row", "col")
F32 = jnp.float32
BF16 = jnp.bfloat16
VMEM = pl.BlockSpec(memory_space=pltpu.VMEM)
SMEM = pl.BlockSpec(memory_space=pltpu.SMEM)
CORE, Y, X, Z = 1, 2, 4, 8
GROUP = 4
SLOTS = 3
ROWS = 16


def swap(value, mask, total=32):
    return lax.ppermute(value, BOTH, [(i, i ^ mask) for i in range(total)])


def after(value, *others):
    return lax.optimization_barrier((value,) + others)[0]


def shape(dims, dtype):
    return jax.ShapeDtypeStruct(dims, dtype)


def call(kernel, outs, *operands, scratch=(), smem=1, flops=0, vmem=24):
    moved = sum(o.size * o.dtype.itemsize for o in operands)
    moved += sum(o.size * o.dtype.itemsize for o in outs)
    return pl.pallas_call(
        kernel,
        out_shape=outs,
        in_specs=[SMEM] * smem + [VMEM] * (len(operands) - smem),
        out_specs=[VMEM] * len(outs),
        scratch_shapes=list(scratch),
        compiler_params=pltpu.CompilerParams(vmem_limit_bytes=vmem * 2**20),
        cost_estimate=pl.CostEstimate(flops=flops, bytes_accessed=moved, transcendentals=0),
    )(*operands)


def split_kernel(ids, value, bias, *pieces):
    part = pieces[0].shape[-1]
    many = bias.shape[1]
    own, none = bias[...].astype(F32), jnp.zeros(bias.shape, F32)
    row = jnp.where(
        ids[1] == 0, jnp.concatenate([own, none], axis=1), jnp.concatenate([none, own], axis=1)
    )
    at = pl.ds(pl.multiple_of((ids[5] * 2 + ids[2]) * (2 * many), 2 * many), 2 * many)
    for i, piece in enumerate(pieces):
        piece[:-ROWS] = value[:, pl.ds(pl.multiple_of((ids[7] ^ i) * part, part), part)]
        piece[-ROWS:] = jnp.zeros((ROWS, part), BF16)
        piece[-ROWS:, at] = jnp.broadcast_to(row, (ROWS, 2 * many)).astype(BF16)


def split_masked_kernel(ids, mask, value, *pieces):
    part, lanes = pieces[0].shape[-1], mask.shape[-1]
    for i, piece in enumerate(pieces):
        start = pl.multiple_of((ids[7] ^ i) * part, part)
        for j in range(part // lanes):
            cols = pl.ds(start + j * lanes, lanes)
            piece[:, j * lanes : (j + 1) * lanes] = value[:, cols] * mask[...]


def block_kernel(ids, p0, p1, p2, p3, block):
    rows = p0.shape[0] - ROWS
    for i, piece in enumerate((p0, p1, p2, p3)):
        at = (i >> 1) * 2 + (ids[1] ^ (i & 1))
        block[pl.ds(pl.multiple_of(at * rows, rows), rows), :] = piece[:rows]
    block[4 * rows :] = p0[rows:] + p1[rows:] + p2[rows:] + p3[rows:]


def columns_kernel(ids, own, far, *pieces):
    member = ids[0]
    part, half = pieces[0].shape[-1] // 2, far.shape[-1] // 2
    for i, piece in enumerate(pieces):
        for j in range(2):
            cols = pl.ds(pl.multiple_of(j * half + (member ^ i) * part, part), part)
            piece[0, :, j * part : (j + 1) * part] = own[0, :, cols]
            piece[1, :, j * part : (j + 1) * part] = far[:, cols]


def gather_kernel(ids, lists, a0, a1, a2, a3, h0, h1, h2, h3, keep, send, source):
    member, core, row = ids[0], ids[1], ids[8]
    tile, dests = keep.shape[2], 2 * keep.shape[1]
    for i, piece in enumerate((h0, h1, h2, h3)):
        source[row ^ i] = piece[0]
        source[row ^ i ^ GROUP] = piece[1]
    for i, tiles in enumerate((a0, a1, a2, a3)):
        for pair in range(dests // 2):
            for other in range(2):
                m = pair * 2 + (core if other == 0 else 1 - core)
                left, right = [], []
                for s in range(SLOTS):
                    slot = m * SLOTS + s
                    listed = lists[i, slot]
                    block = tiles[pl.ds(pl.multiple_of(slot * tile, tile), tile), :]
                    left.append(jnp.where(listed >= 0, block, jnp.zeros_like(block)))
                    right.append(source[jnp.maximum(listed, 0)])
                total = jnp.dot(
                    jnp.concatenate(left, axis=1),
                    jnp.concatenate(right, axis=0),
                    preferred_element_type=F32,
                )
                if other == 0:
                    keep[member ^ i, pair] = total
                else:
                    send[member ^ i, pair] = total.astype(send.dtype)


def pair_sum_kernel(ids, kept, received, mine, send):
    y = ids[2]
    for g in range(GROUP):
        mine[g] = kept[g, y] + received[g, y].astype(F32)
        send[g] = (kept[g, 1 - y] + received[g, 1 - y].astype(F32)).astype(BF16)


def group_kernel(ids, mine, received, near, far):
    low = ids[6]
    for out, z in ((near, low), (far, 1 - low)):
        for x in range(2):
            nodes = mine.shape[1]
            total = mine[2 * z + x] + received[2 * z + x].astype(F32)
            out[x * nodes : (x + 1) * nodes, :] = total.astype(BF16)
        out[2 * nodes :, :] = jnp.zeros((out.shape[0] - 2 * nodes, out.shape[1]), BF16)


def dense_kernel(ids, p0, p1, p2, p3, q0, q1, q2, q3, o0, o1, o2, o3, *rest):
    weights = rest[:8]
    a0, a1, a2, a3, pre_grad, b0, b1, b2, b3, back_other, left, grads, acts = rest[8:]
    back_own = (b0, b1, b2, b3)
    y, high, z, x = ids[2], ids[4], ids[3], ids[5]
    part = pre_grad.shape[1]
    pair, block = b0.shape[0], part // 4
    nodes = pair // 2

    def lanes(i):
        return pl.ds(pl.multiple_of(((high ^ (i >> 2)) * 2 + (y ^ (i & 1))) * block, block), block)

    def quarter(i, j):
        return (i & 2) + j

    def place(i):
        return pl.ds(pl.multiple_of((i & 1) * pair + (x ^ (i >> 1)) * nodes, nodes), nodes)

    for i in range(8):
        for j in range(2):
            cols = slice((2 * i + j) * block, (2 * i + j + 1) * block)
            left[:pair, cols] = (p0, p1, p2, p3)[quarter(i, j)][:pair, lanes(i)]
            left[pair:, cols] = (q0, q1, q2, q3)[quarter(i, j)][:pair, lanes(i)]
    for i, piece in enumerate((o0, o1, o2, o3)):
        grads[place(i), :] = piece[...]
    many = 2 * block
    bias = sum(
        w[many:, :].astype(F32) * (z ^ (i >> 1) == ids[7]).astype(F32) for i, w in enumerate(weights)
    )[:1]
    step = 256
    for n in range(part // step):
        cols = slice(n * step, (n + 1) * step)
        matrix = jnp.concatenate([w[:many, cols] for w in weights], axis=0)
        pre = jnp.dot(left[...], matrix, preferred_element_type=F32) + bias[:, cols]
        sigmoid = 1.0 / (1.0 + jnp.exp(-pre))
        acts[:, cols] = (pre * sigmoid).astype(BF16)
        slope = sigmoid * (1.0 + pre * (1.0 - sigmoid))
        pre_grad[:, cols] = (grads[:, cols].astype(F32) * slope).astype(BF16)
    for i, piece in enumerate((a0, a1, a2, a3)):
        piece[...] = acts[place(i), :]
    for i, weight in enumerate(weights):
        back = lax.dot_general(
            pre_grad[...], weight[:many, :], (((1,), (1,)), ((), ())), preferred_element_type=F32
        )
        for j in range(2):
            cols = slice(j * block, (j + 1) * block)
            back_own[quarter(i, j)][:, lanes(i)] = back[:pair, cols]
            back_other[quarter(i, j), :, lanes(i)] = back[pair:, cols].astype(BF16)


def back_kernel(b1, b2, b3, received, v1, v2, v3):
    nodes = v1.shape[1]
    for i, (own, out) in enumerate(((b1, v1), (b2, v2), (b3, v3))):
        for x in range(2):
            rows = slice(x * nodes, (x + 1) * nodes)
            out[x] = (own[rows, :] + received[i + 1, rows, :].astype(F32)).astype(BF16)


def add_kernel(own, received, vx, vz, vxz, out):
    nodes = vx.shape[1]
    for x in range(2):
        rows = slice(x * nodes, (x + 1) * nodes)
        out[x] = (own[rows, :] + received[0, rows, :].astype(F32) + vx[x].astype(F32)).astype(BF16)
        out[2 + x] = (vz[x].astype(F32) + vxz[x].astype(F32)).astype(BF16)


def spread_kernel(near, ids, lists, a0, a1, a2, a3, same, cross, *rest):
    start, out, total = (None,) + rest if near else rest
    core, y, x = ids[1], ids[2], ids[5]
    tile = out.shape[1]
    total[...] = jnp.zeros_like(total) if near else start[...]
    for i, tiles in enumerate((a0, a1, a2, a3)):
        for other, grads in enumerate((same, cross)):
            m = (y if near else 1 - y) * 2 + (core ^ other)
            left = []
            for s in range(SLOTS):
                slot = m * SLOTS + s
                block = tiles[pl.ds(pl.multiple_of(slot * tile, tile), tile), :]
                left.append(jnp.where(lists[i, slot] >= 0, block, jnp.zeros_like(block)))
            terms = lax.dot_general(
                jnp.concatenate(left, axis=1), grads[2 * (i >> 1) + (x ^ (i & 1))],
                (((0,), (0,)), ((), ())), preferred_element_type=F32,
            )
            for s in range(SLOTS):
                at = jnp.maximum(lists[i, m * SLOTS + s], 0)
                total[at] += terms[s * tile : (s + 1) * tile]
    out[...] = total[...].astype(out.dtype)


def finish_kernel(terms, out):
    part, half = terms.shape[-1] // 2, out.shape[-1] // 2
    for g in range(GROUP):
        total = sum(terms[i].astype(F32) for i in range(g, terms.shape[0], GROUP)).astype(BF16)
        out[:, g * part : (g + 1) * part] = total[:, :part]
        out[:, half + g * part : half + (g + 1) * part] = total[:, part:]


def act_kernel(ids, mask, a0, a1, a2, a3, out):
    part, lanes = a0.shape[-1], mask.shape[-1]
    for i, piece in enumerate((a0, a1, a2, a3)):
        start = pl.multiple_of((ids[7] ^ i) * part, part)
        for j in range(part // lanes):
            out[:, pl.ds(start + j * lanes, lanes)] = piece[:, j * lanes : (j + 1) * lanes] * mask[...]


def weight_grad_kernel(far, ids, own0, own1, other0, other1, grads, keep, send, *rest):
    y, x = ids[2], ids[5]
    block = keep.shape[1]
    row, total = rest if far else (None,) + rest
    pair = grads.shape[0] // 2
    for j, (own, other) in enumerate(((own0, other0), (own1, other1))):
        total[4 * j * block : 4 * (j + 1) * block, :] = lax.dot_general(
            jnp.concatenate([own[:pair, :], other[:pair, :]], axis=0), grads[...],
            (((0,), (0,)), ((), ())), preferred_element_type=F32,
        )
    for i in range(4):
        at = ((i & 1) ^ x) * 4 + (i >> 1) * 2
        keep[i] = total[pl.ds(pl.multiple_of((at + y) * block, block), block), :]
        value = total[pl.ds(pl.multiple_of((at + 1 - y) * block, block), block), :]
        send[i * block : (i + 1) * block, :] = value.astype(BF16)
    if far:
        sums = jnp.sum(grads[...].astype(F32), axis=0, keepdims=True)
        row[...] = jnp.broadcast_to(sums, row.shape)
        send[4 * block :, :] = row[...].astype(BF16)


def fold_y_kernel(keep, row, received, send, both):
    block = keep.shape[1]
    for i in range(4):
        rows = slice(i * block, (i + 1) * block)
        send[rows, :] = (keep[i] + received[rows, :].astype(F32)).astype(BF16)
    both[...] = row[...] + received[4 * block :, :].astype(F32)
    send[4 * block :, :] = both[...].astype(BF16)


def fold_low_kernel(ids, keep, row, from_y, from_z, own, s1, s2, s3):
    high, x, block = ids[4], ids[5], keep.shape[1]
    sums = row[...] + from_z[4 * block :, :].astype(F32)
    for i, out in enumerate((own, s1, s2, s3)):
        at = (high ^ (i >> 1)) * 2 + (x ^ (i & 1))
        rows = pl.ds(pl.multiple_of(at * block, block), block)
        total = keep[at] + from_y[rows, :].astype(F32) + from_z[rows, :].astype(F32)
        out[:block, :] = total.astype(out.dtype)
        out[block:, :] = sums.astype(out.dtype)


def weight_out_kernel(ids, own, r1, r2, r3, own_c, r1_c, r2_c, r3_c, out, bias):
    many, part = out.shape[0], own.shape[1]
    block = 2 * many
    rows = pl.ds(pl.multiple_of(ids[1] * many, many), many)
    pairs = ((own, r2), (own_c, r2_c), (r1, r3), (r1_c, r3_c))
    total = 0.0
    for i, (left, right) in enumerate(pairs):
        cols = pl.ds(pl.multiple_of((ids[7] ^ i) * part, part), part)
        out[:, cols] = left[rows, :].astype(F32) + right[rows, :].astype(F32)
        quarter = left[block:, :].astype(F32) + right[block:, :].astype(F32)
        total += quarter * (ids[3] ^ ids[7] == i).astype(F32)
    step = 2 * many
    picked = sum(
        total[:1, i * step : (i + 1) * step] * ((ids[5] * 2 + ids[2]) == i).astype(F32) for i in range(4)
    )
    bias[...] = jnp.where(ids[1] == 0, picked[:, :many], picked[:, many:])


def chip_body(features, weight, bias, node_mask, neighbour_tiles, tile_weights, out_grad):
    rows, cols = lax.axis_size("row"), lax.axis_size("col")
    devices = rows * cols
    r, c = lax.axis_index("row"), lax.axis_index("col")
    core, z = c & 1, r >> 1
    place = (r & 1) * 2 + core
    ids = jnp.stack([r & 3, core, c >> 1, z, r >> 2, r & 1, z & 1, place, r]).astype(jnp.int32)
    nodes, width = features.shape[1:]
    half, quarter = width // 2, width // GROUP
    lists, tiles = neighbour_tiles[0, 0], tile_weights[0, 0]
    dests, slots, tile = tiles.shape[0], tiles.shape[1], tiles.shape[2]
    masks = (X, Z, X | Z)
    shares = (CORE, X, X | CORE)

    own_rows = weight.shape[0]
    pieces = call(split_kernel, [shape((own_rows + ROWS, quarter), BF16)] * 4, ids, weight, bias[None])
    pieces = [pieces[0]] + [swap(p, m) for p, m in zip(pieces[1:], shares)]
    (block,) = call(block_kernel, [shape((4 * own_rows + ROWS, quarter), BF16)], ids, *pieces)

    lists = jnp.pad(lists.reshape(1, -1), ((0, 15), (0, tile - dests * slots))).astype(BF16)
    tiles = jnp.concatenate([tiles.reshape(-1, tile), lists], axis=0)
    tiles_of = [tiles, swap(after(tiles, *pieces[2:]), X), swap(tiles, Z)]
    tiles_of.append(swap(tiles_of[2], X))
    lists_of = jnp.stack([t[-16, : dests * slots] for t in tiles_of]).astype(jnp.int32)

    columns = call(
        columns_kernel, [shape((2, nodes, quarter), BF16)] * 4, ids, features, after(swap(features[0], 2 * Z), tiles_of[1])
    )
    source = [columns[0]] + [swap(value, m) for value, m in zip(columns[1:], masks)]
    lanes = jnp.broadcast_to(node_mask[0][:, None].astype(BF16), (nodes, 128))
    grads = call(split_masked_kernel, [shape((nodes, quarter), BF16)] * 4, ids, lanes, out_grad[0])
    grads = [grads[0]] + [swap(g, m) for g, m in zip(grads[1:], shares)]

    y0, z1 = swap(block, Y), swap(block, Z)
    z2 = swap(after(block, y0, z1), 2 * Z)
    z3 = swap(after(z2, *grads[2:]), Z)
    y1, y2, y3 = [swap(value, Y) for value in (z1, z2, z3)]
    weights = [block, y0, z1, y1, z2, y2, z3, y3]

    source[0] = after(source[0], y0, z1)
    piece = (GROUP, dests // 2, tile, quarter)
    kept, sent = call(
        gather_kernel, [shape(piece, F32)] * 2,
        ids, lists_of, *tiles_of, *source,
        scratch=[pltpu.VMEM((rows, tile, quarter), BF16)],
        smem=2, flops=2 * GROUP * dests * slots * tile * tile * quarter,
    )
    mine, send = call(
        pair_sum_kernel, [shape((GROUP, tile, quarter), F32), shape((GROUP, tile, quarter), BF16)],
        ids, kept, swap(after(sent, y1), CORE),
    )
    received = after(swap(send, Y), y1, z2, grads[1])
    near, far = call(group_kernel, [shape((2 * tile + 2 * ROWS, quarter), BF16)] * 2, ids, mine, received)
    near = [near, swap(near, X), swap(far, Z), swap(far, X | Z)]
    near[2] = after(near[2], y2, y3)
    other = [swap(value, CORE) for value in near]

    *acts, pre_grad, b0, b1, b2, b3, back_other = call(
        dense_kernel,
        [shape((nodes, quarter), BF16)] * 4
        + [shape((4 * nodes, quarter), BF16)]
        + [shape((2 * nodes, quarter), F32)] * 4 + [shape((4, 2 * nodes, quarter), BF16)],
        ids, *near, *other, *grads, *weights,
        scratch=[pltpu.VMEM((4 * nodes, width), BF16)] + [pltpu.VMEM((4 * nodes, quarter), BF16)] * 2,
        flops=16 * nodes * quarter * width, vmem=40,
    )

    far, send_far, row = call(
        functools.partial(weight_grad_kernel, True),
        [shape((4, tile, quarter), F32), shape((4 * tile + ROWS, quarter), BF16), shape((ROWS, quarter), F32)],
        ids, *near[2:], *other[2:], pre_grad,
        scratch=[pltpu.VMEM((half, quarter), F32)], flops=4 * nodes * quarter * width, vmem=28,
    )
    received = after(swap(back_other, CORE), send_far)
    others = call(
        back_kernel, [shape((2, nodes, quarter), BF16)] * 3, b1, b2, b3, received, smem=0
    )
    vx, vz, vxz = [swap(v, m) for v, m in zip(others, masks)]
    from_y = swap(send_far, Y)
    kept_near, send_near = call(
        functools.partial(weight_grad_kernel, False),
        [shape((4, tile, quarter), F32), shape((4 * tile, quarter), BF16)],
        ids, *near[:2], *other[:2], after(pre_grad, others[0]),
        scratch=[pltpu.VMEM((half, quarter), F32)], flops=4 * nodes * quarter * width, vmem=28,
    )
    vx, from_y, kept_near = lax.optimization_barrier((vx, from_y, kept_near))
    grads_own = call(add_kernel, [shape((4, nodes, quarter), BF16)], b0, received, vx, vz, vxz, smem=0)[0]
    grads_away = swap(grads_own, Y)
    send, row = call(
        fold_y_kernel, [shape((4 * tile + ROWS, quarter), BF16), shape((ROWS, quarter), F32)],
        far, row, from_y, smem=0,
    )
    from_z = swap(send, Z)
    grads_away = after(grads_away, from_z)
    from_y = swap(after(send_near, grads_own), Y)
    acts = [acts[0]] + [swap(after(a, grads_own), m) for a, m in zip(acts[1:], shares)]
    (spread,) = call(
        functools.partial(spread_kernel, True), [shape((rows, tile, quarter), F32)],
        ids, lists_of, *tiles_of, grads_own, swap(grads_own, CORE),
        scratch=[pltpu.VMEM((rows, tile, quarter), F32)],
        smem=2, flops=GROUP * dests * slots * tile * tile * quarter,
    )
    (spread,) = call(
        functools.partial(spread_kernel, False), [shape((rows, tile, quarter), BF16)],
        ids, lists_of, *tiles_of, grads_away, swap(grads_away, CORE), spread,
        scratch=[pltpu.VMEM((rows, tile, quarter), F32)],
        smem=2, flops=GROUP * dests * slots * tile * tile * quarter,
    )
    spread_all = lax.all_to_all(spread, "row", 0, 0, tiled=True)
    from_y = after(from_y, *acts[1:])
    own, *send = call(
        fold_low_kernel,
        [shape((tile + ROWS, quarter), F32)] + [shape((tile + ROWS, quarter), BF16)] * 3,
        ids, kept_near, row, from_y, from_z,
    )
    own_other = swap(own, CORE)
    send[0] = after(send[0], own_other)
    received = [swap(s, m) for s, m in zip(send, (X, 2 * Z, 2 * Z | X))]
    (input_grad,) = call(finish_kernel, [shape((nodes, width), BF16)], spread_all, smem=0)
    (activations,) = call(act_kernel, [shape((nodes, width), BF16)], ids, lanes, *acts)
    received_other = [
        swap(received[0], CORE),
        swap(after(received[1], input_grad, activations), CORE),
        swap(received[2], CORE),
    ]
    weight_grad, row = call(
        weight_out_kernel, [shape((own_rows, width), F32), shape((1, own_rows), F32)],
        ids, own, *received, own_other, *received_other,
    )
    bias_grad = row.reshape(own_rows)

    return activations[None], input_grad[None], weight_grad, bias_grad


def fetch_weights(weight, bias):
    return (
        lax.all_gather(weight, ("row", "col"), axis=0, tiled=True),
        lax.all_gather(bias, ("row", "col"), axis=0, tiled=True),
    )


def body(features, weight, bias, node_mask, neighbour_tiles, tile_weights, out_grad):
    tile = tile_weights.shape[-1]
    dest_count = neighbour_tiles.shape[2]
    slot_count = neighbour_tiles.shape[3]
    lists = neighbour_tiles[0, 0]
    valid = lists >= 0
    blocks = jnp.where(valid[:, :, None, None], tile_weights[0, 0], jnp.zeros((), jnp.bfloat16))
    group = 4
    turns = dest_count // group
    full_weight, full_bias = fetch_weights(weight, bias)
    source = lax.all_gather(features, "row", axis=1, tiled=True)[0]
    width = source.shape[-1]
    source_count = source.shape[0] // tile
    source_index = jnp.arange(source_count, dtype=jnp.int32)
    selector = ((lists[:, :, None] == source_index[None, None, :]) & valid[:, :, None]).astype(
        jnp.bfloat16
    )
    grouped_selector = selector.reshape(turns, group, slot_count, source_count)
    grouped_blocks = blocks.reshape(turns, group, slot_count, tile, tile)

    def dense_strip(group_selector, group_blocks):
        strip = jnp.einsum(
            "gsj,gsik->gijk", group_selector, group_blocks, preferred_element_type=jnp.float32
        )
        return strip.astype(jnp.bfloat16).reshape(group * tile, source_count * tile)

    def aggregate_group(pieces):
        group_selector, group_blocks = pieces
        strip = dense_strip(group_selector, group_blocks)
        return jnp.dot(strip, source, preferred_element_type=jnp.float32)

    partial_value = lax.map(aggregate_group, (grouped_selector, grouped_blocks)).reshape(-1, width)
    summed = lax.psum_scatter(partial_value, "col", scatter_dimension=0, tiled=True)
    aggregate = summed.astype(jnp.bfloat16)
    pre = jnp.dot(aggregate, full_weight, preferred_element_type=jnp.float32) + full_bias.astype(
        jnp.float32
    )
    keep = node_mask[0].astype(jnp.float32)[:, None]
    sigmoid_pre = jax.nn.sigmoid(pre)
    activations = (keep * (pre * sigmoid_pre)).astype(jnp.bfloat16)[None]
    slope = sigmoid_pre * (1.0 + pre * (1.0 - sigmoid_pre))
    pre_grad = (out_grad[0].astype(jnp.float32) * keep * slope).astype(jnp.bfloat16)
    weight_term = lax.dot_general(
        aggregate, pre_grad, (((0,), (0,)), ((), ())), preferred_element_type=jnp.float32
    )
    bias_term = jnp.sum(pre_grad.astype(jnp.float32), axis=0)
    weight_grad, bias_grad = (
        lax.psum_scatter(weight_term, ("row", "col"), scatter_dimension=0, tiled=True),
        lax.psum_scatter(bias_term, ("row", "col"), scatter_dimension=0, tiled=True),
    )
    aggregate_grad = lax.dot_general(
        pre_grad, full_weight, (((1,), (1,)), ((), ())), preferred_element_type=jnp.float32
    ).astype(jnp.bfloat16)
    dest_rows = lax.all_gather(aggregate_grad, "col", axis=0, tiled=True)
    grouped_grads = dest_rows.reshape(turns, group * tile, width)

    def spread_group(totals, pieces):
        group_selector, group_blocks, group_grads = pieces
        strip = dense_strip(group_selector, group_blocks)
        terms = lax.dot_general(
            strip, group_grads, (((0,), (0,)), ((), ())), preferred_element_type=jnp.float32
        )
        return (totals + terms, None)

    initial = jnp.zeros((source_count * tile, width), jnp.float32)
    source_terms, unused = lax.scan(
        spread_group, initial, (grouped_selector, grouped_blocks, grouped_grads)
    )
    input_grad = lax.psum_scatter(source_terms, "row", scatter_dimension=0, tiled=True)
    input_grad = input_grad.astype(jnp.bfloat16)[None]
    return (activations, input_grad, weight_grad, bias_grad)


def solution(mesh):
    chips = mesh.shape["row"] == 8 and mesh.shape["col"] == 4
    return jax.shard_map(
        chip_body if chips else body,
        mesh=mesh,
        in_specs=(
            P("col", "row", None),
            P(("row", "col"), None),
            P(("row", "col")),
            P("row", "col"),
            P("row", "col", None, None),
            P("row", "col", None, None, None, None),
            P("row", "col", None),
        ),
        out_specs=(
            P("row", "col", None),
            P("col", "row", None),
            P(("row", "col"), None),
            P(("row", "col")),
        ),
        check_vma=False,
    )
```

```python
import functools

import jax
import jax.numpy as jnp
from jax import lax
from jax.experimental import pallas as pl
from jax.experimental.pallas import tpu as pltpu
from jax.sharding import PartitionSpec as P

BOTH = ("row", "col")
F32 = jnp.float32
BF16 = jnp.bfloat16
VMEM = pl.BlockSpec(memory_space=pltpu.VMEM)
SMEM = pl.BlockSpec(memory_space=pltpu.SMEM)
CORE, Y, X, Z = 1, 2, 4, 8
GROUP = 4
SLOTS = 3
ROWS = 16


def swap(value, mask, total=32):
    return lax.ppermute(value, BOTH, [(i, i ^ mask) for i in range(total)])


def after(value, *others):
    return lax.optimization_barrier((value,) + others)[0]


def shape(dims, dtype):
    return jax.ShapeDtypeStruct(dims, dtype)


def call(kernel, outs, *operands, scratch=(), smem=1, flops=0, vmem=24):
    moved = sum(o.size * o.dtype.itemsize for o in operands)
    moved += sum(o.size * o.dtype.itemsize for o in outs)
    return pl.pallas_call(
        kernel,
        out_shape=outs,
        in_specs=[SMEM] * smem + [VMEM] * (len(operands) - smem),
        out_specs=[VMEM] * len(outs),
        scratch_shapes=list(scratch),
        compiler_params=pltpu.CompilerParams(vmem_limit_bytes=vmem * 2**20),
        cost_estimate=pl.CostEstimate(flops=flops, bytes_accessed=moved, transcendentals=0),
    )(*operands)


def split_kernel(ids, value, bias, *pieces):
    part = pieces[0].shape[-1]
    many = bias.shape[1]
    own, none = bias[...].astype(F32), jnp.zeros(bias.shape, F32)
    row = jnp.where(
        ids[1] == 0, jnp.concatenate([own, none], axis=1), jnp.concatenate([none, own], axis=1)
    )
    at = pl.ds(pl.multiple_of((ids[5] * 2 + ids[2]) * (2 * many), 2 * many), 2 * many)
    for i, piece in enumerate(pieces):
        piece[:-ROWS] = value[:, pl.ds(pl.multiple_of((ids[7] ^ i) * part, part), part)]
        piece[-ROWS:] = jnp.zeros((ROWS, part), BF16)
        piece[-ROWS:, at] = jnp.broadcast_to(row, (ROWS, 2 * many)).astype(BF16)


def split_masked_kernel(ids, mask, value, *pieces):
    part, lanes = pieces[0].shape[-1], mask.shape[-1]
    for i, piece in enumerate(pieces):
        start = pl.multiple_of((ids[7] ^ i) * part, part)
        for j in range(part // lanes):
            cols = pl.ds(start + j * lanes, lanes)
            piece[:, j * lanes : (j + 1) * lanes] = value[:, cols] * mask[...]


def block_kernel(ids, p0, p1, p2, p3, block):
    rows = p0.shape[0] - ROWS
    for i, piece in enumerate((p0, p1, p2, p3)):
        at = (i >> 1) * 2 + (ids[1] ^ (i & 1))
        block[pl.ds(pl.multiple_of(at * rows, rows), rows), :] = piece[:rows]
    block[4 * rows :] = p0[rows:] + p1[rows:] + p2[rows:] + p3[rows:]


def columns_kernel(ids, own, far, *pieces):
    member = ids[0]
    part, half = pieces[0].shape[-1] // 2, far.shape[-1] // 2
    for i, piece in enumerate(pieces):
        for j in range(2):
            cols = pl.ds(pl.multiple_of(j * half + (member ^ i) * part, part), part)
            piece[0, :, j * part : (j + 1) * part] = own[0, :, cols]
            piece[1, :, j * part : (j + 1) * part] = far[:, cols]


def gather_kernel(ids, lists, a0, a1, a2, a3, h0, h1, h2, h3, keep, send, source):
    member, core, row = ids[0], ids[1], ids[8]
    tile, dests = keep.shape[2], 2 * keep.shape[1]
    for i, piece in enumerate((h0, h1, h2, h3)):
        source[row ^ i] = piece[0]
        source[row ^ i ^ GROUP] = piece[1]
    for i, tiles in enumerate((a0, a1, a2, a3)):
        for pair in range(dests // 2):
            for other in range(2):
                m = pair * 2 + (core if other == 0 else 1 - core)
                left, right = [], []
                for s in range(SLOTS):
                    slot = m * SLOTS + s
                    listed = lists[i, slot]
                    block = tiles[pl.ds(pl.multiple_of(slot * tile, tile), tile), :]
                    left.append(jnp.where(listed >= 0, block, jnp.zeros_like(block)))
                    right.append(source[jnp.maximum(listed, 0)])
                total = jnp.dot(
                    jnp.concatenate(left, axis=1),
                    jnp.concatenate(right, axis=0),
                    preferred_element_type=F32,
                )
                if other == 0:
                    keep[member ^ i, pair] = total
                else:
                    send[member ^ i, pair] = total.astype(send.dtype)


def pair_sum_kernel(ids, kept, received, mine, send):
    y = ids[2]
    for g in range(GROUP):
        mine[g] = kept[g, y] + received[g, y].astype(F32)
        send[g] = (kept[g, 1 - y] + received[g, 1 - y].astype(F32)).astype(send.dtype)


def group_kernel(ids, mine, received, near, far):
    low = ids[6]
    for out, z in ((near, low), (far, 1 - low)):
        for x in range(2):
            nodes = mine.shape[1]
            total = mine[2 * z + x] + received[2 * z + x].astype(F32)
            out[x * nodes : (x + 1) * nodes, :] = total.astype(BF16)
        out[2 * nodes :, :] = jnp.zeros((out.shape[0] - 2 * nodes, out.shape[1]), BF16)


def dense_kernel(ids, p0, p1, p2, p3, q0, q1, q2, q3, o0, o1, o2, o3, *rest):
    weights = rest[:8]
    a0, a1, a2, a3, pre_grad, b0, b1, b2, b3, back_other, left, grads, acts = rest[8:]
    back_own = (b0, b1, b2, b3)
    y, high, z, x = ids[2], ids[4], ids[3], ids[5]
    part = pre_grad.shape[1]
    pair, block = b0.shape[0], part // 4
    nodes = pair // 2

    def lanes(i):
        return pl.ds(pl.multiple_of(((high ^ (i >> 2)) * 2 + (y ^ (i & 1))) * block, block), block)

    def quarter(i, j):
        return (i & 2) + j

    def place(i):
        return pl.ds(pl.multiple_of((i & 1) * pair + (x ^ (i >> 1)) * nodes, nodes), nodes)

    for i in range(8):
        for j in range(2):
            cols = slice((2 * i + j) * block, (2 * i + j + 1) * block)
            left[:pair, cols] = (p0, p1, p2, p3)[quarter(i, j)][:pair, lanes(i)]
            left[pair:, cols] = (q0, q1, q2, q3)[quarter(i, j)][:pair, lanes(i)]
    for i, piece in enumerate((o0, o1, o2, o3)):
        grads[place(i), :] = piece[...]
    many = 2 * block
    bias = sum(
        w[many:, :].astype(F32) * (z ^ (i >> 1) == ids[7]).astype(F32) for i, w in enumerate(weights)
    )[:1]
    step = 256
    for n in range(part // step):
        cols = slice(n * step, (n + 1) * step)
        matrix = jnp.concatenate([w[:many, cols] for w in weights], axis=0)
        pre = jnp.dot(left[...], matrix, preferred_element_type=F32) + bias[:, cols]
        sigmoid = 1.0 / (1.0 + jnp.exp(-pre))
        acts[:, cols] = (pre * sigmoid).astype(BF16)
        slope = sigmoid * (1.0 + pre * (1.0 - sigmoid))
        pre_grad[:, cols] = (grads[:, cols].astype(F32) * slope).astype(BF16)
    for i, piece in enumerate((a0, a1, a2, a3)):
        piece[...] = acts[place(i), :]
    for i, weight in enumerate(weights):
        back = lax.dot_general(
            pre_grad[...], weight[:many, :], (((1,), (1,)), ((), ())), preferred_element_type=F32
        )
        for j in range(2):
            cols = slice(j * block, (j + 1) * block)
            back_own[quarter(i, j)][:, lanes(i)] = back[:pair, cols]
            back_other[quarter(i, j), :, lanes(i)] = back[pair:, cols].astype(BF16)


def back_kernel(b1, b2, b3, received, v1, v2, v3):
    nodes = v1.shape[1]
    for i, (own, out) in enumerate(((b1, v1), (b2, v2), (b3, v3))):
        for x in range(2):
            rows = slice(x * nodes, (x + 1) * nodes)
            out[x] = (own[rows, :] + received[i + 1, rows, :].astype(F32)).astype(BF16)


def add_kernel(own, received, vx, vz, vxz, out):
    nodes = vx.shape[1]
    for x in range(2):
        rows = slice(x * nodes, (x + 1) * nodes)
        out[x] = (own[rows, :] + received[0, rows, :].astype(F32) + vx[x].astype(F32)).astype(BF16)
        out[2 + x] = (vz[x].astype(F32) + vxz[x].astype(F32)).astype(BF16)


def spread_kernel(near, ids, lists, a0, a1, a2, a3, same, cross, *rest):
    start, out, total = (None,) + rest if near else rest
    core, y, x = ids[1], ids[2], ids[5]
    tile = out.shape[1]
    total[...] = jnp.zeros_like(total) if near else start[...]
    for i, tiles in enumerate((a0, a1, a2, a3)):
        for other, grads in enumerate((same, cross)):
            m = (y if near else 1 - y) * 2 + (core ^ other)
            left = []
            for s in range(SLOTS):
                slot = m * SLOTS + s
                block = tiles[pl.ds(pl.multiple_of(slot * tile, tile), tile), :]
                left.append(jnp.where(lists[i, slot] >= 0, block, jnp.zeros_like(block)))
            terms = lax.dot_general(
                jnp.concatenate(left, axis=1), grads[2 * (i >> 1) + (x ^ (i & 1))],
                (((0,), (0,)), ((), ())), preferred_element_type=F32,
            )
            for s in range(SLOTS):
                at = jnp.maximum(lists[i, m * SLOTS + s], 0)
                total[at] += terms[s * tile : (s + 1) * tile]
    out[...] = total[...].astype(out.dtype)


def finish_kernel(terms, out):
    part, half = terms.shape[-1] // 2, out.shape[-1] // 2
    for g in range(GROUP):
        total = sum(terms[i].astype(F32) for i in range(g, terms.shape[0], GROUP)).astype(BF16)
        out[:, g * part : (g + 1) * part] = total[:, :part]
        out[:, half + g * part : half + (g + 1) * part] = total[:, part:]


def act_kernel(ids, mask, a0, a1, a2, a3, out):
    part, lanes = a0.shape[-1], mask.shape[-1]
    for i, piece in enumerate((a0, a1, a2, a3)):
        start = pl.multiple_of((ids[7] ^ i) * part, part)
        for j in range(part // lanes):
            out[:, pl.ds(start + j * lanes, lanes)] = piece[:, j * lanes : (j + 1) * lanes] * mask[...]


def weight_grad_kernel(far, ids, own0, own1, other0, other1, grads, keep, send, *rest):
    y, x = ids[2], ids[5]
    block = keep.shape[1]
    row, total = rest if far else (None,) + rest
    pair = grads.shape[0] // 2
    for j, (own, other) in enumerate(((own0, other0), (own1, other1))):
        total[4 * j * block : 4 * (j + 1) * block, :] = lax.dot_general(
            jnp.concatenate([own[:pair, :], other[:pair, :]], axis=0), grads[...],
            (((0,), (0,)), ((), ())), preferred_element_type=F32,
        )
    for i in range(4):
        at = ((i & 1) ^ x) * 4 + (i >> 1) * 2
        keep[i] = total[pl.ds(pl.multiple_of((at + y) * block, block), block), :]
        value = total[pl.ds(pl.multiple_of((at + 1 - y) * block, block), block), :]
        send[i * block : (i + 1) * block, :] = value.astype(BF16)
    if far:
        sums = jnp.sum(grads[...].astype(F32), axis=0, keepdims=True)
        row[...] = jnp.broadcast_to(sums, row.shape)
        send[4 * block :, :] = row[...].astype(BF16)


def fold_y_kernel(keep, row, received, send, both):
    block = keep.shape[1]
    for i in range(4):
        rows = slice(i * block, (i + 1) * block)
        send[rows, :] = (keep[i] + received[rows, :].astype(F32)).astype(BF16)
    both[...] = row[...] + received[4 * block :, :].astype(F32)
    send[4 * block :, :] = both[...].astype(BF16)


def fold_low_kernel(ids, keep, row, from_y, from_z, own, s1, s2, s3):
    high, x, block = ids[4], ids[5], keep.shape[1]
    sums = row[...] + from_z[4 * block :, :].astype(F32)
    for i, out in enumerate((own, s1, s2, s3)):
        at = (high ^ (i >> 1)) * 2 + (x ^ (i & 1))
        rows = pl.ds(pl.multiple_of(at * block, block), block)
        total = keep[at] + from_y[rows, :].astype(F32) + from_z[rows, :].astype(F32)
        out[:block, :] = total.astype(out.dtype)
        out[block:, :] = sums.astype(out.dtype)


def weight_out_kernel(ids, own, r1, r2, r3, own_c, r1_c, r2_c, r3_c, out, bias):
    many, part = out.shape[0], own.shape[1]
    block = 2 * many
    rows = pl.ds(pl.multiple_of(ids[1] * many, many), many)
    pairs = ((own, r2), (own_c, r2_c), (r1, r3), (r1_c, r3_c))
    total = 0.0
    for i, (left, right) in enumerate(pairs):
        cols = pl.ds(pl.multiple_of((ids[7] ^ i) * part, part), part)
        out[:, cols] = left[rows, :].astype(F32) + right[rows, :].astype(F32)
        quarter = left[block:, :].astype(F32) + right[block:, :].astype(F32)
        total += quarter * (ids[3] ^ ids[7] == i).astype(F32)
    step = 2 * many
    picked = sum(
        total[:1, i * step : (i + 1) * step] * ((ids[5] * 2 + ids[2]) == i).astype(F32) for i in range(4)
    )
    bias[...] = jnp.where(ids[1] == 0, picked[:, :many], picked[:, many:])


def chip_body(features, weight, bias, node_mask, neighbour_tiles, tile_weights, out_grad):
    rows, cols = lax.axis_size("row"), lax.axis_size("col")
    devices = rows * cols
    r, c = lax.axis_index("row"), lax.axis_index("col")
    core, z = c & 1, r >> 1
    place = (r & 1) * 2 + core
    ids = jnp.stack([r & 3, core, c >> 1, z, r >> 2, r & 1, z & 1, place, r]).astype(jnp.int32)
    nodes, width = features.shape[1:]
    half, quarter = width // 2, width // GROUP
    lists, tiles = neighbour_tiles[0, 0], tile_weights[0, 0]
    dests, slots, tile = tiles.shape[0], tiles.shape[1], tiles.shape[2]
    masks = (X, Z, X | Z)
    shares = (CORE, X, X | CORE)

    own_rows = weight.shape[0]
    pieces = call(split_kernel, [shape((own_rows + ROWS, quarter), BF16)] * 4, ids, weight, bias[None])
    pieces = [pieces[0]] + [swap(p, m) for p, m in zip(pieces[1:], shares)]
    (block,) = call(block_kernel, [shape((4 * own_rows + ROWS, quarter), BF16)], ids, *pieces)

    lists = jnp.pad(lists.reshape(1, -1), ((0, 15), (0, tile - dests * slots))).astype(BF16)
    tiles = jnp.concatenate([tiles.reshape(-1, tile), lists], axis=0)
    tiles_of = [tiles, swap(after(tiles, *pieces[2:]), X), swap(tiles, Z)]
    tiles_of.append(swap(tiles_of[2], X))
    lists_of = jnp.stack([t[-16, : dests * slots] for t in tiles_of]).astype(jnp.int32)

    columns = call(
        columns_kernel, [shape((2, nodes, quarter), BF16)] * 4, ids, features, after(swap(features[0], 2 * Z), tiles_of[1])
    )
    source = [columns[0]] + [swap(value, m) for value, m in zip(columns[1:], masks)]
    lanes = jnp.broadcast_to(node_mask[0][:, None].astype(BF16), (nodes, 128))
    grads = call(split_masked_kernel, [shape((nodes, quarter), BF16)] * 4, ids, lanes, out_grad[0])
    grads = [grads[0]] + [swap(g, m) for g, m in zip(grads[1:], shares)]

    y0, z1 = swap(block, Y), swap(block, Z)
    z2 = swap(after(block, y0, z1), 2 * Z)
    z3 = swap(after(z2, *grads[2:]), Z)
    y1, y2, y3 = [swap(value, Y) for value in (z1, z2, z3)]
    weights = [block, y0, z1, y1, z2, y2, z3, y3]

    source[0] = after(source[0], y0, z1)
    piece = (GROUP, dests // 2, tile, quarter)
    kept, sent = call(
        gather_kernel, [shape(piece, F32)] * 2,
        ids, lists_of, *tiles_of, *source,
        scratch=[pltpu.VMEM((rows, tile, quarter), BF16)],
        smem=2, flops=2 * GROUP * dests * slots * tile * tile * quarter,
    )
    mine, send = call(
        pair_sum_kernel, [shape((GROUP, tile, quarter), F32)] * 2,
        ids, kept, swap(after(sent, y1), CORE),
    )
    received = after(swap(send, Y), y1, z2, grads[1])
    near, far = call(group_kernel, [shape((2 * tile + 2 * ROWS, quarter), BF16)] * 2, ids, mine, received)
    near = [near, swap(near, X), swap(far, Z), swap(far, X | Z)]
    near[2] = after(near[2], y2, y3)
    other = [swap(value, CORE) for value in near]

    *acts, pre_grad, b0, b1, b2, b3, back_other = call(
        dense_kernel,
        [shape((nodes, quarter), BF16)] * 4
        + [shape((4 * nodes, quarter), BF16)]
        + [shape((2 * nodes, quarter), F32)] * 4 + [shape((4, 2 * nodes, quarter), BF16)],
        ids, *near, *other, *grads, *weights,
        scratch=[pltpu.VMEM((4 * nodes, width), BF16)] + [pltpu.VMEM((4 * nodes, quarter), BF16)] * 2,
        flops=16 * nodes * quarter * width, vmem=40,
    )

    far, send_far, row = call(
        functools.partial(weight_grad_kernel, True),
        [shape((4, tile, quarter), F32), shape((4 * tile + ROWS, quarter), BF16), shape((ROWS, quarter), F32)],
        ids, *near[2:], *other[2:], pre_grad,
        scratch=[pltpu.VMEM((half, quarter), F32)], flops=4 * nodes * quarter * width, vmem=28,
    )
    received = after(swap(back_other, CORE), send_far)
    others = call(
        back_kernel, [shape((2, nodes, quarter), BF16)] * 3, b1, b2, b3, received, smem=0
    )
    vx, vz, vxz = [swap(v, m) for v, m in zip(others, masks)]
    from_y = swap(send_far, Y)
    kept_near, send_near = call(
        functools.partial(weight_grad_kernel, False),
        [shape((4, tile, quarter), F32), shape((4 * tile, quarter), BF16)],
        ids, *near[:2], *other[:2], after(pre_grad, others[0]),
        scratch=[pltpu.VMEM((half, quarter), F32)], flops=4 * nodes * quarter * width, vmem=28,
    )
    vx, from_y, kept_near = lax.optimization_barrier((vx, from_y, kept_near))
    grads_own = call(add_kernel, [shape((4, nodes, quarter), BF16)], b0, received, vx, vz, vxz, smem=0)[0]
    grads_away = swap(grads_own, Y)
    send, row = call(
        fold_y_kernel, [shape((4 * tile + ROWS, quarter), BF16), shape((ROWS, quarter), F32)],
        far, row, from_y, smem=0,
    )
    from_z = swap(send, Z)
    grads_away = after(grads_away, from_z)
    from_y = swap(after(send_near, grads_own), Y)
    acts = [acts[0]] + [swap(after(a, grads_own), m) for a, m in zip(acts[1:], shares)]
    (spread,) = call(
        functools.partial(spread_kernel, True), [shape((rows, tile, quarter), F32)],
        ids, lists_of, *tiles_of, grads_own, swap(grads_own, CORE),
        scratch=[pltpu.VMEM((rows, tile, quarter), F32)],
        smem=2, flops=GROUP * dests * slots * tile * tile * quarter,
    )
    (spread,) = call(
        functools.partial(spread_kernel, False), [shape((rows, tile, quarter), BF16)],
        ids, lists_of, *tiles_of, grads_away, swap(grads_away, CORE), spread,
        scratch=[pltpu.VMEM((rows, tile, quarter), F32)],
        smem=2, flops=GROUP * dests * slots * tile * tile * quarter,
    )
    spread_all = lax.all_to_all(spread, "row", 0, 0, tiled=True)
    from_y = after(from_y, *acts[1:])
    own, *send = call(
        fold_low_kernel,
        [shape((tile + ROWS, quarter), F32)] + [shape((tile + ROWS, quarter), BF16)] * 3,
        ids, kept_near, row, from_y, from_z,
    )
    own_other = swap(own, CORE)
    send[0] = after(send[0], own_other)
    received = [swap(s, m) for s, m in zip(send, (X, 2 * Z, 2 * Z | X))]
    (input_grad,) = call(finish_kernel, [shape((nodes, width), BF16)], spread_all, smem=0)
    (activations,) = call(act_kernel, [shape((nodes, width), BF16)], ids, lanes, *acts)
    received_other = [
        swap(received[0], CORE),
        swap(after(received[1], input_grad, activations), CORE),
        swap(received[2], CORE),
    ]
    weight_grad, row = call(
        weight_out_kernel, [shape((own_rows, width), F32), shape((1, own_rows), F32)],
        ids, own, *received, own_other, *received_other,
    )
    bias_grad = row.reshape(own_rows)

    return activations[None], input_grad[None], weight_grad, bias_grad


def fetch_weights(weight, bias):
    return (
        lax.all_gather(weight, ("row", "col"), axis=0, tiled=True),
        lax.all_gather(bias, ("row", "col"), axis=0, tiled=True),
    )


def body(features, weight, bias, node_mask, neighbour_tiles, tile_weights, out_grad):
    tile = tile_weights.shape[-1]
    dest_count = neighbour_tiles.shape[2]
    slot_count = neighbour_tiles.shape[3]
    lists = neighbour_tiles[0, 0]
    valid = lists >= 0
    blocks = jnp.where(valid[:, :, None, None], tile_weights[0, 0], jnp.zeros((), jnp.bfloat16))
    group = 4
    turns = dest_count // group
    full_weight, full_bias = fetch_weights(weight, bias)
    source = lax.all_gather(features, "row", axis=1, tiled=True)[0]
    width = source.shape[-1]
    source_count = source.shape[0] // tile
    source_index = jnp.arange(source_count, dtype=jnp.int32)
    selector = ((lists[:, :, None] == source_index[None, None, :]) & valid[:, :, None]).astype(
        jnp.bfloat16
    )
    grouped_selector = selector.reshape(turns, group, slot_count, source_count)
    grouped_blocks = blocks.reshape(turns, group, slot_count, tile, tile)

    def dense_strip(group_selector, group_blocks):
        strip = jnp.einsum(
            "gsj,gsik->gijk", group_selector, group_blocks, preferred_element_type=jnp.float32
        )
        return strip.astype(jnp.bfloat16).reshape(group * tile, source_count * tile)

    def aggregate_group(pieces):
        group_selector, group_blocks = pieces
        strip = dense_strip(group_selector, group_blocks)
        return jnp.dot(strip, source, preferred_element_type=jnp.float32)

    partial_value = lax.map(aggregate_group, (grouped_selector, grouped_blocks)).reshape(-1, width)
    summed = lax.psum_scatter(partial_value, "col", scatter_dimension=0, tiled=True)
    aggregate = summed.astype(jnp.bfloat16)
    pre = jnp.dot(aggregate, full_weight, preferred_element_type=jnp.float32) + full_bias.astype(
        jnp.float32
    )
    keep = node_mask[0].astype(jnp.float32)[:, None]
    sigmoid_pre = jax.nn.sigmoid(pre)
    activations = (keep * (pre * sigmoid_pre)).astype(jnp.bfloat16)[None]
    slope = sigmoid_pre * (1.0 + pre * (1.0 - sigmoid_pre))
    pre_grad = (out_grad[0].astype(jnp.float32) * keep * slope).astype(jnp.bfloat16)
    weight_term = lax.dot_general(
        aggregate, pre_grad, (((0,), (0,)), ((), ())), preferred_element_type=jnp.float32
    )
    bias_term = jnp.sum(pre_grad.astype(jnp.float32), axis=0)
    weight_grad, bias_grad = (
        lax.psum_scatter(weight_term, ("row", "col"), scatter_dimension=0, tiled=True),
        lax.psum_scatter(bias_term, ("row", "col"), scatter_dimension=0, tiled=True),
    )
    aggregate_grad = lax.dot_general(
        pre_grad, full_weight, (((1,), (1,)), ((), ())), preferred_element_type=jnp.float32
    ).astype(jnp.bfloat16)
    dest_rows = lax.all_gather(aggregate_grad, "col", axis=0, tiled=True)
    grouped_grads = dest_rows.reshape(turns, group * tile, width)

    def spread_group(totals, pieces):
        group_selector, group_blocks, group_grads = pieces
        strip = dense_strip(group_selector, group_blocks)
        terms = lax.dot_general(
            strip, group_grads, (((0,), (0,)), ((), ())), preferred_element_type=jnp.float32
        )
        return (totals + terms, None)

    initial = jnp.zeros((source_count * tile, width), jnp.float32)
    source_terms, unused = lax.scan(
        spread_group, initial, (grouped_selector, grouped_blocks, grouped_grads)
    )
    input_grad = lax.psum_scatter(source_terms, "row", scatter_dimension=0, tiled=True)
    input_grad = input_grad.astype(jnp.bfloat16)[None]
    return (activations, input_grad, weight_grad, bias_grad)


def solution(mesh):
    chips = mesh.shape["row"] == 8 and mesh.shape["col"] == 4
    return jax.shard_map(
        chip_body if chips else body,
        mesh=mesh,
        in_specs=(
            P("col", "row", None),
            P(("row", "col"), None),
            P(("row", "col")),
            P("row", "col"),
            P("row", "col", None, None),
            P("row", "col", None, None, None, None),
            P("row", "col", None),
        ),
        out_specs=(
            P("row", "col", None),
            P("col", "row", None),
            P(("row", "col"), None),
            P(("row", "col")),
        ),
        check_vma=False,
    )
```
